512 devices in a mesh: dp: 8 (over y, core), space: 64 (over x, z).
Axes of the slice: x: 4, y: 4, z: 16, core: 2. Of those that a mesh axis runs over, the one named last changes fastest.
Arguments:
- fine_features: bfloat16 [8, 1536, 4, 4, 256], P('dp', 'space'), may hold values from -6 to 6
- cotangent: bfloat16 [8, 1536, 4, 4, 256], P('dp', 'space'), may hold values from -0.01953125 to 0.01953125
- down_weight: bfloat16 [1728, 128], replicated, may hold values from -0.15625 to 0.15625
- coarse_weight: bfloat16 [3456, 128], replicated, may hold values from -0.109375 to 0.109375
- up_weight: bfloat16 [128, 512], replicated, may hold values from -0.5 to 0.5
- fine_neighbours: int32 [8, 1536, 7], P('dp', 'space'), may hold values from -1 to 1535, as said below
- children: int32 [8, 384, 8], P('dp', 'space'), may hold values from -1 to 1535, as said below
- parent_slots: int32 [8, 1536], P('dp', 'space'), may hold values from 0 to 3071, as said below
- coarse_neighbours: int32 [8, 384, 26], P('dp', 'space'), may hold values from -1 to 383, as said below
Outputs:
- decoded: bfloat16 [8, 1536, 4, 4, 256], P('dp', 'space')
- grad_down: float32 [221184], P('space')
- grad_coarse: float32 [442368], P('space')
- grad_up: float32 [65536], P('space')
The draws below stay inside these ranges and needn't reach their ends.
Inputs may be any that keep to these rules, and one draw needn't show every extreme that they name: Bricks sit in a strip of the map with coordinates; fine_neighbours lists the occupied brick at the named lower offset. Every listed neighbour of fine brick f is lower than f and at least 24 * (f // 24 - 1). Each coarse brick has 3 to 5 children; children[t, c, o] = f exactly when parent_slots[t, f] = 8 c + o, and every fine brick is the child of one coarse brick. The children of coarse brick c lie from 24 * (c // 6) to 24 * (c // 6 + 1), both included. `parent_slots`: the parent of fine brick f is a coarse brick from 6 * (f // 24) to 6 * (f // 24 + 1) - 1, or the coarse brick 6 * (f // 24) - 1. `coarse_neighbours`: Symmetric: if the entry of c for offset (sx, sy, sz) is d, the entry of d for the opposite offset is c. Coarse brick c lies in cross-section c // 2 of the strip, and a listed neighbour of c for offset (sx, sy, sz) lies in cross-section c // 2 + sx.
All inputs are finite; a program needn't handle non-finite values.
Results may differ from the reference program's by a relative error of at most 0.0065.
The reference program's roundings to bfloat16 on the way count: a program that leaves them out, or rounds other values in their place, can miss the bound.
Values may be sent and summed in bfloat16 or wider, within the bound.
No kernel may reach another device: no remote copies, remote signals or barrier semaphores. Data moves between devices by JAX's collectives and lax.ppermute only.
A program may use at most 64 MiB of HBM per device.

```python
import jax
import jax.numpy as jnp
from jax import lax

CH_FINE = 64
CH_COARSE = 128
BRICK = 4
COARSE = 384
FINE = 1536
TILES = 8


pair_choices = ((0, 1), (0, 2), (0, 3), (1, 2), (1, 3), (2, 3))


def tile_geometry(tile_key):
    slices = COARSE // 2
    key_pair, key_drift, key_order = jax.random.split(jax.random.fold_in(tile_key, 71), 3)
    pair_array = jnp.array(pair_choices, dtype=jnp.int32)
    chosen_pair = jax.random.randint(key_pair, (slices,), 0, 6)
    positions = pair_array[chosen_pair].reshape(COARSE)
    coarse_ids = jnp.arange(COARSE, dtype=jnp.int32)
    coarse_x = coarse_ids // 2
    coarse_y = positions // 2
    coarse_z = positions % 2
    drift_bits = jax.random.randint(key_drift, (COARSE,), 0, 2).astype(jnp.int32)
    drift_bits = jnp.where(coarse_ids == COARSE - 1, 0, drift_bits)
    before = jnp.concatenate([jnp.zeros((1,), jnp.int32), drift_bits[:-1]])
    counts = 4 + drift_bits - before
    first_child = 4 * coarse_ids + before
    octant = jnp.arange(8, dtype=jnp.int32)
    scores = jax.random.randint(key_order, (COARSE, 8), 0, 1 << 20).astype(jnp.int32) * 8 + octant[None, :]
    octant_rank = jnp.argsort(jnp.argsort(scores, axis=1), axis=1)
    chosen = octant_rank < counts[:, None]
    chosen_int = chosen.astype(jnp.int32)
    prefix = jnp.cumsum(chosen_int, axis=1) - chosen_int
    children = jnp.where(chosen, first_child[:, None] + prefix, -1).astype(jnp.int32)
    slot_values = coarse_ids[:, None] * 8 + octant[None, :]
    targets = jnp.where(chosen, children, FINE)
    parents = jnp.zeros((FINE,), jnp.int32).at[targets.reshape(-1)].set(slot_values.reshape(-1), mode='drop')
    parent_coarse = parents // 8
    parent_octant = parents % 8
    fine_x = 2 * coarse_x[parent_coarse] + parent_octant // 4
    fine_y = 2 * coarse_y[parent_coarse] + parent_octant // 2 % 2
    fine_z = 2 * coarse_z[parent_coarse] + parent_octant % 2
    fine_grid = jnp.full((2 * slices + 1, 5, 5), -1, jnp.int32)
    fine_grid = fine_grid.at[fine_x + 1, fine_y + 1, fine_z + 1].set(jnp.arange(FINE, dtype=jnp.int32))
    fine_list = []
    for bit_code in range(1, 8):
        fine_list.append(fine_grid[fine_x + 1 - bit_code // 4, fine_y + 1 - bit_code // 2 % 2, fine_z + 1 - bit_code % 2])
    fine_nbr = jnp.stack(fine_list, axis=1)
    coarse_grid = jnp.full((slices + 2, 4, 4), -1, jnp.int32)
    coarse_grid = coarse_grid.at[coarse_x + 1, coarse_y + 1, coarse_z + 1].set(coarse_ids)
    coarse_list = []
    for offset_code in range(27):
        if offset_code != 13:
            coarse_list.append(coarse_grid[coarse_x + offset_code // 9, coarse_y + offset_code // 3 % 3, coarse_z + offset_code % 3])
    coarse_nbr = jnp.stack(coarse_list, axis=1)
    return (fine_nbr, children, parents, coarse_nbr)


def all_tiles(key):

    def one_tile(tile_number):
        return tile_geometry(jax.random.fold_in(key, tile_number))
    return jax.vmap(one_tile)(jnp.arange(TILES, dtype=jnp.int32))


def draw_fine_neighbours(key, part):
    return all_tiles(key)[0]


def draw_children(key, part):
    return all_tiles(key)[1]


def draw_parent_slots(key, part):
    return all_tiles(key)[2]


def draw_coarse_neighbours(key, part):
    return all_tiles(key)[3]


def block_scale(own_key, extent, shards, least, top_value):
    def one(dim, shards_of):
        steps = jax.random.uniform(jax.random.fold_in(jax.random.fold_in(own_key, 6), dim), (shards_of,), jnp.float32, least / len(shards), top_value / len(shards))
        return jnp.repeat(jnp.exp(steps), extent[dim] // shards_of).reshape((-1,) + (1,) * (len(extent) - dim - 1))

    factor_of = one(*shards[0])
    for cut in shards[1:]:
        factor_of = factor_of * one(*cut)
    return factor_of


def scatter_about(own_key, extent, scale, limit, cuts=(), held_as=jnp.bfloat16):
    entries = jax.random.normal(own_key, extent, jnp.float32) * scale
    if len(cuts) > 0:
        entries = block_scale(own_key, extent, cuts, -0.22, 0.18) * entries
    return jnp.clip(entries, min=-limit, max=limit).astype(held_as)


def setup_inputs(seed: int = 0) -> dict:
    streams_of = jax.random.split(jax.random.key(seed), 10)
    fine_features = scatter_about(streams_of[0], (TILES, FINE, BRICK, BRICK, BRICK * CH_FINE), 1.0, 6.0, ((0, 8), (1, 64)))
    cotangent = scatter_about(streams_of[1], (TILES, FINE, BRICK, BRICK, BRICK * CH_FINE), (FINE * TILES * BRICK ** 3 // 8) ** -0.5, 0.01953125, ((0, 8), (1, 64)))
    down_weight = scatter_about(streams_of[2], (27 * CH_FINE, CH_COARSE), (27 * CH_FINE) ** -0.5, 0.15625)
    coarse_weight = scatter_about(streams_of[3], (27 * CH_COARSE, CH_COARSE), (27 * CH_COARSE) ** -0.5, 0.109375)
    up_weight = scatter_about(streams_of[4], (CH_COARSE, 8 * CH_FINE), CH_COARSE ** -0.5, 0.5)
    fine_neighbours = draw_fine_neighbours(jax.random.fold_in(streams_of[9], 71), 0)
    children = draw_children(jax.random.fold_in(streams_of[9], 71), 0)
    parent_slots = draw_parent_slots(jax.random.fold_in(streams_of[9], 71), 0)
    coarse_neighbours = draw_coarse_neighbours(jax.random.fold_in(streams_of[9], 71), 0)
    return dict(fine_features=fine_features, cotangent=cotangent, down_weight=down_weight, coarse_weight=coarse_weight, up_weight=up_weight, fine_neighbours=fine_neighbours, children=children, parent_slots=parent_slots, coarse_neighbours=coarse_neighbours)


def silu_slope(inputs):
    squash = jax.nn.sigmoid(inputs)
    return squash * (1.0 + inputs * (1.0 - squash))

def edge_pick(offset_value, brick_edge):
    if offset_value < 0:
        return slice(brick_edge - 1, brick_edge)
    if offset_value > 0:
        return slice(0, 1)
    return slice(0, brick_edge)

def edge_place(offset_value, brick_edge):
    if offset_value < 0:
        return slice(0, 1)
    if offset_value > 0:
        return slice(brick_edge + 1, brick_edge + 2)
    return slice(1, brick_edge + 1)

def fine_planes(bricks):
    return jnp.stack([bricks[:, -1], bricks[:, :, -1], bricks[:, :, :, -1]], axis=1)

def fine_padded(bricks, planes_all, neighbours):
    brick_edge = bricks.shape[1]
    padded = jnp.pad(bricks, ((0, 0), (1, 0), (1, 0), (1, 0), (0, 0)))
    for bit_code in range(1, 8):
        shift_x = bit_code // 4
        shift_y = bit_code // 2 % 2
        shift_z = bit_code % 2
        picked = planes_all[neighbours[:, bit_code - 1]]
        if shift_x:
            values = picked[:, 0][:, edge_pick(-shift_y, brick_edge), edge_pick(-shift_z, brick_edge)][:, None]
        elif shift_y:
            values = picked[:, 1][:, :, edge_pick(-shift_z, brick_edge)][:, :, None]
        else:
            values = picked[:, 2][:, :, :, None]
        place_x = slice(0, 1) if shift_x else slice(1, brick_edge + 1)
        place_y = slice(0, 1) if shift_y else slice(1, brick_edge + 1)
        place_z = slice(0, 1) if shift_z else slice(1, brick_edge + 1)
        padded = padded.at[:, place_x, place_y, place_z].set(values)
    return padded

def fine_columns(padded, half_edge):
    tap_list = []
    for tap_code in range(27):
        along_x = tap_code // 9
        along_y = tap_code // 3 % 3
        along_z = tap_code % 3
        tap_list.append(padded[:, along_x:along_x + 2 * half_edge - 1:2, along_y:along_y + 2 * half_edge - 1:2, along_z:along_z + 2 * half_edge - 1:2])
    stacked = jnp.stack(tap_list, axis=4)
    return stacked.reshape(-1, 27 * stacked.shape[-1])

def octants_to_bricks(patches):
    brick_count = patches.shape[0]
    half_edge = patches.shape[2]
    channels = patches.shape[-1]
    arranged = patches.reshape(brick_count, 2, 2, 2, half_edge, half_edge, half_edge, channels)
    arranged = arranged.transpose(0, 1, 4, 2, 5, 3, 6, 7)
    return arranged.reshape(brick_count, 2 * half_edge, 2 * half_edge, 2 * half_edge, channels)

def bricks_to_octants(bricks):
    brick_count = bricks.shape[0]
    half_edge = bricks.shape[1] // 2
    channels = bricks.shape[-1]
    arranged = bricks.reshape(brick_count, 2, half_edge, 2, half_edge, 2, half_edge, channels)
    arranged = arranged.transpose(0, 1, 3, 5, 2, 4, 6, 7)
    return arranged.reshape(brick_count * 8, half_edge, half_edge, half_edge, channels)

def coarse_faces(bricks):
    return jnp.stack([bricks[:, 0], bricks[:, -1], bricks[:, :, 0], bricks[:, :, -1], bricks[:, :, :, 0], bricks[:, :, :, -1]], axis=1)

def coarse_padded(bricks, faces_all, neighbours):
    brick_edge = bricks.shape[1]
    padded = jnp.pad(bricks, ((0, 0), (1, 1), (1, 1), (1, 1), (0, 0)))
    offset_codes = [offset_code for offset_code in range(27) if offset_code != 13]
    for column_index, offset_code in enumerate(offset_codes):
        off_x = offset_code // 9 - 1
        off_y = offset_code // 3 % 3 - 1
        off_z = offset_code % 3 - 1
        picked = faces_all[neighbours[:, column_index]]
        if off_x != 0:
            values = picked[:, 1 if off_x < 0 else 0][:, edge_pick(off_y, brick_edge), edge_pick(off_z, brick_edge)][:, None]
        elif off_y != 0:
            values = picked[:, 3 if off_y < 0 else 2][:, :, edge_pick(off_z, brick_edge)][:, :, None]
        else:
            values = picked[:, 5 if off_z < 0 else 4][:, :, :, None]
        padded = padded.at[:, edge_place(off_x, brick_edge), edge_place(off_y, brick_edge), edge_place(off_z, brick_edge)].set(values)
    return padded

def pair_taps(padded, along_x, along_y, reverse):
    brick_edge = padded.shape[1] - 2
    pieces = []
    for along_z in range(3):
        if reverse:
            lows = (2 - along_x, 2 - along_y, 2 - along_z)
        else:
            lows = (along_x, along_y, along_z)
        pieces.append(padded[:, lows[0]:lows[0] + brick_edge, lows[1]:lows[1] + brick_edge, lows[2]:lows[2] + brick_edge])
    gathered_taps = jnp.concatenate(pieces, axis=-1)
    return gathered_taps.reshape(-1, gathered_taps.shape[-1])

def coarse_forward(padded, weight):
    channels = weight.shape[0] // 27
    summed = None
    for pair_code in range(9):
        gathered_taps = pair_taps(padded, pair_code // 3, pair_code % 3, False)
        weight_rows = weight[pair_code * 3 * channels:(pair_code + 1) * 3 * channels]
        partial_value = jnp.dot(gathered_taps, weight_rows, preferred_element_type=jnp.float32)
        summed = partial_value if summed is None else summed + partial_value
    return summed

def coarse_weight_grad(padded, slope_rows):
    blocks = []
    for pair_code in range(9):
        gathered_taps = pair_taps(padded, pair_code // 3, pair_code % 3, False)
        blocks.append(lax.dot_general(gathered_taps, slope_rows, (((0,), (0,)), ((), ())), preferred_element_type=jnp.float32))
    return jnp.concatenate(blocks, axis=0)

def coarse_transpose(padded, weight):
    channels_in = weight.shape[0] // 27
    channels_out = weight.shape[1]
    summed = None
    for pair_code in range(9):
        gathered_taps = pair_taps(padded, pair_code // 3, pair_code % 3, True)
        weight_block = weight[pair_code * 3 * channels_in:(pair_code + 1) * 3 * channels_in]
        weight_block = weight_block.reshape(3, channels_in, channels_out).transpose(0, 2, 1).reshape(3 * channels_out, channels_in)
        partial_value = jnp.dot(gathered_taps, weight_block, preferred_element_type=jnp.float32)
        summed = partial_value if summed is None else summed + partial_value
    return summed

def reference(fine_features, cotangent, down_weight, coarse_weight, up_weight, fine_neighbours, children, parent_slots, coarse_neighbours):
    brick_edge = BRICK
    half_edge = BRICK // 2

    def tile_pass(inputs):
        fine_tile, cot_tile, fine_nbr, child_list, parent_list, coarse_nbr = inputs
        bricks = fine_tile.reshape(FINE, brick_edge, brick_edge, brick_edge, CH_FINE)
        zero_planes = jnp.zeros((1, 3, brick_edge, brick_edge, CH_FINE), bricks.dtype)
        planes_all = jnp.concatenate([fine_planes(bricks), zero_planes], axis=0)
        padded_fine = fine_padded(bricks, planes_all, jnp.where(fine_nbr < 0, FINE, fine_nbr).astype(jnp.int32))
        columns = fine_columns(padded_fine, half_edge)
        pre_down = jnp.dot(columns, down_weight, preferred_element_type=jnp.float32)
        hidden = jax.nn.silu(pre_down).astype(jnp.bfloat16)
        zero_patch = jnp.zeros((1, half_edge, half_edge, half_edge, CH_COARSE), hidden.dtype)
        patch_pool = jnp.concatenate([hidden.reshape(FINE, half_edge, half_edge, half_edge, CH_COARSE), zero_patch], axis=0)
        child_index = jnp.where(child_list < 0, FINE, child_list).astype(jnp.int32)
        coarse_in = octants_to_bricks(patch_pool[child_index])
        coarse_index = jnp.where(coarse_nbr < 0, COARSE, coarse_nbr).astype(jnp.int32)
        zero_faces = jnp.zeros((1, 6, brick_edge, brick_edge, CH_COARSE), hidden.dtype)
        padded_in = coarse_padded(coarse_in, jnp.concatenate([coarse_faces(coarse_in), zero_faces], axis=0), coarse_index)
        pre_coarse = coarse_forward(padded_in, coarse_weight)
        coarse_out = jax.nn.silu(pre_coarse).astype(jnp.bfloat16).reshape(COARSE, brick_edge, brick_edge, brick_edge, CH_COARSE)
        up_input = bricks_to_octants(coarse_out)[parent_list]
        up_rows = up_input.reshape(-1, CH_COARSE)
        up_out = jnp.dot(up_rows, up_weight, preferred_element_type=jnp.float32)
        up_grid = up_out.reshape(FINE, half_edge, half_edge, half_edge, 2, 2, 2, CH_FINE).transpose(0, 1, 4, 2, 5, 3, 6, 7)
        up_grid = up_grid.reshape(FINE, brick_edge, brick_edge, brick_edge, CH_FINE)
        joined = up_grid + bricks.astype(jnp.float32)
        decoded = jax.nn.silu(joined).astype(jnp.bfloat16).reshape(FINE, brick_edge, brick_edge, brick_edge * CH_FINE)
        cot_grid = cot_tile.reshape(FINE, brick_edge, brick_edge, brick_edge, CH_FINE).astype(jnp.float32)
        out_grad = (cot_grid * silu_slope(joined)).astype(jnp.bfloat16)
        out_rows = out_grad.reshape(FINE, half_edge, 2, half_edge, 2, half_edge, 2, CH_FINE).transpose(0, 1, 3, 5, 2, 4, 6, 7)
        out_rows = out_rows.reshape(-1, 8 * CH_FINE)
        grad_up = lax.dot_general(up_rows, out_rows, (((0,), (0,)), ((), ())), preferred_element_type=jnp.float32)
        patch_grad = lax.dot_general(out_rows, up_weight, (((1,), (1,)), ((), ())), preferred_element_type=jnp.float32).astype(jnp.bfloat16)
        grad_pool = jnp.concatenate([patch_grad.reshape(FINE, half_edge, half_edge, half_edge, CH_COARSE), zero_patch], axis=0)
        coarse_grad_out = octants_to_bricks(grad_pool[child_index])
        coarse_slope = (coarse_grad_out.reshape(-1, CH_COARSE).astype(jnp.float32) * silu_slope(pre_coarse)).astype(jnp.bfloat16)
        grad_coarse = coarse_weight_grad(padded_in, coarse_slope)
        slope_bricks = coarse_slope.reshape(COARSE, brick_edge, brick_edge, brick_edge, CH_COARSE)
        padded_slope = coarse_padded(slope_bricks, jnp.concatenate([coarse_faces(slope_bricks), zero_faces], axis=0), coarse_index)
        input_grad = coarse_transpose(padded_slope, coarse_weight).astype(jnp.bfloat16)
        input_bricks = input_grad.reshape(COARSE, brick_edge, brick_edge, brick_edge, CH_COARSE)
        hidden_grad = bricks_to_octants(input_bricks)[parent_list]
        down_slope = (hidden_grad.reshape(-1, CH_COARSE).astype(jnp.float32) * silu_slope(pre_down)).astype(jnp.bfloat16)
        grad_down = lax.dot_general(columns, down_slope, (((0,), (0,)), ((), ())), preferred_element_type=jnp.float32)
        return (decoded, grad_down, grad_coarse, grad_up)
    decoded, grad_down, grad_coarse, grad_up = lax.map(tile_pass, (fine_features, cotangent, fine_neighbours, children, parent_slots, coarse_neighbours))
    return (decoded, lax.optimization_barrier(jnp.sum(grad_down, axis=0)).reshape(-1), lax.optimization_barrier(jnp.sum(grad_coarse, axis=0)).reshape(-1), lax.optimization_barrier(jnp.sum(grad_up, axis=0)).reshape(-1))
```

```python
import functools

import jax
import jax.numpy as jnp
from jax import lax
from jax.experimental import pallas as pl
from jax.experimental.pallas import tpu as pltpu
from jax.sharding import PartitionSpec as P

BF = jnp.bfloat16
F32 = jnp.float32
FB = 24
CB = 6
ROWS = 80
CR = 16
XL = 4096
IDX = 2 * XL
TILES = 96


def plane_lanes(i, j):
    if i == 3:
        return (j * 256, 256)
    if j == 3:
        return (1024 + i * 256, 256)
    return (1792 + (i * 3 + j) * 128, 128)


def upper_pieces():
    pieces = [(3 * 1024, 1024)]
    pieces += [((i * 4 + 3) * 256, 256) for i in range(3)]
    pieces += [((i * 4 + j) * 256 + 128, 128) for i in range(3) for j in range(3)]
    return pieces


UPPER = sum(width for _, width in upper_pieces())


def dot(a, b, dims=((1,), (0,))):
    return lax.dot_general(a, b, (dims, ((), ())), preferred_element_type=F32)


def gate(v):
    s = 1.0 / (1.0 + jnp.exp(-v))
    return v * s, s * (1.0 + v * (1.0 - s))


def axis_sides(half):
    inner = [(0, 0, half + 1), (0, 1, half + 3)]
    return inner + ([(-1, 1, 0)] if half else [(1, 0, 5)])


def halo_blocks(p, q):
    blocks = []
    for sx, ox, cx in axis_sides(p):
        for sy, oy, cy in axis_sides(q):
            for sz, oz, cells in (
                (0, 0, [(0, 1), (1, 2)]),
                (0, 1, [(0, 3), (1, 4)]),
                (-1, 1, [(1, 0)]),
                (1, 0, [(0, 5)]),
            ):
                code = 9 * (sx + 1) + 3 * (sy + 1) + sz + 1
                if code != 13:
                    targets = [(r, (cx, cy, cz)) for r, cz in cells]
                    blocks.append((code - (code > 13), 4 * ox + 2 * oy + oz, targets))
    return blocks


HALO = len(halo_blocks(0, 0)) * CR


def octant_of(x, y, z):
    return 4 * (x // 2) + 2 * (y // 2) + z // 2, 4 * (x % 2) + 2 * (y % 2) + z % 2


def kernel(
    core_ref,
    own_ref,
    prev_ref,
    next_ref,
    far_ref,
    wd_ref,
    wc_ref,
    wt_ref,
    wu_ref,
    dec_ref,
    sum_ref,
    wide_ref,
    src_ref,
    pad_ref,
    hid_ref,
    nl_ref,
    cin_ref,
    cp_ref,
    cslope_ref,
    cout_ref,
    cs_ref,
    sp_ref,
    cst_ref,
    gd_ref,
    gc_ref,
    gu_ref,
    t_ref,
):
    zeros8 = functools.partial(jnp.zeros, dtype=F32)

    def rows(lane, width):
        at = slice(lane, lane + width)
        parts = [r[:, at].astype(F32) for r in (prev_ref, own_ref, next_ref)]
        return jnp.concatenate(parts + [zeros8((ROWS - 3 * FB, width))], axis=0)

    idx = rows(IDX, 128)
    row = lax.broadcasted_iota(jnp.int32, (ROWS, 128), 0)
    lane = lax.broadcasted_iota(jnp.int32, (ROWS, 128), 1)
    block = jnp.where(row >= FB, 1.0, 0.0) + jnp.where(row >= 2 * FB, 1.0, 0.0)
    lane_f = lane.astype(F32)

    wide_ref[...] = jnp.zeros(wide_ref.shape, BF)
    for ab in range(9):
        tap = [wd_ref[(3 * ab + e) * 64 : (3 * ab + e + 1) * 64, :] for e in range(3)]
        for at, e in ((0, 1), (64, 2), (320, 0)):
            wide_ref[ab, at : at + 64, 0:128] = tap[e]
        for at, e in ((64, 0), (128, 1), (192, 2)):
            wide_ref[ab, at : at + 64, 128:256] = tap[e]

    at = 0
    for start, width in upper_pieces():
        parts = [far_ref[:, at : at + width].astype(F32)]
        parts += [r[:, start : start + width].astype(F32) for r in (prev_ref, own_ref, next_ref)]
        src_ref[:, at : at + width] = jnp.concatenate(parts, axis=0).astype(BF)
        at += width

    def pick(code):
        wanted = idx[:, code - 1 : code] + (24.0 * block[:, 0:1] - 1.0)
        wanted = jnp.where(idx[:, code - 1 : code] > 0.0, wanted, -1.0)
        hit = jnp.where(lane_f[:, 0 : 4 * FB] == wanted, 1.0, 0.0)
        return hit.astype(BF)

    picks = {code: pick(code) for code in range(1, 8)}

    def fetch(code, i, j, last):
        start, width = plane_lanes(i, j)
        if last:
            start, width = start + width - 128, 128
        return dot(picks[code], src_ref[:, start : start + width]).astype(BF)

    for ip in range(5):
        for jp in range(5):
            i, j = (ip - 1) % 4, (jp - 1) % 4
            code = 4 * (ip == 0) + 2 * (jp == 0)
            if code:
                own = fetch(code, i, j, False)
            else:
                own = rows((i * 4 + j) * 256, 256).astype(BF)
            pad_ref[ip * 5 + jp, :, 0:256] = own
            pad_ref[ip * 5 + jp, :, 256:384] = fetch(code + 1, i, j, True)

    slope_down = []
    for pq in range(4):
        p, q = pq // 2, pq % 2
        taps = [pad_ref[(2 * p + a) * 5 + 2 * q + b] for a in range(3) for b in range(3)]
        pre = dot(jnp.concatenate(taps, axis=1), wide_ref[...].reshape(9 * 384, 256))
        value, slope = gate(pre)
        hid_ref[:, pq * 256 : (pq + 1) * 256] = value.astype(BF)
        slope_down.append(slope[FB : 2 * FB])

    code = idx[:, 7:8]
    slot = jnp.where(code > 0.0, code + (48.0 * block[:, 0:1] - 9.0), -1.0)
    column = (lane % CR * 8 + lane // CR).astype(F32)
    up_f = jnp.where(column == slot, 1.0, 0.0)
    up = up_f.astype(BF)

    def to_coarse(ref):
        return dot(up, ref[...], ((0,), (0,)))

    row16 = lax.broadcasted_iota(jnp.int32, (CR, ROWS), 0)
    lane80 = lax.broadcasted_iota(jnp.int32, (CR, ROWS), 1)
    device = jnp.where(row16 >= CB, 1, 0) + jnp.where(row16 >= 2 * CB, 1, 0)
    choose = jnp.where(lane80 == row16 + (FB - CB) * device, 1.0, 0.0).astype(BF)
    listed = dot(choose, idx.astype(BF))
    device = device[:, 0:1].astype(F32)
    place = listed + (6.0 * device - 7.0)
    place = jnp.where((listed > 0.0) & (place >= 0.0) & (place < CR), place, -1000.0)
    lane16 = lane_f[0:CR]
    for pq in range(4):
        blocks = []
        for m, octant, _ in halo_blocks(pq // 2, pq % 2):
            wanted = place[:, 8 + m : 9 + m] + float(CR * octant)
            blocks.append(jnp.where(lane16 == wanted, 1.0, 0.0))
        nl_ref[pq] = jnp.concatenate(blocks, axis=0).astype(BF)

    def fill(flat_ref, padded_ref):
        for x in range(4):
            for y in range(4):
                for z in range(4):
                    o, v = octant_of(x, y, z)
                    padded_ref[x + 1, y + 1, z + 1] = flat_ref[
                        o * CR : (o + 1) * CR, v * 128 : (v + 1) * 128
                    ]
        for pq in range(4):
            got = dot(nl_ref[pq], flat_ref[:, pq * 256 : (pq + 1) * 256]).astype(BF)
            for n, (_, _, targets) in enumerate(halo_blocks(pq // 2, pq % 2)):
                for r, (cx, cy, cz) in targets:
                    padded_ref[cx, cy, cz] = got[n * CR : (n + 1) * CR, r * 128 : (r + 1) * 128]

    def convolve(padded_ref, weight_ref, x):
        taps = [
            padded_ref[x + a, b : b + 4, e : e + 4].reshape(16 * CR, 128)
            for a in range(3)
            for b in range(3)
            for e in range(3)
        ]
        return dot(jnp.concatenate(taps, axis=1), weight_ref[...])

    def scatter_flat(ref, value, x):
        for yz in range(16):
            o, v = octant_of(x, yz // 4, yz % 4)
            ref[o * CR : (o + 1) * CR, v * 128 : (v + 1) * 128] = value[yz * CR : (yz + 1) * CR]

    cin_ref[...] = to_coarse(hid_ref).astype(BF)
    fill(cin_ref, cp_ref)
    for x in range(4):
        value, slope = gate(convolve(cp_ref, wc_ref, x))
        cslope_ref[x] = slope
        scatter_flat(cout_ref, value.astype(BF), x)

    up_in = dot(up, cout_ref[...])
    own_in, own_grad = [], []
    for v in range(8):
        p, q, r = v // 4, v // 2 % 2, v % 2
        piece = up_in[:, v * 128 : (v + 1) * 128]
        own_in.append(piece[FB : 2 * FB])
        out = dot(piece.astype(BF), wu_ref[...])
        grads = []
        for ab in range(4):
            a, b = ab // 2, ab % 2
            at = ((2 * p + a) * 4 + 2 * q + b) * 256 + r * 128
            joined = out[:, ab * 128 : (ab + 1) * 128] + rows(at, 128)
            value, slope = gate(joined)
            dec_ref[:, at : at + 128] = value[FB : 2 * FB].astype(BF)
            grads.append(rows(XL + at, 128) * slope)
        grad = jnp.concatenate(grads, axis=1)
        own_grad.append(grad[FB : 2 * FB])
        back = dot(grad.astype(BF), wu_ref[...], ((1,), (1,)))
        hid_ref[:, v * 128 : (v + 1) * 128] = back.astype(BF)
    own_in = jnp.concatenate(own_in, axis=0).astype(BF)
    own_grad = jnp.concatenate(own_grad, axis=0).astype(BF)
    found = dot(own_in, own_grad, ((0,), (0,)))
    for n in range(4):
        gu_ref[n] = found[:, n * 128 : (n + 1) * 128]

    cin_ref[...] = to_coarse(hid_ref).astype(BF)
    row_c = lax.broadcasted_iota(jnp.int32, (16 * CR, 128), 0) % CR
    mine = (row_c >= CB) & (row_c < 2 * CB)
    for x in range(4):
        pieces = []
        for yz in range(16):
            o, v = octant_of(x, yz // 4, yz % 4)
            pieces.append(cin_ref[o * CR : (o + 1) * CR, v * 128 : (v + 1) * 128])
        grad = jnp.concatenate(pieces, axis=0).astype(F32) * cslope_ref[x]
        scatter_flat(cs_ref, grad.astype(BF), x)
        kept = jnp.where(mine, grad, 0.0)
        cst_ref[:, x * 256 : (x + 1) * 256] = jnp.transpose(kept).astype(BF)
    for ab in range(9):
        a, b = ab // 3, ab % 3
        taps = [
            cp_ref[a : a + 4, b : b + 4, e : e + 4].reshape(64 * CR, 128) for e in range(3)
        ]
        found = dot(cst_ref[...], jnp.concatenate(taps, axis=1))
        for e in range(3):
            at = (3 * ab + e) * 128
            gc_ref[at : at + 128, :] = jnp.transpose(found[:, e * 128 : (e + 1) * 128])

    fill(cs_ref, sp_ref)
    for x in range(4):
        scatter_flat(cin_ref, convolve(sp_ref, wt_ref, x).astype(BF), x)

    hidden_grad = dot(up_f[FB : 2 * FB].astype(BF), cin_ref[...])
    pieces = []
    for pq in range(4):
        slope = hidden_grad[:, pq * 256 : (pq + 1) * 256] * slope_down[pq]
        pieces += [zeros8((FB, 256)), slope, zeros8((ROWS - 2 * FB, 256))]
    down = jnp.concatenate(pieces, axis=0).astype(BF)
    for ab in range(9):
        a, b = ab // 3, ab % 3
        taps = [pad_ref[(2 * p + a) * 5 + 2 * q + b] for p in range(2) for q in range(2)]
        found = dot(down, jnp.concatenate(taps, axis=0), ((0,), (0,)))
        later = found[0:128, 0:128] + found[128:256, 128:256]
        first = found[0:128, 256:384] + found[128:256, 0:128]
        gd_ref[(3 * ab) * 64 : (3 * ab + 1) * 64, :] = jnp.transpose(first)[64:128]
        gd_ref[(3 * ab + 1) * 64 : (3 * ab + 3) * 64, :] = jnp.transpose(later)

    for t in range(27):
        t_ref[t] = gd_ref[pl.ds(t, 64, stride=27), :]
    for t in range(54):
        t_ref[27 + t] = gc_ref[pl.ds(t, 64, stride=54), :]
    for t in range(8):
        t_ref[81 + t] = gu_ref[t % 4, pl.ds(t // 4, 64, stride=2), :]
    t_ref[89:TILES] = jnp.zeros((TILES - 89, 64, 128), F32)
    core = core_ref[0]
    for side in range(2):
        half = core if side == 0 else 1 - core
        for y in range(4):
            for n in range(12):
                tile = t_ref[24 * y + 12 * half + n]
                sum_ref[side, y, :, n * 128 : (n + 1) * 128] = tile.astype(BF)


def local_pass(core, own, prev, nxt, far, wd, wc, wt, wu):
    vmem = pl.BlockSpec(memory_space=pltpu.VMEM)
    return pl.pallas_call(
        kernel,
        out_shape=(
            jax.ShapeDtypeStruct((FB, XL), BF),
            jax.ShapeDtypeStruct((2, 4, 64, 1536), BF),
        ),
        in_specs=[pl.BlockSpec(memory_space=pltpu.SMEM)] + [vmem] * 8,
        out_specs=(vmem, vmem),
        scratch_shapes=[
            pltpu.VMEM((9, 384, 256), BF),
            pltpu.VMEM((4 * FB, UPPER), BF),
            pltpu.VMEM((25, ROWS, 384), BF),
            pltpu.VMEM((ROWS, 1024), BF),
            pltpu.VMEM((4, HALO, 128), BF),
            pltpu.VMEM((8 * CR, 1024), BF),
            pltpu.VMEM((6, 6, 6, CR, 128), BF),
            pltpu.VMEM((4, 16 * CR, 128), F32),
            pltpu.VMEM((8 * CR, 1024), BF),
            pltpu.VMEM((8 * CR, 1024), BF),
            pltpu.VMEM((6, 6, 6, CR, 128), BF),
            pltpu.VMEM((128, 64 * CR), BF),
            pltpu.VMEM((1728, 128), F32),
            pltpu.VMEM((3456, 128), F32),
            pltpu.VMEM((4, 128, 128), F32),
            pltpu.VMEM((TILES, 64, 128), F32),
        ],
        compiler_params=pltpu.CompilerParams(vmem_limit_bytes=48 * 2**20),
    )(core, own, prev, nxt, far, wd, wc, wt, wu)


def shift(block, distance):
    size = lax.axis_size("space")
    route = [(i, i + distance) for i in range(size) if 0 <= i + distance < size]
    return lax.ppermute(block, "space", route)


def encode(fine_nbr, parents, coarse_nbr):
    place = lax.axis_index("space")
    fine = jnp.where(fine_nbr < 0, 0, fine_nbr - FB * (place - 1) + 1)
    parent = parents - 8 * (CB * place - 1) + 1
    coarse = jnp.where(coarse_nbr < 0, 0, coarse_nbr - CB * (place - 1) + 1)
    coarse = jnp.pad(coarse, ((0, FB - CB), (0, 0)))
    filler = jnp.zeros((FB, 128 - 34), jnp.int32)
    return jnp.concatenate([fine, parent[:, None], coarse, filler], axis=1).astype(BF)


def spread_sum(sums, groups_y, groups_x, groups_z, swap):
    arrived = lax.ppermute(sums[1], "dp", swap)
    held = (sums[0].astype(F32) + arrived.astype(F32)).astype(BF)
    held = lax.all_to_all(held, "dp", 0, 0, axis_index_groups=groups_y)
    held = jnp.sum(held.astype(F32), axis=0).astype(BF)
    x_count = len(groups_x[0])
    held = held.reshape(x_count, 64 // x_count, 1536)
    held = lax.all_to_all(held, "space", 0, 0, axis_index_groups=groups_x)
    held = jnp.sum(held.astype(F32), axis=0).astype(BF)
    held = held.reshape(held.shape[0], 12, 128)
    held = lax.all_to_all(held, "space", 0, 0, axis_index_groups=groups_z)
    held = jnp.sum(held.astype(F32), axis=0)
    whole = lax.all_gather(held, "dp").reshape(TILES, 128)
    return whole


def gradients(
    fine_features,
    cotangent,
    down_weight,
    coarse_weight,
    up_weight,
    fine_neighbours,
    children,
    parent_slots,
    coarse_neighbours,
):
    features = fine_features.reshape(FB, XL)
    index = encode(fine_neighbours[0], parent_slots[0], coarse_neighbours[0])
    own = jnp.concatenate([features, cotangent.reshape(FB, XL), index], axis=1)
    upper = jnp.concatenate([features[:, s : s + w] for s, w in upper_pieces()], axis=1)
    prev = shift(own, 1)
    nxt = shift(own, -1)
    far = shift(upper, 2)
    turned = coarse_weight.reshape(27, 128, 128)[::-1].transpose(0, 2, 1).reshape(27 * 128, 128)
    core = (lax.axis_index("dp") % 2).astype(jnp.int32).reshape(1)
    decoded, sums = local_pass(
        core, own, prev, nxt, far, down_weight, coarse_weight, turned, up_weight
    )
    return decoded, sums


def body(fine_features, *rest):
    decoded, sums = gradients(fine_features, *rest)
    dp, space = lax.axis_size("dp"), lax.axis_size("space")
    depth = 4
    length = space // depth
    groups_y = [[2 * y + c for y in range(dp // 2)] for c in range(2)]
    groups_x = [[x * length + z for x in range(depth)] for z in range(length)]
    groups_z = [[x * length + z for z in range(length)] for x in range(depth)]
    swap = [(i, i ^ 1) for i in range(dp)]
    whole = spread_sum(sums, groups_y, groups_x, groups_z, swap)
    return (
        decoded.reshape(fine_features.shape),
        whole[0:27].reshape(-1),
        whole[27:81].reshape(-1),
        whole[81:89].reshape(-1),
    )


def solution(mesh):
    in_specs = (
        P("dp", "space", None, None, None),
        P("dp", "space", None, None, None),
        P(),
        P(),
        P(),
        P("dp", "space", None),
        P("dp", "space", None),
        P("dp", "space"),
        P("dp", "space", None),
    )
    out_specs = (P("dp", "space", None, None, None), P("space"), P("space"), P("space"))
    return jax.shard_map(body, mesh=mesh, in_specs=in_specs, out_specs=out_specs, check_vma=False)
```

```python
import functools

import jax
import jax.numpy as jnp
from jax import lax
from jax.experimental import pallas as pl
from jax.experimental.pallas import tpu as pltpu
from jax.sharding import PartitionSpec as P

BF = jnp.bfloat16
F32 = jnp.float32
FB = 24
CB = 6
ROWS = 80
CR = 16
XL = 4096
IDX = 2 * XL
TILES = 96


def plane_lanes(i, j):
    if i == 3:
        return (j * 256, 256)
    if j == 3:
        return (1024 + i * 256, 256)
    return (1792 + (i * 3 + j) * 128, 128)


def upper_pieces():
    pieces = [(3 * 1024, 1024)]
    pieces += [((i * 4 + 3) * 256, 256) for i in range(3)]
    pieces += [((i * 4 + j) * 256 + 128, 128) for i in range(3) for j in range(3)]
    return pieces


UPPER = sum(width for _, width in upper_pieces())
SENT = 1792 + 5 * 128


def dot(a, b, dims=((1,), (0,))):
    return lax.dot_general(a, b, (dims, ((), ())), preferred_element_type=F32)


def gate(v):
    s = 1.0 / (1.0 + jnp.exp(-v))
    return v * s, s * (1.0 + v * (1.0 - s))


def axis_sides(half):
    inner = [(0, 0, half + 1), (0, 1, half + 3)]
    return inner + ([(-1, 1, 0)] if half else [(1, 0, 5)])


def halo_blocks(p, q):
    blocks = []
    for sx, ox, cx in axis_sides(p):
        for sy, oy, cy in axis_sides(q):
            for sz, oz, cells in (
                (0, 0, [(0, 1), (1, 2)]),
                (0, 1, [(0, 3), (1, 4)]),
                (-1, 1, [(1, 0)]),
                (1, 0, [(0, 5)]),
            ):
                code = 9 * (sx + 1) + 3 * (sy + 1) + sz + 1
                if code != 13:
                    targets = [(r, (cx, cy, cz)) for r, cz in cells]
                    blocks.append((code - (code > 13), 4 * ox + 2 * oy + oz, targets))
    return blocks


HALO = len(halo_blocks(0, 0)) * CR


def swap_halves(tile):
    return jnp.concatenate([tile[:, 64:128], tile[:, 0:64]], axis=1)


def octant_of(x, y, z):
    return 4 * (x // 2) + 2 * (y // 2) + z // 2, 4 * (x % 2) + 2 * (y % 2) + z % 2


def kernel(
    own_ref,
    prev_ref,
    next_ref,
    far_ref,
    wd_ref,
    wc_ref,
    wt_ref,
    wu_ref,
    dec_ref,
    sum_ref,
    wide_ref,
    src_ref,
    pad_ref,
    hid_ref,
    nl_ref,
    cin_ref,
    cp_ref,
    cslope_ref,
    cout_ref,
    cs_ref,
    sp_ref,
    cst_ref,
    gd_ref,
    gc_ref,
    gu_ref,
):
    zeros8 = functools.partial(jnp.zeros, dtype=F32)

    def rows(lane, width):
        at = slice(lane, lane + width)
        parts = [r[:, at].astype(F32) for r in (prev_ref, own_ref, next_ref)]
        return jnp.concatenate(parts + [zeros8((ROWS - 3 * FB, width))], axis=0)

    idx = rows(IDX, 128)
    row = lax.broadcasted_iota(jnp.int32, (ROWS, 128), 0)
    lane = lax.broadcasted_iota(jnp.int32, (ROWS, 128), 1)
    block = jnp.where(row >= FB, 1.0, 0.0) + jnp.where(row >= 2 * FB, 1.0, 0.0)
    lane_f = lane.astype(F32)

    wide_ref[...] = jnp.zeros(wide_ref.shape, BF)
    for ab in range(9):
        tap = [wd_ref[(3 * ab + e) * 64 : (3 * ab + e + 1) * 64, :] for e in range(3)]
        for at, e in ((0, 1), (64, 2), (320, 0)):
            wide_ref[ab, at : at + 64, 0:128] = tap[e]
        for at, e in ((64, 0), (128, 1), (192, 2)):
            wide_ref[ab, at : at + 64, 128:256] = tap[e]

    at = 0
    for n, (start, width) in enumerate(upper_pieces()):
        if width > 128:
            far = far_ref[:, at : at + width].astype(F32)
        else:
            tile = 1792 + (n - 4) // 2 * 128
            far = far_ref[:, tile : tile + 128].astype(F32)
            far = far if (n - 4) % 2 else swap_halves(far)
        parts = [far]
        parts += [r[:, start : start + width].astype(F32) for r in (prev_ref, own_ref, next_ref)]
        src_ref[:, at : at + width] = jnp.concatenate(parts, axis=0).astype(BF)
        at += width

    def pick(code):
        wanted = idx[:, code - 1 : code] + (24.0 * block[:, 0:1] - 1.0)
        wanted = jnp.where(idx[:, code - 1 : code] > 0.0, wanted, -1.0)
        hit = jnp.where(lane_f[:, 0 : 4 * FB] == wanted, 1.0, 0.0)
        return hit.astype(BF)

    picks = {code: pick(code) for code in range(1, 8)}

    def fetch(code, i, j, last):
        start, width = plane_lanes(i, j)
        if last:
            start, width = start + width - 128, 128
        return dot(picks[code], src_ref[:, start : start + width]).astype(BF)

    for ip in range(5):
        for jp in range(5):
            i, j = (ip - 1) % 4, (jp - 1) % 4
            code = 4 * (ip == 0) + 2 * (jp == 0)
            if code:
                own = fetch(code, i, j, False)
            else:
                own = rows((i * 4 + j) * 256, 256).astype(BF)
            pad_ref[ip * 5 + jp, :, 0:256] = own
            pad_ref[ip * 5 + jp, :, 256:384] = fetch(code + 1, i, j, True)

    slope_down = []
    for pq in range(4):
        p, q = pq // 2, pq % 2
        taps = [pad_ref[(2 * p + a) * 5 + 2 * q + b] for a in range(3) for b in range(3)]
        pre = dot(jnp.concatenate(taps, axis=1), wide_ref[...].reshape(9 * 384, 256))
        value, slope = gate(pre)
        hid_ref[:, pq * 256 : (pq + 1) * 256] = value.astype(BF)
        slope_down.append(slope[FB : 2 * FB])

    code = idx[:, 7:8]
    slot = jnp.where(code > 0.0, code + (48.0 * block[:, 0:1] - 9.0), -1.0)
    column = (lane % CR * 8 + lane // CR).astype(F32)
    up_f = jnp.where(column == slot, 1.0, 0.0)
    up = up_f.astype(BF)

    def to_coarse(ref):
        return dot(up, ref[...], ((0,), (0,)))

    row16 = lax.broadcasted_iota(jnp.int32, (CR, ROWS), 0)
    lane80 = lax.broadcasted_iota(jnp.int32, (CR, ROWS), 1)
    device = jnp.where(row16 >= CB, 1, 0) + jnp.where(row16 >= 2 * CB, 1, 0)
    choose = jnp.where(lane80 == row16 + (FB - CB) * device, 1.0, 0.0).astype(BF)
    listed = dot(choose, idx.astype(BF))
    device = device[:, 0:1].astype(F32)
    place = listed + (6.0 * device - 7.0)
    place = jnp.where((listed > 0.0) & (place >= 0.0) & (place < CR), place, -1000.0)
    lane16 = lane_f[0:CR]
    for pq in range(4):
        blocks = []
        for m, octant, _ in halo_blocks(pq // 2, pq % 2):
            wanted = place[:, 8 + m : 9 + m] + float(CR * octant)
            blocks.append(jnp.where(lane16 == wanted, 1.0, 0.0))
        nl_ref[pq] = jnp.concatenate(blocks, axis=0).astype(BF)

    def fill(flat_ref, padded_ref):
        for x in range(4):
            for y in range(4):
                for z in range(4):
                    o, v = octant_of(x, y, z)
                    padded_ref[x + 1, y + 1, z + 1] = flat_ref[
                        o * CR : (o + 1) * CR, v * 128 : (v + 1) * 128
                    ]
        for pq in range(4):
            got = dot(nl_ref[pq], flat_ref[:, pq * 256 : (pq + 1) * 256]).astype(BF)
            for n, (_, _, targets) in enumerate(halo_blocks(pq // 2, pq % 2)):
                for r, (cx, cy, cz) in targets:
                    padded_ref[cx, cy, cz] = got[n * CR : (n + 1) * CR, r * 128 : (r + 1) * 128]

    def convolve(padded_ref, weight_ref, x):
        taps = [
            padded_ref[x + a, b : b + 4, e : e + 4].reshape(16 * CR, 128)
            for a in range(3)
            for b in range(3)
            for e in range(3)
        ]
        return dot(jnp.concatenate(taps, axis=1), weight_ref[...])

    def scatter_flat(ref, value, x):
        for yz in range(16):
            o, v = octant_of(x, yz // 4, yz % 4)
            ref[o * CR : (o + 1) * CR, v * 128 : (v + 1) * 128] = value[yz * CR : (yz + 1) * CR]

    cin_ref[...] = to_coarse(hid_ref).astype(BF)
    fill(cin_ref, cp_ref)
    for x in range(4):
        value, slope = gate(convolve(cp_ref, wc_ref, x))
        cslope_ref[x] = slope
        scatter_flat(cout_ref, value.astype(BF), x)

    up_in = dot(up, cout_ref[...])
    own_in, own_grad = [], []
    for v in range(8):
        p, q, r = v // 4, v // 2 % 2, v % 2
        piece = up_in[:, v * 128 : (v + 1) * 128]
        own_in.append(piece[FB : 2 * FB])
        out = dot(piece.astype(BF), wu_ref[...])
        grads = []
        for ab in range(4):
            a, b = ab // 2, ab % 2
            at = ((2 * p + a) * 4 + 2 * q + b) * 256 + r * 128
            joined = out[:, ab * 128 : (ab + 1) * 128] + rows(at, 128)
            value, slope = gate(joined)
            dec_ref[:, at : at + 128] = value[FB : 2 * FB].astype(BF)
            grads.append(rows(XL + at, 128) * slope)
        grad = jnp.concatenate(grads, axis=1)
        own_grad.append(grad[FB : 2 * FB])
        back = dot(grad.astype(BF), wu_ref[...], ((1,), (1,)))
        hid_ref[:, v * 128 : (v + 1) * 128] = back.astype(BF)
    own_in = jnp.concatenate(own_in, axis=0).astype(BF)
    own_grad = jnp.concatenate(own_grad, axis=0).astype(BF)
    found = dot(own_in, own_grad, ((0,), (0,)))
    for n in range(4):
        gu_ref[n] = found[:, n * 128 : (n + 1) * 128]

    cin_ref[...] = to_coarse(hid_ref).astype(BF)
    row_c = lax.broadcasted_iota(jnp.int32, (16 * CR, 128), 0) % CR
    mine = (row_c >= CB) & (row_c < 2 * CB)
    for x in range(4):
        pieces = []
        for yz in range(16):
            o, v = octant_of(x, yz // 4, yz % 4)
            pieces.append(cin_ref[o * CR : (o + 1) * CR, v * 128 : (v + 1) * 128])
        grad = jnp.concatenate(pieces, axis=0).astype(F32) * cslope_ref[x]
        scatter_flat(cs_ref, grad.astype(BF), x)
        kept = jnp.where(mine, grad, 0.0)
        cst_ref[:, x * 256 : (x + 1) * 256] = jnp.transpose(kept).astype(BF)
    for ab in range(9):
        a, b = ab // 3, ab % 3
        taps = [
            cp_ref[a : a + 4, b : b + 4, e : e + 4].reshape(64 * CR, 128) for e in range(3)
        ]
        found = dot(cst_ref[...], jnp.concatenate(taps, axis=1))
        for e in range(3):
            at = (3 * ab + e) * 128
            gc_ref[at : at + 128, :] = jnp.transpose(found[:, e * 128 : (e + 1) * 128])

    fill(cs_ref, sp_ref)
    for x in range(4):
        scatter_flat(cin_ref, convolve(sp_ref, wt_ref, x).astype(BF), x)

    hidden_grad = dot(up_f[FB : 2 * FB].astype(BF), cin_ref[...])
    pieces = []
    for pq in range(4):
        slope = hidden_grad[:, pq * 256 : (pq + 1) * 256] * slope_down[pq]
        pieces += [zeros8((FB, 256)), slope, zeros8((ROWS - 2 * FB, 256))]
    down = jnp.concatenate(pieces, axis=0).astype(BF)
    for ab in range(9):
        a, b = ab // 3, ab % 3
        taps = [pad_ref[(2 * p + a) * 5 + 2 * q + b] for p in range(2) for q in range(2)]
        found = dot(down, jnp.concatenate(taps, axis=0), ((0,), (0,)))
        later = found[0:128, 0:128] + found[128:256, 128:256]
        first = found[0:128, 256:384] + found[128:256, 0:128]
        gd_ref[(3 * ab) * 64 : (3 * ab + 1) * 64, :] = jnp.transpose(first)[64:128]
        gd_ref[(3 * ab + 1) * 64 : (3 * ab + 3) * 64, :] = jnp.transpose(later)

    for t in range(TILES):
        if t < 27:
            tile = gd_ref[pl.ds(t, 64, stride=27), :]
        elif t < 81:
            tile = gc_ref[pl.ds(t - 27, 64, stride=54), :]
        elif t < 89:
            tile = gu_ref[(t - 81) % 4, pl.ds((t - 81) // 4, 64, stride=2), :]
        else:
            tile = jnp.zeros((64, 128), F32)
        n = t % 12
        sum_ref[t // 12 % 2, t // 24, :, n * 128 : (n + 1) * 128] = tile.astype(BF)


def local_pass(own, prev, nxt, far, wd, wc, wt, wu):
    vmem = pl.BlockSpec(memory_space=pltpu.VMEM)
    return pl.pallas_call(
        kernel,
        out_shape=(
            jax.ShapeDtypeStruct((FB, XL), BF),
            jax.ShapeDtypeStruct((2, 4, 64, 1536), BF),
        ),
        in_specs=[vmem] * 8,
        out_specs=(vmem, vmem),
        scratch_shapes=[
            pltpu.VMEM((9, 384, 256), BF),
            pltpu.VMEM((4 * FB, UPPER), BF),
            pltpu.VMEM((25, ROWS, 384), BF),
            pltpu.VMEM((ROWS, 1024), BF),
            pltpu.VMEM((4, HALO, 128), BF),
            pltpu.VMEM((8 * CR, 1024), BF),
            pltpu.VMEM((6, 6, 6, CR, 128), BF),
            pltpu.VMEM((4, 16 * CR, 128), F32),
            pltpu.VMEM((8 * CR, 1024), BF),
            pltpu.VMEM((8 * CR, 1024), BF),
            pltpu.VMEM((6, 6, 6, CR, 128), BF),
            pltpu.VMEM((128, 64 * CR), BF),
            pltpu.VMEM((1728, 128), F32),
            pltpu.VMEM((3456, 128), F32),
            pltpu.VMEM((4, 128, 128), F32),
        ],
        compiler_params=pltpu.CompilerParams(vmem_limit_bytes=48 * 2**20),
    )(own, prev, nxt, far, wd, wc, wt, wu)


def pack(place_ref, x_ref, cot_ref, fine_ref, parent_ref, coarse_ref, own_ref, far_ref):
    place = place_ref[0]
    own_ref[:, 0:XL] = x_ref[...]
    own_ref[:, XL:IDX] = cot_ref[...]
    fine = fine_ref[...]
    fine = jnp.where(fine < 0, 0, fine - (FB * (place - 1) - 1)).astype(F32)
    coarse = coarse_ref[...]
    coarse = jnp.where(coarse < 0, 0, coarse - (CB * (place - 1) - 1)).astype(F32)
    coarse = jnp.concatenate([coarse, jnp.zeros((FB - CB, 26), F32)], axis=0)
    parent = (parent_ref[...] - (8 * (CB * place - 1) - 1)).astype(F32)
    diagonal = lax.broadcasted_iota(jnp.int32, (FB, FB), 0) == lax.broadcasted_iota(
        jnp.int32, (FB, FB), 1
    )
    parent = jnp.sum(jnp.where(diagonal, parent, 0.0), axis=1, keepdims=True)
    filler = jnp.zeros((FB, 128 - 34), F32)
    own_ref[:, IDX : IDX + 128] = jnp.concatenate([fine, parent, coarse, filler], axis=1).astype(BF)
    at = 0
    last = []
    for start, width in upper_pieces():
        if width > 128:
            far_ref[:, at : at + width] = x_ref[:, start : start + width]
        else:
            last.append(x_ref[:, start : start + width].astype(F32))
        at += width
    upper_half = lax.broadcasted_iota(jnp.int32, (FB, 128), 1) >= 64
    for n in range(5):
        first = swap_halves(last[2 * n])
        second = last[2 * n + 1] if 2 * n + 1 < 9 else first
        tile = jnp.where(upper_half, second, first)
        far_ref[:, 1792 + n * 128 : 1920 + n * 128] = tile.astype(BF)


def packed(place, features, cotangent, fine_nbr, parents, coarse_nbr):
    vmem = pl.BlockSpec(memory_space=pltpu.VMEM)
    return pl.pallas_call(
        pack,
        out_shape=(
            jax.ShapeDtypeStruct((FB, IDX + 128), BF),
            jax.ShapeDtypeStruct((FB, SENT), BF),
        ),
        in_specs=[pl.BlockSpec(memory_space=pltpu.SMEM)] + [vmem] * 5,
        out_specs=(vmem, vmem),
    )(place, features, cotangent, fine_nbr, parents, coarse_nbr)


SPACE = ("x", "z")


def shift(block, distance):
    size = lax.axis_size(SPACE)
    route = [(i, i + distance) for i in range(size) if 0 <= i + distance < size]
    return lax.ppermute(block, SPACE, route)


def spread_sum(sums):
    held = lax.all_to_all(sums, "core", 0, 0)
    held = jnp.sum(held.astype(F32), axis=0).astype(BF)
    held = held.reshape(16, 16, 1536)
    held = lax.all_to_all(held, ("y", "x"), 0, 0)
    held = jnp.sum(held.astype(F32), axis=0).astype(BF)
    held = held.reshape(16, 12, 128)
    held = lax.all_to_all(held, "z", 0, 0)
    held = jnp.sum(held.astype(F32), axis=0)
    held = jnp.broadcast_to(held[None], (8, 12, 128))
    held = lax.all_to_all(held, ("y", "core"), 0, 0)
    return held.reshape(TILES, 128)


def gradients(
    fine_features,
    cotangent,
    down_weight,
    coarse_weight,
    up_weight,
    fine_neighbours,
    children,
    parent_slots,
    coarse_neighbours,
):
    place = lax.axis_index(SPACE).astype(jnp.int32).reshape(1)
    own, upper = packed(
        place,
        fine_features.reshape(FB, XL),
        cotangent.reshape(FB, XL),
        fine_neighbours[0],
        parent_slots,
        coarse_neighbours[0],
    )
    prev = shift(own, 1)
    far = shift(upper, 2)
    nxt = shift(own, -1)
    turned = coarse_weight.reshape(27, 128, 128)[::-1].transpose(0, 2, 1).reshape(27 * 128, 128)
    return local_pass(own, prev, nxt, far, down_weight, coarse_weight, turned, up_weight)


def body(fine_features, *rest):
    decoded, sums = gradients(fine_features, *rest)
    whole = spread_sum(sums)
    return (
        decoded.reshape(fine_features.shape),
        whole[0:27].reshape(-1),
        whole[27:81].reshape(-1),
        whole[81:89].reshape(-1),
    )


def solution(mesh):
    mesh = jax.sharding.Mesh(mesh.devices.reshape(4, 2, 4, 16), ("y", "core", "x", "z"))
    dp = ("y", "core")
    in_specs = (
        P(dp, SPACE, None, None, None),
        P(dp, SPACE, None, None, None),
        P(),
        P(),
        P(),
        P(dp, SPACE, None),
        P(dp, SPACE, None),
        P(dp, SPACE),
        P(dp, SPACE, None),
    )
    out_specs = (P(dp, SPACE, None, None, None), P(SPACE), P(SPACE), P(SPACE))
    return jax.shard_map(body, mesh=mesh, in_specs=in_specs, out_specs=out_specs, check_vma=False)
```

```python
import functools

import jax
import jax.numpy as jnp
from jax import lax
from jax.experimental import pallas as pl
from jax.experimental.pallas import tpu as pltpu
from jax.sharding import PartitionSpec as P

BF = jnp.bfloat16
F32 = jnp.float32
FB = 24
CB = 6
ROWS = 80
CR = 16
XL = 4096
IDX = 2 * XL
TILES = 96


def plane_lanes(i, j):
    if i == 3:
        return (j * 256, 256)
    if j == 3:
        return (1024 + i * 256, 256)
    return (1792 + (i * 3 + j) * 128, 128)


def upper_pieces():
    pieces = [(3 * 1024, 1024)]
    pieces += [((i * 4 + 3) * 256, 256) for i in range(3)]
    pieces += [((i * 4 + j) * 256 + 128, 128) for i in range(3) for j in range(3)]
    return pieces


UPPER = sum(width for _, width in upper_pieces())
SENT = 1792 + 5 * 128


def dot(a, b, dims=((1,), (0,))):
    return lax.dot_general(a, b, (dims, ((), ())), preferred_element_type=F32)


def gate(v):
    s = 1.0 / (1.0 + jnp.exp(-v))
    return v * s, s * (1.0 + v * (1.0 - s))


def axis_sides(half):
    inner = [(0, 0, half + 1), (0, 1, half + 3)]
    return inner + ([(-1, 1, 0)] if half else [(1, 0, 5)])


def halo_blocks(p, q):
    blocks = []
    for sx, ox, cx in axis_sides(p):
        for sy, oy, cy in axis_sides(q):
            for sz, oz, cells in (
                (0, 0, [(0, 1), (1, 2)]),
                (0, 1, [(0, 3), (1, 4)]),
                (-1, 1, [(1, 0)]),
                (1, 0, [(0, 5)]),
            ):
                code = 9 * (sx + 1) + 3 * (sy + 1) + sz + 1
                if code != 13:
                    targets = [(r, (cx, cy, cz)) for r, cz in cells]
                    blocks.append((code - (code > 13), 4 * ox + 2 * oy + oz, targets))
    return blocks


HALO = len(halo_blocks(0, 0)) * CR


def swap_halves(tile):
    return jnp.concatenate([tile[:, 64:128], tile[:, 0:64]], axis=1)


def octant_of(x, y, z):
    return 4 * (x // 2) + 2 * (y // 2) + z // 2, 4 * (x % 2) + 2 * (y % 2) + z % 2


def kernel(
    own_ref,
    next_ref,
    prev_ref,
    far_ref,
    wd_ref,
    wc_ref,
    wt_ref,
    wu_ref,
    dec_ref,
    sum_ref,
    wide_ref,
    src_ref,
    pad_ref,
    hid_ref,
    nl_ref,
    cin_ref,
    cp_ref,
    cslope_ref,
    cout_ref,
    cs_ref,
    sp_ref,
    cst_ref,
    gd_ref,
    gc_ref,
    gu_ref,
):
    zeros8 = functools.partial(jnp.zeros, dtype=F32)

    def rows(lane, width):
        at = slice(lane, lane + width)
        parts = [r[:, at].astype(F32) for r in (prev_ref, own_ref, next_ref)]
        return jnp.concatenate(parts + [zeros8((ROWS - 3 * FB, width))], axis=0)

    idx = rows(IDX, 128)
    row = lax.broadcasted_iota(jnp.int32, (ROWS, 128), 0)
    lane = lax.broadcasted_iota(jnp.int32, (ROWS, 128), 1)
    block = jnp.where(row >= FB, 1.0, 0.0) + jnp.where(row >= 2 * FB, 1.0, 0.0)
    lane_f = lane.astype(F32)

    wide_ref[...] = jnp.zeros(wide_ref.shape, BF)
    for ab in range(9):
        tap = [wd_ref[(3 * ab + e) * 64 : (3 * ab + e + 1) * 64, :] for e in range(3)]
        for at, e in ((0, 1), (64, 2), (320, 0)):
            wide_ref[ab, at : at + 64, 0:128] = tap[e]
        for at, e in ((64, 0), (128, 1), (192, 2)):
            wide_ref[ab, at : at + 64, 128:256] = tap[e]

    at = 0
    for n, (start, width) in enumerate(upper_pieces()):
        if width > 128:
            far = far_ref[:, at : at + width].astype(F32)
        else:
            tile = 1792 + (n - 4) // 2 * 128
            far = far_ref[:, tile : tile + 128].astype(F32)
            far = far if (n - 4) % 2 else swap_halves(far)
        parts = [far]
        parts += [r[:, start : start + width].astype(F32) for r in (prev_ref, own_ref, next_ref)]
        src_ref[:, at : at + width] = jnp.concatenate(parts, axis=0).astype(BF)
        at += width

    def pick(code):
        wanted = idx[:, code - 1 : code] + (24.0 * block[:, 0:1] - 1.0)
        wanted = jnp.where(idx[:, code - 1 : code] > 0.0, wanted, -1.0)
        hit = jnp.where(lane_f[:, 0 : 4 * FB] == wanted, 1.0, 0.0)
        return hit.astype(BF)

    picks = {code: pick(code) for code in range(1, 8)}

    def fetch(code, i, j, last):
        start, width = plane_lanes(i, j)
        if last:
            start, width = start + width - 128, 128
        return dot(picks[code], src_ref[:, start : start + width]).astype(BF)

    for ip in range(5):
        for jp in range(5):
            i, j = (ip - 1) % 4, (jp - 1) % 4
            code = 4 * (ip == 0) + 2 * (jp == 0)
            if code:
                own = fetch(code, i, j, False)
            else:
                own = rows((i * 4 + j) * 256, 256).astype(BF)
            pad_ref[ip * 5 + jp, :, 0:256] = own
            pad_ref[ip * 5 + jp, :, 256:384] = fetch(code + 1, i, j, True)

    slope_down = []
    for pq in range(4):
        p, q = pq // 2, pq % 2
        taps = [pad_ref[(2 * p + a) * 5 + 2 * q + b] for a in range(3) for b in range(3)]
        pre = dot(jnp.concatenate(taps, axis=1), wide_ref[...].reshape(9 * 384, 256))
        value, slope = gate(pre)
        hid_ref[:, pq * 256 : (pq + 1) * 256] = value.astype(BF)
        slope_down.append(slope[FB : 2 * FB])

    code = idx[:, 7:8]
    slot = jnp.where(code > 0.0, code + (48.0 * block[:, 0:1] - 9.0), -1.0)
    column = (lane % CR * 8 + lane // CR).astype(F32)
    up_f = jnp.where(column == slot, 1.0, 0.0)
    up = up_f.astype(BF)

    def to_coarse(ref):
        return dot(up, ref[...], ((0,), (0,)))

    row16 = lax.broadcasted_iota(jnp.int32, (CR, ROWS), 0)
    lane80 = lax.broadcasted_iota(jnp.int32, (CR, ROWS), 1)
    device = jnp.where(row16 >= CB, 1, 0) + jnp.where(row16 >= 2 * CB, 1, 0)
    choose = jnp.where(lane80 == row16 + (FB - CB) * device, 1.0, 0.0).astype(BF)
    listed = dot(choose, idx.astype(BF))
    device = device[:, 0:1].astype(F32)
    place = listed + (6.0 * device - 7.0)
    place = jnp.where((listed > 0.0) & (place >= 0.0) & (place < CR), place, -1000.0)
    lane16 = lane_f[0:CR]
    for pq in range(4):
        blocks = []
        for m, octant, _ in halo_blocks(pq // 2, pq % 2):
            wanted = place[:, 8 + m : 9 + m] + float(CR * octant)
            blocks.append(jnp.where(lane16 == wanted, 1.0, 0.0))
        nl_ref[pq] = jnp.concatenate(blocks, axis=0).astype(BF)

    def fill(flat_ref, padded_ref):
        for x in range(4):
            for y in range(4):
                for z in range(4):
                    o, v = octant_of(x, y, z)
                    padded_ref[x + 1, y + 1, z + 1] = flat_ref[
                        o * CR : (o + 1) * CR, v * 128 : (v + 1) * 128
                    ]
        for pq in range(4):
            got = dot(nl_ref[pq], flat_ref[:, pq * 256 : (pq + 1) * 256]).astype(BF)
            for n, (_, _, targets) in enumerate(halo_blocks(pq // 2, pq % 2)):
                for r, (cx, cy, cz) in targets:
                    padded_ref[cx, cy, cz] = got[n * CR : (n + 1) * CR, r * 128 : (r + 1) * 128]

    def convolve(padded_ref, weight_ref, x):
        taps = [
            padded_ref[x + a, b : b + 4, e : e + 4].reshape(16 * CR, 128)
            for a in range(3)
            for b in range(3)
            for e in range(3)
        ]
        return dot(jnp.concatenate(taps, axis=1), weight_ref[...])

    def scatter_flat(ref, value, x):
        for yz in range(16):
            o, v = octant_of(x, yz // 4, yz % 4)
            ref[o * CR : (o + 1) * CR, v * 128 : (v + 1) * 128] = value[yz * CR : (yz + 1) * CR]

    cin_ref[...] = to_coarse(hid_ref).astype(BF)
    fill(cin_ref, cp_ref)
    for x in range(4):
        value, slope = gate(convolve(cp_ref, wc_ref, x))
        cslope_ref[x] = slope
        scatter_flat(cout_ref, value.astype(BF), x)

    up_in = dot(up, cout_ref[...])
    own_in, own_grad = [], []
    for v in range(8):
        p, q, r = v // 4, v // 2 % 2, v % 2
        piece = up_in[:, v * 128 : (v + 1) * 128]
        own_in.append(piece[FB : 2 * FB])
        out = dot(piece.astype(BF), wu_ref[...])
        grads = []
        for ab in range(4):
            a, b = ab // 2, ab % 2
            at = ((2 * p + a) * 4 + 2 * q + b) * 256 + r * 128
            joined = out[:, ab * 128 : (ab + 1) * 128] + rows(at, 128)
            value, slope = gate(joined)
            dec_ref[:, at : at + 128] = value[FB : 2 * FB].astype(BF)
            grads.append(rows(XL + at, 128) * slope)
        grad = jnp.concatenate(grads, axis=1)
        own_grad.append(grad[FB : 2 * FB])
        back = dot(grad.astype(BF), wu_ref[...], ((1,), (1,)))
        hid_ref[:, v * 128 : (v + 1) * 128] = back.astype(BF)
    own_in = jnp.concatenate(own_in, axis=0).astype(BF)
    own_grad = jnp.concatenate(own_grad, axis=0).astype(BF)
    found = dot(own_in, own_grad, ((0,), (0,)))
    for n in range(4):
        gu_ref[n] = found[:, n * 128 : (n + 1) * 128]

    cin_ref[...] = to_coarse(hid_ref).astype(BF)
    row_c = lax.broadcasted_iota(jnp.int32, (16 * CR, 128), 0) % CR
    mine = (row_c >= CB) & (row_c < 2 * CB)
    for x in range(4):
        pieces = []
        for yz in range(16):
            o, v = octant_of(x, yz // 4, yz % 4)
            pieces.append(cin_ref[o * CR : (o + 1) * CR, v * 128 : (v + 1) * 128])
        grad = jnp.concatenate(pieces, axis=0).astype(F32) * cslope_ref[x]
        scatter_flat(cs_ref, grad.astype(BF), x)
        kept = jnp.where(mine, grad, 0.0)
        cst_ref[:, x * 256 : (x + 1) * 256] = jnp.transpose(kept).astype(BF)
    for ab in range(9):
        a, b = ab // 3, ab % 3
        taps = [
            cp_ref[a : a + 4, b : b + 4, e : e + 4].reshape(64 * CR, 128) for e in range(3)
        ]
        found = dot(cst_ref[...], jnp.concatenate(taps, axis=1))
        for e in range(3):
            at = (3 * ab + e) * 128
            gc_ref[at : at + 128, :] = jnp.transpose(found[:, e * 128 : (e + 1) * 128])

    fill(cs_ref, sp_ref)
    for x in range(4):
        scatter_flat(cin_ref, convolve(sp_ref, wt_ref, x).astype(BF), x)

    hidden_grad = dot(up_f[FB : 2 * FB].astype(BF), cin_ref[...])
    pieces = []
    for pq in range(4):
        slope = hidden_grad[:, pq * 256 : (pq + 1) * 256] * slope_down[pq]
        pieces += [zeros8((FB, 256)), slope, zeros8((ROWS - 2 * FB, 256))]
    down = jnp.concatenate(pieces, axis=0).astype(BF)
    for ab in range(9):
        a, b = ab // 3, ab % 3
        taps = [pad_ref[(2 * p + a) * 5 + 2 * q + b] for p in range(2) for q in range(2)]
        found = dot(down, jnp.concatenate(taps, axis=0), ((0,), (0,)))
        later = found[0:128, 0:128] + found[128:256, 128:256]
        first = found[0:128, 256:384] + found[128:256, 0:128]
        gd_ref[(3 * ab) * 64 : (3 * ab + 1) * 64, :] = jnp.transpose(first)[64:128]
        gd_ref[(3 * ab + 1) * 64 : (3 * ab + 3) * 64, :] = jnp.transpose(later)

    for t in range(TILES):
        if t < 27:
            tile = gd_ref[pl.ds(t, 64, stride=27), :]
        elif t < 81:
            tile = gc_ref[pl.ds(t - 27, 64, stride=54), :]
        elif t < 89:
            tile = gu_ref[(t - 81) % 4, pl.ds((t - 81) // 4, 64, stride=2), :]
        else:
            tile = jnp.zeros((64, 128), F32)
        n = t % 12
        sum_ref[t // 12 % 2, t // 24, :, n * 128 : (n + 1) * 128] = tile.astype(BF)


def local_pass(own, prev, nxt, far, wd, wc, wt, wu):
    vmem = pl.BlockSpec(memory_space=pltpu.VMEM)
    return pl.pallas_call(
        kernel,
        out_shape=(
            jax.ShapeDtypeStruct((FB, XL), BF),
            jax.ShapeDtypeStruct((2, 4, 64, 1536), BF),
        ),
        in_specs=[vmem] * 8,
        out_specs=(vmem, vmem),
        scratch_shapes=[
            pltpu.VMEM((9, 384, 256), BF),
            pltpu.VMEM((4 * FB, UPPER), BF),
            pltpu.VMEM((25, ROWS, 384), BF),
            pltpu.VMEM((ROWS, 1024), BF),
            pltpu.VMEM((4, HALO, 128), BF),
            pltpu.VMEM((8 * CR, 1024), BF),
            pltpu.VMEM((6, 6, 6, CR, 128), BF),
            pltpu.VMEM((4, 16 * CR, 128), F32),
            pltpu.VMEM((8 * CR, 1024), BF),
            pltpu.VMEM((8 * CR, 1024), BF),
            pltpu.VMEM((6, 6, 6, CR, 128), BF),
            pltpu.VMEM((128, 64 * CR), BF),
            pltpu.VMEM((1728, 128), F32),
            pltpu.VMEM((3456, 128), F32),
            pltpu.VMEM((4, 128, 128), F32),
        ],
        compiler_params=pltpu.CompilerParams(vmem_limit_bytes=48 * 2**20),
    )(own, nxt, prev, far, wd, wc, wt, wu)


def pack(place_ref, x_ref, cot_ref, fine_ref, parent_ref, coarse_ref, own_ref, far_ref):
    place = place_ref[0]
    own_ref[:, 0:XL] = x_ref[...].reshape(FB, XL)
    own_ref[:, XL:IDX] = cot_ref[...].reshape(FB, XL)
    fine = jnp.concatenate([fine_ref[m] for m in range(7)], axis=0)
    fine = jnp.where(fine < 0, 0, fine - (FB * (place - 1) - 1)).astype(F32)
    coarse = jnp.concatenate([coarse_ref[c] for c in range(CB)], axis=0)
    coarse = jnp.where(coarse < 0, 0, coarse - (CB * (place - 1) - 1)).astype(F32)
    coarse = jnp.concatenate([coarse, jnp.zeros((FB - CB, 26), F32)], axis=0)
    parent = (parent_ref[...] - (8 * (CB * place - 1) - 1)).astype(F32)
    lists = jnp.concatenate([fine, parent], axis=0).astype(BF)
    unit = lax.broadcasted_iota(jnp.int32, (FB, FB), 0) == lax.broadcasted_iota(
        jnp.int32, (FB, FB), 1
    )
    lists = dot(jnp.where(unit, 1.0, 0.0).astype(BF), lists, ((1,), (1,)))
    filler = jnp.zeros((FB, 128 - 34), F32)
    own_ref[:, IDX : IDX + 128] = jnp.concatenate([lists, coarse, filler], axis=1).astype(BF)
    at = 0
    last = []
    for start, width in upper_pieces():
        if width > 128:
            far_ref[:, at : at + width] = own_ref[:, start : start + width]
        else:
            last.append(own_ref[:, start : start + width].astype(F32))
        at += width
    upper_half = lax.broadcasted_iota(jnp.int32, (FB, 128), 1) >= 64
    for n in range(5):
        first = swap_halves(last[2 * n])
        second = last[2 * n + 1] if 2 * n + 1 < 9 else first
        tile = jnp.where(upper_half, second, first)
        far_ref[:, 1792 + n * 128 : 1920 + n * 128] = tile.astype(BF)


def packed(place, features, cotangent, fine_nbr, parents, coarse_nbr):
    vmem = pl.BlockSpec(memory_space=pltpu.VMEM)
    return pl.pallas_call(
        pack,
        out_shape=(
            jax.ShapeDtypeStruct((FB, IDX + 128), BF),
            jax.ShapeDtypeStruct((FB, SENT), BF),
        ),
        in_specs=[pl.BlockSpec(memory_space=pltpu.SMEM)] + [vmem] * 5,
        out_specs=(vmem, vmem),
        compiler_params=pltpu.CompilerParams(vmem_limit_bytes=8 * 2**20),
    )(place, features, cotangent, fine_nbr, parents, coarse_nbr)


SPACE = ("x", "z")


def shift(block, distance):
    size = lax.axis_size(SPACE)
    route = [(i, i + distance) for i in range(size) if 0 <= i + distance < size]
    return lax.ppermute(block, SPACE, route)


def sum_copies(in_ref, out_ref):
    total = jnp.sum(in_ref[...].astype(F32), axis=0)
    for n in range(out_ref.shape[0]):
        out_ref[n] = total


def split(in_ref, down_ref, coarse_ref, up_ref):
    whole = jnp.concatenate([in_ref[n] for n in range(8)], axis=0)
    down_ref[...] = whole[0:27]
    coarse_ref[...] = whole[27:81]
    up_ref[...] = whole[81:89]


def spread_sum(sums):
    held = lax.all_to_all(sums, "core", 0, 0)
    held = jnp.sum(held.astype(F32), axis=0).astype(BF)
    held = held.reshape(16, 16, 1536)
    held = lax.all_to_all(held, ("y", "x"), 0, 0)
    held = jnp.sum(held.astype(F32), axis=0).astype(BF)
    held = held.reshape(16, 12, 128)
    held = lax.all_to_all(held, "z", 0, 0)
    held = pl.pallas_call(
        sum_copies,
        out_shape=jax.ShapeDtypeStruct((8, 12, 128), F32),
        compiler_params=pltpu.CompilerParams(vmem_limit_bytes=2 * 2**20),
    )(held)
    held = lax.all_to_all(held, ("y", "core"), 0, 0)
    shares = pl.pallas_call(
        split,
        out_shape=tuple(jax.ShapeDtypeStruct((n, 128), F32) for n in (27, 54, 8)),
        compiler_params=pltpu.CompilerParams(vmem_limit_bytes=2 * 2**20),
    )(held)
    return tuple(share.reshape(-1) for share in shares)


def gradients(
    fine_features,
    cotangent,
    down_weight,
    coarse_weight,
    up_weight,
    fine_neighbours,
    children,
    parent_slots,
    coarse_neighbours,
):
    place = lax.axis_index(SPACE).astype(jnp.int32).reshape(1)
    own, upper = packed(
        place,
        fine_features[0],
        cotangent[0],
        fine_neighbours.transpose(2, 0, 1),
        parent_slots,
        coarse_neighbours[0].reshape(CB, 1, 26),
    )
    prev = shift(own, 1)
    far = shift(upper, 2)
    nxt = shift(own, -1)
    turned = coarse_weight.reshape(27, 128, 128)[::-1].transpose(0, 2, 1).reshape(27 * 128, 128)
    return local_pass(own, prev, nxt, far, down_weight, coarse_weight, turned, up_weight)


def body(fine_features, *rest):
    decoded, sums = gradients(fine_features, *rest)
    return (decoded.reshape(fine_features.shape), *spread_sum(sums))


def solution(mesh):
    mesh = jax.sharding.Mesh(mesh.devices.reshape(4, 2, 4, 16), ("y", "core", "x", "z"))
    dp = ("y", "core")
    in_specs = (
        P(dp, SPACE, None, None, None),
        P(dp, SPACE, None, None, None),
        P(),
        P(),
        P(),
        P(dp, SPACE, None),
        P(dp, SPACE, None),
        P(dp, SPACE),
        P(dp, SPACE, None),
    )
    out_specs = (P(dp, SPACE, None, None, None), P(SPACE), P(SPACE), P(SPACE))
    return jax.shard_map(body, mesh=mesh, in_specs=in_specs, out_specs=out_specs, check_vma=False)
```

```python
import functools

import jax
import jax.numpy as jnp
from jax import lax
from jax.experimental import pallas as pl
from jax.experimental.pallas import tpu as pltpu
from jax.sharding import PartitionSpec as P

BF = jnp.bfloat16
F32 = jnp.float32
FB = 24
CB = 6
ROWS = 80
CR = 16
XL = 4096
IDX = 2 * XL
TILES = 96


def plane_lanes(i, j):
    if i == 3:
        return (j * 256, 256)
    if j == 3:
        return (1024 + i * 256, 256)
    return (1792 + (i * 3 + j) * 128, 128)


def upper_pieces():
    pieces = [(3 * 1024, 1024)]
    pieces += [((i * 4 + 3) * 256, 256) for i in range(3)]
    pieces += [((i * 4 + j) * 256 + 128, 128) for i in range(3) for j in range(3)]
    return pieces


UPPER = sum(width for _, width in upper_pieces())
SENT = 1792 + 5 * 128


def dot(a, b, dims=((1,), (0,))):
    return lax.dot_general(a, b, (dims, ((), ())), preferred_element_type=F32)


def gate(v):
    s = 1.0 / (1.0 + jnp.exp(-v))
    return v * s, s * (1.0 + v * (1.0 - s))


def axis_sides(half):
    inner = [(0, 0, half + 1), (0, 1, half + 3)]
    return inner + ([(-1, 1, 0)] if half else [(1, 0, 5)])


def halo_blocks(p, q):
    blocks = []
    for sx, ox, cx in axis_sides(p):
        for sy, oy, cy in axis_sides(q):
            for sz, oz, cells in (
                (0, 0, [(0, 1), (1, 2)]),
                (0, 1, [(0, 3), (1, 4)]),
                (-1, 1, [(1, 0)]),
                (1, 0, [(0, 5)]),
            ):
                code = 9 * (sx + 1) + 3 * (sy + 1) + sz + 1
                if code != 13:
                    targets = [(r, (cx, cy, cz)) for r, cz in cells]
                    blocks.append((code - (code > 13), 4 * ox + 2 * oy + oz, targets))
    return blocks


HALO = len(halo_blocks(0, 0)) * CR


def swap_halves(tile):
    return jnp.concatenate([tile[:, 64:128], tile[:, 0:64]], axis=1)


def octant_of(x, y, z):
    return 4 * (x // 2) + 2 * (y // 2) + z // 2, 4 * (x % 2) + 2 * (y % 2) + z % 2


def widen(wd_ref, wc_ref, down_ref, coarse_ref, turned_ref):
    down_ref[...] = jnp.zeros(down_ref.shape, BF)
    for ab in range(9):
        tap = [wd_ref[(3 * ab + e) * 64 : (3 * ab + e + 1) * 64, :] for e in range(3)]
        at = ab * 384
        for row, e in ((0, 1), (64, 2), (320, 0)):
            down_ref[at + row : at + row + 64, 0:128] = tap[e]
        for row, e in ((64, 0), (128, 1), (192, 2)):
            down_ref[at + row : at + row + 64, 128:256] = tap[e]
    zero = jnp.zeros((128, 128), BF)
    for ab in range(9):
        for e in range(3):
            tap = 3 * ab + e
            plain = wc_ref[tap * 128 : (tap + 1) * 128, :]
            other = (26 - tap) * 128
            turned = jnp.transpose(wc_ref[other : other + 128, :].astype(F32)).astype(BF)
            for ref, block in ((coarse_ref, plain), (turned_ref, turned)):
                for r in range(2):
                    row = ab * 512 + (e + r) * 128
                    ref[row : row + 128, r * 128 : (r + 1) * 128] = block
        for ref in (coarse_ref, turned_ref):
            ref[ab * 512 + 384 : ab * 512 + 512, 0:128] = zero
            ref[ab * 512 : ab * 512 + 128, 128:256] = zero


def widened(down_weight, coarse_weight):
    vmem = pl.BlockSpec(memory_space=pltpu.VMEM)
    shapes = ((9 * 384, 256), (9 * 512, 256), (9 * 512, 256))
    return pl.pallas_call(
        widen,
        out_shape=tuple(jax.ShapeDtypeStruct(shape, BF) for shape in shapes),
        in_specs=[vmem] * 2,
        out_specs=(vmem,) * 3,
        compiler_params=pltpu.CompilerParams(vmem_limit_bytes=12 * 2**20),
    )(down_weight, coarse_weight)


def kernel(
    own_ref,
    next_ref,
    prev_ref,
    far_ref,
    wd_ref,
    wc_ref,
    wt_ref,
    wu_ref,
    dec_ref,
    sum_ref,
    src_ref,
    pad_ref,
    mine_ref,
    hid_ref,
    nl_ref,
    cin_ref,
    cp_ref,
    cslope_ref,
    cout_ref,
    cs_ref,
    sp_ref,
    cst_ref,
    gd_ref,
    gc_ref,
    gu_ref,
):
    zeros8 = functools.partial(jnp.zeros, dtype=F32)

    def rows(lane, width):
        at = slice(lane, lane + width)
        parts = [r[:, at].astype(F32) for r in (prev_ref, own_ref, next_ref)]
        return jnp.concatenate(parts + [zeros8((ROWS - 3 * FB, width))], axis=0)

    idx = rows(IDX, 128)
    row = lax.broadcasted_iota(jnp.int32, (ROWS, 128), 0)
    lane = lax.broadcasted_iota(jnp.int32, (ROWS, 128), 1)
    block = jnp.where(row >= FB, 1.0, 0.0) + jnp.where(row >= 2 * FB, 1.0, 0.0)
    lane_f = lane.astype(F32)

    at = 0
    for n, (start, width) in enumerate(upper_pieces()):
        if width > 128:
            far = far_ref[:, at : at + width].astype(F32)
        else:
            tile = 1792 + (n - 4) // 2 * 128
            far = far_ref[:, tile : tile + 128].astype(F32)
            far = far if (n - 4) % 2 else swap_halves(far)
        parts = [far]
        parts += [r[:, start : start + width].astype(F32) for r in (prev_ref, own_ref, next_ref)]
        src_ref[:, at : at + width] = jnp.concatenate(parts, axis=0).astype(BF)
        at += width

    def pick(code):
        wanted = idx[:, code - 1 : code] + (24.0 * block[:, 0:1] - 1.0)
        wanted = jnp.where(idx[:, code - 1 : code] > 0.0, wanted, -1.0)
        hit = jnp.where(lane_f[:, 0 : 4 * FB] == wanted, 1.0, 0.0)
        return hit.astype(BF)

    picks = {code: pick(code) for code in range(1, 8)}

    def fetch(code, i, j, last):
        start, width = plane_lanes(i, j)
        if last:
            start, width = start + width - 128, 128
        return dot(picks[code], src_ref[:, start : start + width])

    def only_own(array):
        return jnp.concatenate([array[FB : 2 * FB], zeros8((8, array.shape[1]))], axis=0)

    for ip in range(5):
        for jp in range(5):
            i, j = (ip - 1) % 4, (jp - 1) % 4
            code = 4 * (ip == 0) + 2 * (jp == 0)
            if code:
                own = fetch(code, i, j, False)
            else:
                own = rows((i * 4 + j) * 256, 256)
            behind = fetch(code + 1, i, j, True)
            pad_ref[ip * 5 + jp, :, 0:256] = own.astype(BF)
            pad_ref[ip * 5 + jp, :, 256:384] = behind.astype(BF)
            mine_ref[ip * 5 + jp, :, 0:256] = only_own(own).astype(BF)
            mine_ref[ip * 5 + jp, :, 256:384] = only_own(behind).astype(BF)

    outs = []
    for p in range(2):
        for q in range(2):
            taps = [pad_ref[(2 * p + a) * 5 + 2 * q + b] for a in range(3) for b in range(3)]
            outs.append(dot(jnp.concatenate(taps, axis=1), wd_ref[...]))
    pre = jnp.concatenate(outs, axis=0)
    slope_down = []
    for pq in range(4):
        value, slope = gate(pre[pq * ROWS : (pq + 1) * ROWS])
        hid_ref[:, pq * 256 : (pq + 1) * 256] = value.astype(BF)
        slope_down.append(slope[FB : 2 * FB])

    code = idx[:, 7:8]
    slot = jnp.where(code > 0.0, code + (48.0 * block[:, 0:1] - 9.0), -1.0)
    column = (lane % CR * 8 + lane // CR).astype(F32)
    up_f = jnp.where(column == slot, 1.0, 0.0)
    up = up_f.astype(BF)

    def to_coarse(ref):
        return dot(up, ref[...], ((0,), (0,)))

    row16 = lax.broadcasted_iota(jnp.int32, (CR, ROWS), 0)
    lane80 = lax.broadcasted_iota(jnp.int32, (CR, ROWS), 1)
    device = jnp.where(row16 >= CB, 1, 0) + jnp.where(row16 >= 2 * CB, 1, 0)
    choose = jnp.where(lane80 == row16 + (FB - CB) * device, 1.0, 0.0).astype(BF)
    listed = dot(choose, idx.astype(BF))
    device = device[:, 0:1].astype(F32)
    place = listed + (6.0 * device - 7.0)
    place = jnp.where((listed > 0.0) & (place >= 0.0) & (place < CR), place, -1000.0)
    lane16 = lane_f[0:CR]
    for pq in range(4):
        blocks = []
        for m, octant, _ in halo_blocks(pq // 2, pq % 2):
            wanted = place[:, 8 + m : 9 + m] + float(CR * octant)
            blocks.append(jnp.where(lane16 == wanted, 1.0, 0.0))
        nl_ref[pq] = jnp.concatenate(blocks, axis=0).astype(BF)

    def fill(flat_ref, padded_ref):
        for x in range(4):
            for y in range(4):
                for z in range(4):
                    o, v = octant_of(x, y, z)
                    padded_ref[x + 1, y + 1, (z + 1) // 2, (z + 1) % 2] = flat_ref[
                        o * CR : (o + 1) * CR, v * 128 : (v + 1) * 128
                    ]
        for pq in range(4):
            got = dot(nl_ref[pq], flat_ref[:, pq * 256 : (pq + 1) * 256]).astype(BF)
            for n, (_, _, targets) in enumerate(halo_blocks(pq // 2, pq % 2)):
                for r, (cx, cy, cz) in targets:
                    padded_ref[cx, cy, cz // 2, cz % 2] = got[
                        n * CR : (n + 1) * CR, r * 128 : (r + 1) * 128
                    ]

    def convolve(padded_ref, weight_ref):
        outs = []
        for x in range(0, 4, 1):
            taps = [
                padded_ref[x + a : x + a + 1, b : b + 4, zz // 2 : zz // 2 + 2, zz % 2].reshape(1 * 8 * CR, 128)
                for a in range(3)
                for b in range(3)
                for zz in range(4)
            ]
            outs.append(dot(jnp.concatenate(taps, axis=1), weight_ref[...]))
        return jnp.concatenate(outs, axis=0)

    voxels = [
        (row * CR, r * 128, octant_of(row // 8, row // 2 % 4, row % 2 * 2 + r))
        for row in range(32)
        for r in range(2)
    ]

    def scatter_flat(ref, value):
        for row, lane, (o, v) in voxels:
            piece = value[row : row + CR, lane : lane + 128]
            ref[o * CR : (o + 1) * CR, v * 128 : (v + 1) * 128] = piece

    cin_ref[...] = to_coarse(hid_ref).astype(BF)
    fill(cin_ref, cp_ref)
    value, slope = gate(convolve(cp_ref, wc_ref))
    cslope_ref[...] = slope
    scatter_flat(cout_ref, value.astype(BF))

    up_in = dot(up, cout_ref[...])
    pieces = [up_in[:, v * 128 : (v + 1) * 128] for v in range(8)]
    own_in = [piece[FB : 2 * FB] for piece in pieces]
    out = dot(jnp.concatenate(pieces, axis=0).astype(BF), wu_ref[...])
    all_grad, own_grad = [], []
    for v in range(8):
        p, q, r = v // 4, v // 2 % 2, v % 2
        grads = []
        for ab in range(4):
            a, b = ab // 2, ab % 2
            at = ((2 * p + a) * 4 + 2 * q + b) * 256 + r * 128
            joined = out[v * ROWS : (v + 1) * ROWS, ab * 128 : (ab + 1) * 128] + rows(at, 128)
            value, slope = gate(joined)
            dec_ref[:, at : at + 128] = value[FB : 2 * FB].astype(BF)
            grads.append(rows(XL + at, 128) * slope)
        grad = jnp.concatenate(grads, axis=1)
        own_grad.append(grad[FB : 2 * FB])
        all_grad.append(grad.astype(BF))
    back = dot(jnp.concatenate(all_grad, axis=0), wu_ref[...], ((1,), (1,))).astype(BF)
    for v in range(8):
        hid_ref[:, v * 128 : (v + 1) * 128] = back[v * ROWS : (v + 1) * ROWS]
    own_in = jnp.concatenate(own_in, axis=0).astype(BF)
    own_grad = jnp.concatenate(own_grad, axis=0).astype(BF)
    found = dot(own_in, own_grad, ((0,), (0,)))
    for n in range(4):
        gu_ref[n] = found[:, n * 128 : (n + 1) * 128]

    cin_ref[...] = to_coarse(hid_ref).astype(BF)
    row_c = lax.broadcasted_iota(jnp.int32, (8 * CR, 128), 0) % CR
    mine = (row_c >= CB) & (row_c < 2 * CB)
    for row, lane, (o, v) in voxels:
        grad = cin_ref[o * CR : (o + 1) * CR, v * 128 : (v + 1) * 128].astype(F32)
        grad = grad * cslope_ref[row : row + CR, lane : lane + 128]
        cslope_ref[row : row + CR, lane : lane + 128] = grad
        cs_ref[o * CR : (o + 1) * CR, v * 128 : (v + 1) * 128] = grad.astype(BF)
    for x in range(4):
        for r in range(2):
            kept = cslope_ref[x * 128 : (x + 1) * 128, r * 128 : (r + 1) * 128]
            kept = jnp.transpose(jnp.where(mine, kept, 0.0)).astype(BF)
            cst_ref[:, r * 512 + x * 128 : r * 512 + (x + 1) * 128] = kept
    for ab in range(9):
        a, b = ab // 3, ab % 3
        taps = []
        for e in range(3):
            parts = [
                cp_ref[a : a + 4, b : b + 4, (e + r) // 2 : (e + r) // 2 + 2, (e + r) % 2]
                for r in range(2)
            ]
            parts = [part.reshape(32 * CR, 128) for part in parts]
            taps.append(jnp.concatenate(parts, axis=0))
        found = dot(cst_ref[...], jnp.concatenate(taps, axis=1))
        for e in range(3):
            at = (3 * ab + e) * 128
            gc_ref[at : at + 128, :] = jnp.transpose(found[:, e * 128 : (e + 1) * 128])

    fill(cs_ref, sp_ref)
    scatter_flat(cin_ref, convolve(sp_ref, wt_ref).astype(BF))

    hidden_grad = dot(up_f[FB : 2 * FB].astype(BF), cin_ref[...])
    pieces = []
    for pq in range(4):
        slope = hidden_grad[:, pq * 256 : (pq + 1) * 256] * slope_down[pq]
        pieces += [slope, zeros8((8, 256))]
    down = jnp.transpose(jnp.concatenate(pieces, axis=0)).astype(BF)
    for ab in range(9):
        a, b = ab // 3, ab % 3
        taps = [mine_ref[(2 * p + a) * 5 + 2 * q + b] for p in range(2) for q in range(2)]
        taps = jnp.concatenate(taps, axis=0)
        low = dot(down[0:128], jnp.concatenate([taps[:, 0:128], taps[:, 256:384]], axis=1))
        high = dot(down[128:256], taps[:, 0:256])
        later = low[:, 0:128] + high[:, 128:256]
        first = low[:, 128:256] + high[:, 0:128]
        gd_ref[(3 * ab) * 64 : (3 * ab + 1) * 64, :] = jnp.transpose(first)[64:128]
        gd_ref[(3 * ab + 1) * 64 : (3 * ab + 3) * 64, :] = jnp.transpose(later)

    for t in range(TILES):
        if t < 27:
            tile = gd_ref[pl.ds(t, 64, stride=27), :]
        elif t < 81:
            tile = gc_ref[pl.ds(t - 27, 64, stride=54), :]
        elif t < 89:
            tile = gu_ref[(t - 81) % 4, pl.ds((t - 81) // 4, 64, stride=2), :]
        else:
            tile = jnp.zeros((64, 128), F32)
        n = t % 12
        sum_ref[t // 12 % 2, t // 24, :, n * 128 : (n + 1) * 128] = tile.astype(BF)


def local_pass(own, prev, nxt, far, wd, wc, wt, wu):
    vmem = pl.BlockSpec(memory_space=pltpu.VMEM)
    return pl.pallas_call(
        kernel,
        out_shape=(
            jax.ShapeDtypeStruct((FB, XL), BF),
            jax.ShapeDtypeStruct((2, 4, 64, 1536), BF),
        ),
        in_specs=[vmem] * 8,
        out_specs=(vmem, vmem),
        scratch_shapes=[
            pltpu.VMEM((4 * FB, UPPER), BF),
            pltpu.VMEM((25, ROWS, 384), BF),
            pltpu.VMEM((25, FB + 8, 384), BF),
            pltpu.VMEM((ROWS, 1024), BF),
            pltpu.VMEM((4, HALO, 128), BF),
            pltpu.VMEM((8 * CR, 1024), BF),
            pltpu.VMEM((6, 6, 3, 2, CR, 128), BF),
            pltpu.VMEM((32 * CR, 256), F32),
            pltpu.VMEM((8 * CR, 1024), BF),
            pltpu.VMEM((8 * CR, 1024), BF),
            pltpu.VMEM((6, 6, 3, 2, CR, 128), BF),
            pltpu.VMEM((128, 64 * CR), BF),
            pltpu.VMEM((1728, 128), F32),
            pltpu.VMEM((3456, 128), F32),
            pltpu.VMEM((4, 128, 128), F32),
        ],
        compiler_params=pltpu.CompilerParams(vmem_limit_bytes=32 * 2**20),
    )(own, nxt, prev, far, wd, wc, wt, wu)


def pack(place_ref, *refs):
    given, own_ref, far_ref, held, sems = refs[:5], refs[5], refs[6], refs[7:12], refs[12]
    copies = [
        pltpu.make_async_copy(source, target, sems.at[n])
        for n, (source, target) in enumerate(zip(given, held))
    ]
    for copy in copies:
        copy.start()
    for copy in copies:
        copy.wait()
    x_ref, cot_ref, fine_ref, parent_ref, coarse_ref = held
    place = place_ref[0]
    own_ref[:, 0:XL] = x_ref[...].reshape(FB, XL)
    own_ref[:, XL:IDX] = cot_ref[...].reshape(FB, XL)
    fine = jnp.concatenate([fine_ref[m] for m in range(7)], axis=0)
    fine = jnp.where(fine < 0, 0, fine - (FB * (place - 1) - 1)).astype(F32)
    coarse = jnp.concatenate([coarse_ref[c] for c in range(CB)], axis=0)
    coarse = jnp.where(coarse < 0, 0, coarse - (CB * (place - 1) - 1)).astype(F32)
    coarse = jnp.concatenate([coarse, jnp.zeros((FB - CB, 26), F32)], axis=0)
    parent = (parent_ref[...] - (8 * (CB * place - 1) - 1)).astype(F32)
    lists = jnp.concatenate([fine, parent], axis=0).astype(BF)
    unit = lax.broadcasted_iota(jnp.int32, (FB, FB), 0) == lax.broadcasted_iota(
        jnp.int32, (FB, FB), 1
    )
    lists = dot(jnp.where(unit, 1.0, 0.0).astype(BF), lists, ((1,), (1,)))
    filler = jnp.zeros((FB, 128 - 34), F32)
    own_ref[:, IDX : IDX + 128] = jnp.concatenate([lists, coarse, filler], axis=1).astype(BF)
    at = 0
    last = []
    for start, width in upper_pieces():
        if width > 128:
            far_ref[:, at : at + width] = own_ref[:, start : start + width]
        else:
            last.append(own_ref[:, start : start + width].astype(F32))
        at += width
    upper_half = lax.broadcasted_iota(jnp.int32, (FB, 128), 1) >= 64
    for n in range(5):
        first = swap_halves(last[2 * n])
        second = last[2 * n + 1] if 2 * n + 1 < 9 else first
        tile = jnp.where(upper_half, second, first)
        far_ref[:, 1792 + n * 128 : 1920 + n * 128] = tile.astype(BF)


def packed(place, features, cotangent, fine_nbr, parents, coarse_nbr):
    vmem = pl.BlockSpec(memory_space=pltpu.VMEM)
    return pl.pallas_call(
        pack,
        out_shape=(
            jax.ShapeDtypeStruct((FB, IDX + 128), BF),
            jax.ShapeDtypeStruct((FB, SENT), BF),
        ),
        in_specs=[pl.BlockSpec(memory_space=pltpu.SMEM)]
        + [pl.BlockSpec(memory_space=pltpu.HBM)] * 5,
        out_specs=(vmem, vmem),
        scratch_shapes=[
            pltpu.VMEM(array.shape, array.dtype)
            for array in (features, cotangent, fine_nbr, parents, coarse_nbr)
        ]
        + [pltpu.SemaphoreType.DMA((5,))],
    )(place, features, cotangent, fine_nbr, parents, coarse_nbr)


SPACE = ("x", "z")


def shift(block, distance):
    size = lax.axis_size(SPACE)
    route = [(i, i + distance) for i in range(size) if 0 <= i + distance < size]
    return lax.ppermute(block, SPACE, route)


def sum_copies(in_ref, out_ref):
    total = jnp.sum(in_ref[...].astype(F32), axis=0)
    for n in range(out_ref.shape[0]):
        out_ref[n] = total


def split(in_ref, down_ref, coarse_ref, up_ref):
    whole = jnp.concatenate([in_ref[n] for n in range(8)], axis=0)
    down_ref[...] = whole[0:27]
    coarse_ref[...] = whole[27:81]
    up_ref[...] = whole[81:89]


def spread_sum(sums):
    held = lax.all_to_all(sums, "core", 0, 0)
    held = jnp.sum(held.astype(F32), axis=0).astype(BF)
    held = held.reshape(16, 16, 1536)
    held = lax.all_to_all(held, ("y", "x"), 0, 0)
    held = jnp.sum(held.astype(F32), axis=0).astype(BF)
    held = held.reshape(16, 12, 128)
    held = lax.all_to_all(held, "z", 0, 0)
    held = pl.pallas_call(
        sum_copies,
        out_shape=jax.ShapeDtypeStruct((8, 12, 128), F32),
        compiler_params=pltpu.CompilerParams(vmem_limit_bytes=2 * 2**20),
    )(held)
    held = lax.all_to_all(held, ("y", "core"), 0, 0)
    shares = pl.pallas_call(
        split,
        out_shape=tuple(jax.ShapeDtypeStruct((n, 128), F32) for n in (27, 54, 8)),
        compiler_params=pltpu.CompilerParams(vmem_limit_bytes=2 * 2**20),
    )(held)
    return tuple(share.reshape(-1) for share in shares)


def gradients(
    fine_features,
    cotangent,
    down_weight,
    coarse_weight,
    up_weight,
    fine_neighbours,
    children,
    parent_slots,
    coarse_neighbours,
):
    place = lax.axis_index(SPACE).astype(jnp.int32).reshape(1)
    own, upper = packed(
        place,
        fine_features[0],
        cotangent[0],
        fine_neighbours.transpose(2, 0, 1),
        parent_slots,
        coarse_neighbours[0].reshape(CB, 1, 26),
    )
    prev = shift(own, 1)
    far = shift(upper, 2)
    nxt = shift(own, -1)
    wide = widened(down_weight, coarse_weight)
    return local_pass(own, prev, nxt, far, *wide, up_weight)


def body(fine_features, *rest):
    decoded, sums = gradients(fine_features, *rest)
    return (decoded.reshape(fine_features.shape), *spread_sum(sums))


def solution(mesh):
    mesh = jax.sharding.Mesh(mesh.devices.reshape(4, 2, 4, 16), ("y", "core", "x", "z"))
    dp = ("y", "core")
    in_specs = (
        P(dp, SPACE, None, None, None),
        P(dp, SPACE, None, None, None),
        P(),
        P(),
        P(),
        P(dp, SPACE, None),
        P(dp, SPACE, None),
        P(dp, SPACE),
        P(dp, SPACE, None),
    )
    out_specs = (P(dp, SPACE, None, None, None), P(SPACE), P(SPACE), P(SPACE))
    return jax.shard_map(body, mesh=mesh, in_specs=in_specs, out_specs=out_specs, check_vma=False)
```

```python
import functools

import jax
import jax.numpy as jnp
from jax import lax
from jax.experimental import pallas as pl
from jax.experimental.pallas import tpu as pltpu
from jax.sharding import PartitionSpec as P

BF = jnp.bfloat16
F32 = jnp.float32
FB = 24
CB = 6
ROWS = 80
CR = 16
XL = 4096
EARLY = 7 * 256
IDX = XL + EARLY
VMEM_A, VMEM_B = 20 * 2**20, 24 * 2**20
TILES = 96


def plane_lanes(i, j):
    if i == 3:
        return (j * 256, 256)
    if j == 3:
        return (1024 + i * 256, 256)
    return (1792 + (i * 3 + j) * 128, 128)


def upper_pieces():
    pieces = [(3 * 1024, 1024)]
    pieces += [((i * 4 + 3) * 256, 256) for i in range(3)]
    pieces += [((i * 4 + j) * 256 + 128, 128) for i in range(3) for j in range(3)]
    return pieces


UPPER = sum(width for _, width in upper_pieces())
SENT = 1792 + 5 * 128


def dot(a, b, dims=((1,), (0,))):
    return lax.dot_general(a, b, (dims, ((), ())), preferred_element_type=F32)


def gate(v):
    s = 1.0 / (1.0 + jnp.exp(-v))
    return v * s, s * (1.0 + v * (1.0 - s))


def axis_sides(half):
    inner = [(0, 0, half + 1), (0, 1, half + 3)]
    return inner + ([(-1, 1, 0)] if half else [(1, 0, 5)])


def halo_blocks(p, q):
    blocks = []
    for sx, ox, cx in axis_sides(p):
        for sy, oy, cy in axis_sides(q):
            for sz, oz, cells in (
                (0, 0, [(0, 1), (1, 2)]),
                (0, 1, [(0, 3), (1, 4)]),
                (-1, 1, [(1, 0)]),
                (1, 0, [(0, 5)]),
            ):
                code = 9 * (sx + 1) + 3 * (sy + 1) + sz + 1
                if code != 13:
                    targets = [(r, (cx, cy, cz)) for r, cz in cells]
                    blocks.append((code - (code > 13), 4 * ox + 2 * oy + oz, targets))
    return blocks


HALO = len(halo_blocks(0, 0)) * CR


def swap_halves(tile):
    return jnp.concatenate([tile[:, 64:128], tile[:, 0:64]], axis=1)


def octant_of(x, y, z):
    return 4 * (x // 2) + 2 * (y // 2) + z // 2, 4 * (x % 2) + 2 * (y % 2) + z % 2


def widen(wd_ref, wc_ref, x_ref, cot_ref, down_ref, coarse_ref, turned_ref, own_ref, cots_ref):
    own_ref[...] = x_ref[...]
    cots_ref[...] = cot_ref[...]
    down_ref[...] = jnp.zeros(down_ref.shape, BF)
    for ab in range(9):
        tap = [wd_ref[(3 * ab + e) * 64 : (3 * ab + e + 1) * 64, :] for e in range(3)]
        at = ab * 384
        for row, e in ((0, 1), (64, 2), (320, 0)):
            down_ref[at + row : at + row + 64, 0:128] = tap[e]
        for row, e in ((64, 0), (128, 1), (192, 2)):
            down_ref[at + row : at + row + 64, 128:256] = tap[e]
    zero = jnp.zeros((128, 128), BF)
    for ab in range(9):
        for e in range(3):
            tap = 3 * ab + e
            plain = wc_ref[tap * 128 : (tap + 1) * 128, :]
            other = (26 - tap) * 128
            turned = jnp.transpose(wc_ref[other : other + 128, :].astype(F32)).astype(BF)
            for ref, block in ((coarse_ref, plain), (turned_ref, turned)):
                for r in range(2):
                    row = ab * 512 + (e + r) * 128
                    ref[row : row + 128, r * 128 : (r + 1) * 128] = block
        for ref in (coarse_ref, turned_ref):
            ref[ab * 512 + 384 : ab * 512 + 512, 0:128] = zero
            ref[ab * 512 : ab * 512 + 128, 128:256] = zero


def widened(down_weight, coarse_weight, own, cot):
    vmem = pl.BlockSpec(memory_space=pltpu.VMEM)
    shapes = ((9 * 384, 256), (9 * 512, 256), (9 * 512, 256), own.shape, cot.shape)
    return pl.pallas_call(
        widen,
        out_shape=tuple(jax.ShapeDtypeStruct(shape, BF) for shape in shapes),
        in_specs=[vmem] * 4,
        out_specs=(vmem,) * 5,
        compiler_params=pltpu.CompilerParams(vmem_limit_bytes=12 * 2**20),
    )(down_weight, coarse_weight, own, cot)


def rows_of(refs, lane, width):
    parts = [ref[:, lane : lane + width].astype(F32) for ref in refs]
    return jnp.concatenate(parts + [jnp.zeros((ROWS - 3 * FB, width), F32)], axis=0)


def to_coarse(up, ref):
    return dot(up, ref[...], ((0,), (0,)))


def fill(nl_ref, flat_ref, padded_ref):
    for x in range(4):
        for y in range(4):
            for z in range(4):
                o, v = octant_of(x, y, z)
                padded_ref[x + 1, y + 1, (z + 1) // 2, (z + 1) % 2] = flat_ref[
                    o * CR : (o + 1) * CR, v * 128 : (v + 1) * 128
                ]
    for pq in range(4):
        got = dot(nl_ref[pq], flat_ref[:, pq * 256 : (pq + 1) * 256]).astype(BF)
        for n, (_, _, targets) in enumerate(halo_blocks(pq // 2, pq % 2)):
            for r, (cx, cy, cz) in targets:
                padded_ref[cx, cy, cz // 2, cz % 2] = got[
                    n * CR : (n + 1) * CR, r * 128 : (r + 1) * 128
                ]


def convolve(padded_ref, weight_ref):
    outs = []
    for x in range(0, 4, 1):
        taps = [
            padded_ref[x + a : x + a + 1, b : b + 4, zz // 2 : zz // 2 + 2, zz % 2].reshape(1 * 8 * CR, 128)
            for a in range(3)
            for b in range(3)
            for zz in range(4)
        ]
        outs.append(dot(jnp.concatenate(taps, axis=1), weight_ref[...]))
    return jnp.concatenate(outs, axis=0)


VOXELS = [
    (row * CR, r * 128, octant_of(row // 8, row // 2 % 4, row % 2 * 2 + r))
    for row in range(32)
    for r in range(2)
]


def scatter_flat(ref, value):
    for row, lane, (o, v) in VOXELS:
        piece = value[row : row + CR, lane : lane + 128]
        ref[o * CR : (o + 1) * CR, v * 128 : (v + 1) * 128] = piece


def forward(
    own_ref,
    prev_ref,
    next_ref,
    far_ref,
    wd_ref,
    wc_ref,
    mine_ref,
    up_ref,
    nl_ref,
    cp_ref,
    cslope_ref,
    cout_ref,
    dslope_ref,
    src_ref,
    pad_ref,
    hid_ref,
    cin_ref,
):
    zeros8 = functools.partial(jnp.zeros, dtype=F32)
    rows = functools.partial(rows_of, (prev_ref, own_ref, next_ref))

    idx = rows(IDX, 128)
    row = lax.broadcasted_iota(jnp.int32, (ROWS, 128), 0)
    lane = lax.broadcasted_iota(jnp.int32, (ROWS, 128), 1)
    block = jnp.where(row >= FB, 1.0, 0.0) + jnp.where(row >= 2 * FB, 1.0, 0.0)
    lane_f = lane.astype(F32)

    at = 0
    for n, (start, width) in enumerate(upper_pieces()):
        if width > 128:
            far = far_ref[:, at : at + width].astype(F32)
        else:
            tile = 1792 + (n - 4) // 2 * 128
            far = far_ref[:, tile : tile + 128].astype(F32)
            far = far if (n - 4) % 2 else swap_halves(far)
        parts = [far]
        parts += [r[:, start : start + width].astype(F32) for r in (prev_ref, own_ref, next_ref)]
        src_ref[:, at : at + width] = jnp.concatenate(parts, axis=0).astype(BF)
        at += width

    def pick(code):
        wanted = idx[:, code - 1 : code] + (24.0 * block[:, 0:1] - 1.0)
        wanted = jnp.where(idx[:, code - 1 : code] > 0.0, wanted, -1.0)
        hit = jnp.where(lane_f[:, 0 : 4 * FB] == wanted, 1.0, 0.0)
        return hit.astype(BF)

    picks = {code: pick(code) for code in range(1, 8)}

    def fetch(code, i, j, last):
        start, width = plane_lanes(i, j)
        if last:
            start, width = start + width - 128, 128
        return dot(picks[code], src_ref[:, start : start + width])

    def only_own(array):
        return jnp.concatenate([array[FB : 2 * FB], zeros8((8, array.shape[1]))], axis=0)

    for ip in range(5):
        for jp in range(5):
            i, j = (ip - 1) % 4, (jp - 1) % 4
            code = 4 * (ip == 0) + 2 * (jp == 0)
            if code:
                own = fetch(code, i, j, False)
            else:
                own = rows((i * 4 + j) * 256, 256)
            behind = fetch(code + 1, i, j, True)
            pad_ref[ip * 5 + jp, :, 0:256] = own.astype(BF)
            pad_ref[ip * 5 + jp, :, 256:384] = behind.astype(BF)
            mine_ref[ip * 5 + jp, :, 0:256] = only_own(own).astype(BF)
            mine_ref[ip * 5 + jp, :, 256:384] = only_own(behind).astype(BF)

    outs = []
    for p in range(2):
        for q in range(2):
            taps = [pad_ref[(2 * p + a) * 5 + 2 * q + b] for a in range(3) for b in range(3)]
            outs.append(dot(jnp.concatenate(taps, axis=1), wd_ref[...]))
    pre = jnp.concatenate(outs, axis=0)
    for pq in range(4):
        value, slope = gate(pre[pq * ROWS : (pq + 1) * ROWS])
        hid_ref[:, pq * 256 : (pq + 1) * 256] = value.astype(BF)
        dslope_ref[pq] = slope[FB : 2 * FB]

    code = idx[:, 7:8]
    slot = jnp.where(code > 0.0, code + (48.0 * block[:, 0:1] - 9.0), -1.0)
    column = (lane % CR * 8 + lane // CR).astype(F32)
    up_f = jnp.where(column == slot, 1.0, 0.0)
    up_ref[...] = up_f
    up = up_f.astype(BF)

    row16 = lax.broadcasted_iota(jnp.int32, (CR, ROWS), 0)
    lane80 = lax.broadcasted_iota(jnp.int32, (CR, ROWS), 1)
    device = jnp.where(row16 >= CB, 1, 0) + jnp.where(row16 >= 2 * CB, 1, 0)
    choose = jnp.where(lane80 == row16 + (FB - CB) * device, 1.0, 0.0).astype(BF)
    listed = dot(choose, idx.astype(BF))
    device = device[:, 0:1].astype(F32)
    place = listed + (6.0 * device - 7.0)
    place = jnp.where((listed > 0.0) & (place >= 0.0) & (place < CR), place, -1000.0)
    lane16 = lane_f[0:CR]
    for pq in range(4):
        blocks = []
        for m, octant, _ in halo_blocks(pq // 2, pq % 2):
            wanted = place[:, 8 + m : 9 + m] + float(CR * octant)
            blocks.append(jnp.where(lane16 == wanted, 1.0, 0.0))
        nl_ref[pq] = jnp.concatenate(blocks, axis=0).astype(BF)

    cin_ref[...] = to_coarse(up, hid_ref).astype(BF)
    fill(nl_ref, cin_ref, cp_ref)
    value, slope = gate(convolve(cp_ref, wc_ref))
    cslope_ref[...] = slope
    scatter_flat(cout_ref, value.astype(BF))


def backward(
    own_ref,
    prev_ref,
    next_ref,
    cot_own_ref,
    cot_prev_ref,
    cot_next_ref,
    wt_ref,
    wu_ref,
    mine_ref,
    up_ref,
    nl_ref,
    cp_ref,
    cslope_ref,
    cout_ref,
    dslope_ref,
    dec_ref,
    sum_ref,
    hid_ref,
    cin_ref,
    cs_ref,
    sp_ref,
    cst_ref,
    grad_ref,
    gd_ref,
    gc_ref,
    gu_ref,
):
    zeros8 = functools.partial(jnp.zeros, dtype=F32)
    rows = functools.partial(rows_of, (prev_ref, own_ref, next_ref))


    def cot_rows(lane, width):
        if lane < EARLY:
            return rows(XL + lane, width)
        return rows_of((cot_prev_ref, cot_own_ref, cot_next_ref), lane - EARLY, width)

    up_f = up_ref[...]
    up = up_f.astype(BF)

    up_in = dot(up, cout_ref[...])
    pieces = [up_in[:, v * 128 : (v + 1) * 128] for v in range(8)]
    own_in = [piece[FB : 2 * FB] for piece in pieces]
    out = dot(jnp.concatenate(pieces, axis=0).astype(BF), wu_ref[...])
    all_grad, own_grad = [], []
    for v in range(8):
        p, q, r = v // 4, v // 2 % 2, v % 2
        grads = []
        for ab in range(4):
            a, b = ab // 2, ab % 2
            at = ((2 * p + a) * 4 + 2 * q + b) * 256 + r * 128
            joined = out[v * ROWS : (v + 1) * ROWS, ab * 128 : (ab + 1) * 128] + rows(at, 128)
            value, slope = gate(joined)
            dec_ref[:, at : at + 128] = value[FB : 2 * FB].astype(BF)
            grads.append(cot_rows(at, 128) * slope)
        grad = jnp.concatenate(grads, axis=1)
        own_grad.append(grad[FB : 2 * FB])
        all_grad.append(grad.astype(BF))
    back = dot(jnp.concatenate(all_grad, axis=0), wu_ref[...], ((1,), (1,))).astype(BF)
    for v in range(8):
        hid_ref[:, v * 128 : (v + 1) * 128] = back[v * ROWS : (v + 1) * ROWS]
    own_in = jnp.concatenate(own_in, axis=0).astype(BF)
    own_grad = jnp.concatenate(own_grad, axis=0).astype(BF)
    found = dot(own_in, own_grad, ((0,), (0,)))
    for n in range(4):
        gu_ref[n] = found[:, n * 128 : (n + 1) * 128]

    cin_ref[...] = to_coarse(up, hid_ref).astype(BF)
    row_c = lax.broadcasted_iota(jnp.int32, (8 * CR, 128), 0) % CR
    mine = (row_c >= CB) & (row_c < 2 * CB)
    for row, lane, (o, v) in VOXELS:
        grad = cin_ref[o * CR : (o + 1) * CR, v * 128 : (v + 1) * 128].astype(F32)
        grad = grad * cslope_ref[row : row + CR, lane : lane + 128]
        grad_ref[row : row + CR, lane : lane + 128] = grad
        cs_ref[o * CR : (o + 1) * CR, v * 128 : (v + 1) * 128] = grad.astype(BF)
    for x in range(4):
        for r in range(2):
            kept = grad_ref[x * 128 : (x + 1) * 128, r * 128 : (r + 1) * 128]
            kept = jnp.transpose(jnp.where(mine, kept, 0.0)).astype(BF)
            cst_ref[:, r * 512 + x * 128 : r * 512 + (x + 1) * 128] = kept
    for ab in range(9):
        a, b = ab // 3, ab % 3
        taps = []
        for e in range(3):
            parts = [
                cp_ref[a : a + 4, b : b + 4, (e + r) // 2 : (e + r) // 2 + 2, (e + r) % 2]
                for r in range(2)
            ]
            parts = [part.reshape(32 * CR, 128) for part in parts]
            taps.append(jnp.concatenate(parts, axis=0))
        found = dot(cst_ref[...], jnp.concatenate(taps, axis=1))
        for e in range(3):
            at = (3 * ab + e) * 128
            gc_ref[at : at + 128, :] = jnp.transpose(found[:, e * 128 : (e + 1) * 128])

    fill(nl_ref, cs_ref, sp_ref)
    scatter_flat(cin_ref, convolve(sp_ref, wt_ref).astype(BF))

    hidden_grad = dot(up_f[FB : 2 * FB].astype(BF), cin_ref[...])
    pieces = []
    for pq in range(4):
        slope = hidden_grad[:, pq * 256 : (pq + 1) * 256] * dslope_ref[pq]
        pieces += [slope, zeros8((8, 256))]
    down = jnp.transpose(jnp.concatenate(pieces, axis=0)).astype(BF)
    for ab in range(9):
        a, b = ab // 3, ab % 3
        taps = [mine_ref[(2 * p + a) * 5 + 2 * q + b] for p in range(2) for q in range(2)]
        taps = jnp.concatenate(taps, axis=0)
        low = dot(down[0:128], jnp.concatenate([taps[:, 0:128], taps[:, 256:384]], axis=1))
        high = dot(down[128:256], taps[:, 0:256])
        later = low[:, 0:128] + high[:, 128:256]
        first = low[:, 128:256] + high[:, 0:128]
        gd_ref[(3 * ab) * 64 : (3 * ab + 1) * 64, :] = jnp.transpose(first)[64:128]
        gd_ref[(3 * ab + 1) * 64 : (3 * ab + 3) * 64, :] = jnp.transpose(later)

    for t in range(TILES):
        if t < 27:
            tile = gd_ref[pl.ds(t, 64, stride=27), :]
        elif t < 81:
            tile = gc_ref[pl.ds(t - 27, 64, stride=54), :]
        elif t < 89:
            tile = gu_ref[(t - 81) % 4, pl.ds((t - 81) // 4, 64, stride=2), :]
        else:
            tile = jnp.zeros((64, 128), F32)
        n = t % 12
        sum_ref[t // 12 % 2, t // 24, :, n * 128 : (n + 1) * 128] = tile.astype(BF)


def forward_pass(own, prev, nxt, far, wd, wc):
    vmem = pl.BlockSpec(memory_space=pltpu.VMEM)
    made = (
        ((25, FB + 8, 384), BF),
        ((ROWS, 128), F32),
        ((4, HALO, 128), BF),
        ((6, 6, 3, 2, CR, 128), BF),
        ((32 * CR, 256), F32),
        ((8 * CR, 1024), BF),
        ((4, FB, 256), F32),
    )
    return pl.pallas_call(
        forward,
        out_shape=tuple(jax.ShapeDtypeStruct(*one) for one in made),
        in_specs=[vmem] * 6,
        out_specs=(vmem,) * len(made),
        scratch_shapes=[
            pltpu.VMEM((4 * FB, UPPER), BF),
            pltpu.VMEM((25, ROWS, 384), BF),
            pltpu.VMEM((ROWS, 1024), BF),
            pltpu.VMEM((8 * CR, 1024), BF),
        ],
        compiler_params=pltpu.CompilerParams(vmem_limit_bytes=VMEM_A),
    )(own, prev, nxt, far, wd, wc)


def backward_pass(*given):
    vmem = pl.BlockSpec(memory_space=pltpu.VMEM)
    return pl.pallas_call(
        backward,
        out_shape=(
            jax.ShapeDtypeStruct((FB, XL), BF),
            jax.ShapeDtypeStruct((2, 4, 64, 1536), BF),
        ),
        in_specs=[vmem] * len(given),
        out_specs=(vmem, vmem),
        scratch_shapes=[
            pltpu.VMEM((ROWS, 1024), BF),
            pltpu.VMEM((8 * CR, 1024), BF),
            pltpu.VMEM((8 * CR, 1024), BF),
            pltpu.VMEM((6, 6, 3, 2, CR, 128), BF),
            pltpu.VMEM((128, 64 * CR), BF),
            pltpu.VMEM((32 * CR, 256), F32),
            pltpu.VMEM((1728, 128), F32),
            pltpu.VMEM((3456, 128), F32),
            pltpu.VMEM((4, 128, 128), F32),
        ],
        compiler_params=pltpu.CompilerParams(vmem_limit_bytes=VMEM_B),
    )(*given)


def pack(place_ref, *refs):
    given, held, sems = refs[:5], refs[8:13], refs[13]
    own_ref, cots_ref, far_ref = refs[5:8]
    copies = [
        pltpu.make_async_copy(source, target, sems.at[n])
        for n, (source, target) in enumerate(zip(given, held))
    ]
    for copy in copies:
        copy.start()
    for copy in copies:
        copy.wait()
    x_ref, cot_ref, fine_ref, parent_ref, coarse_ref = held
    place = place_ref[0]
    own_ref[:, 0:XL] = x_ref[...].reshape(FB, XL)
    cot = cot_ref[...].reshape(FB, XL)
    own_ref[:, XL:IDX] = cot[:, 0:EARLY]
    cots_ref[...] = cot[:, EARLY:XL]
    fine = jnp.concatenate([fine_ref[m] for m in range(7)], axis=0)
    fine = jnp.where(fine < 0, 0, fine - (FB * (place - 1) - 1)).astype(F32)
    coarse = jnp.concatenate([coarse_ref[c] for c in range(CB)], axis=0)
    coarse = jnp.where(coarse < 0, 0, coarse - (CB * (place - 1) - 1)).astype(F32)
    coarse = jnp.concatenate([coarse, jnp.zeros((FB - CB, 26), F32)], axis=0)
    parent = (parent_ref[...] - (8 * (CB * place - 1) - 1)).astype(F32)
    lists = jnp.concatenate([fine, parent], axis=0).astype(BF)
    unit = lax.broadcasted_iota(jnp.int32, (FB, FB), 0) == lax.broadcasted_iota(
        jnp.int32, (FB, FB), 1
    )
    lists = dot(jnp.where(unit, 1.0, 0.0).astype(BF), lists, ((1,), (1,)))
    filler = jnp.zeros((FB, 128 - 34), F32)
    own_ref[:, IDX : IDX + 128] = jnp.concatenate([lists, coarse, filler], axis=1).astype(BF)
    at = 0
    last = []
    for start, width in upper_pieces():
        if width > 128:
            far_ref[:, at : at + width] = own_ref[:, start : start + width]
        else:
            last.append(own_ref[:, start : start + width].astype(F32))
        at += width
    upper_half = lax.broadcasted_iota(jnp.int32, (FB, 128), 1) >= 64
    for n in range(5):
        first = swap_halves(last[2 * n])
        second = last[2 * n + 1] if 2 * n + 1 < 9 else first
        tile = jnp.where(upper_half, second, first)
        far_ref[:, 1792 + n * 128 : 1920 + n * 128] = tile.astype(BF)


def packed(place, features, cotangent, fine_nbr, parents, coarse_nbr):
    vmem = pl.BlockSpec(memory_space=pltpu.VMEM)
    return pl.pallas_call(
        pack,
        out_shape=(
            jax.ShapeDtypeStruct((FB, IDX + 128), BF),
            jax.ShapeDtypeStruct((FB, XL - EARLY), BF),
            jax.ShapeDtypeStruct((FB, SENT), BF),
        ),
        in_specs=[pl.BlockSpec(memory_space=pltpu.SMEM)]
        + [pl.BlockSpec(memory_space=pltpu.HBM)] * 5,
        out_specs=(vmem,) * 3,
        scratch_shapes=[
            pltpu.VMEM(array.shape, array.dtype)
            for array in (features, cotangent, fine_nbr, parents, coarse_nbr)
        ]
        + [pltpu.SemaphoreType.DMA((5,))],
    )(place, features, cotangent, fine_nbr, parents, coarse_nbr)


SPACE = ("x", "z")


def shift(block, distance):
    size = lax.axis_size(SPACE)
    route = [(i, i + distance) for i in range(size) if 0 <= i + distance < size]
    return lax.ppermute(block, SPACE, route)


def sum_copies(in_ref, out_ref):
    total = jnp.sum(in_ref[...].astype(F32), axis=0)
    for n in range(out_ref.shape[0]):
        out_ref[n] = total


def split(in_ref, down_ref, coarse_ref, up_ref):
    whole = jnp.concatenate([in_ref[n] for n in range(8)], axis=0)
    down_ref[...] = whole[0:27]
    coarse_ref[...] = whole[27:81]
    up_ref[...] = whole[81:89]


def spread_sum(sums):
    held = lax.all_to_all(sums, "core", 0, 0)
    held = jnp.sum(held.astype(F32), axis=0).astype(BF)
    held = held.reshape(16, 16, 1536)
    held = lax.all_to_all(held, ("y", "x"), 0, 0)
    held = jnp.sum(held.astype(F32), axis=0).astype(BF)
    held = held.reshape(16, 12, 128)
    held = lax.all_to_all(held, "z", 0, 0)
    held = pl.pallas_call(
        sum_copies,
        out_shape=jax.ShapeDtypeStruct((8, 12, 128), F32),
        compiler_params=pltpu.CompilerParams(vmem_limit_bytes=2 * 2**20),
    )(held)
    held = lax.all_to_all(held, ("y", "core"), 0, 0)
    shares = pl.pallas_call(
        split,
        out_shape=tuple(jax.ShapeDtypeStruct((n, 128), F32) for n in (27, 54, 8)),
        compiler_params=pltpu.CompilerParams(vmem_limit_bytes=2 * 2**20),
    )(held)
    return tuple(share.reshape(-1) for share in shares)


def gradients(
    fine_features,
    cotangent,
    down_weight,
    coarse_weight,
    up_weight,
    fine_neighbours,
    children,
    parent_slots,
    coarse_neighbours,
):
    place = lax.axis_index(SPACE).astype(jnp.int32).reshape(1)
    own, cot, upper = packed(
        place,
        fine_features[0],
        cotangent[0],
        fine_neighbours.transpose(2, 0, 1),
        parent_slots,
        coarse_neighbours[0].reshape(CB, 1, 26),
    )
    prev = shift(own, 1)
    far = shift(upper, 2)
    nxt = shift(own, -1)
    cot_prev = shift(cot, 1)
    cot_next = shift(cot, -1)
    wide_down, wide, turned, own, cot = widened(down_weight, coarse_weight, own, cot)
    kept = forward_pass(own, prev, nxt, far, wide_down, wide)
    return backward_pass(own, prev, nxt, cot, cot_prev, cot_next, turned, up_weight, *kept)


def body(fine_features, *rest):
    decoded, sums = gradients(fine_features, *rest)
    return (decoded.reshape(fine_features.shape), *spread_sum(sums))


def solution(mesh):
    mesh = jax.sharding.Mesh(mesh.devices.reshape(4, 2, 4, 16), ("y", "core", "x", "z"))
    dp = ("y", "core")
    in_specs = (
        P(dp, SPACE, None, None, None),
        P(dp, SPACE, None, None, None),
        P(),
        P(),
        P(),
        P(dp, SPACE, None),
        P(dp, SPACE, None),
        P(dp, SPACE),
        P(dp, SPACE, None),
    )
    out_specs = (P(dp, SPACE, None, None, None), P(SPACE), P(SPACE), P(SPACE))
    return jax.shard_map(body, mesh=mesh, in_specs=in_specs, out_specs=out_specs, check_vma=False)
```

```python
import functools

import jax
import jax.numpy as jnp
from jax import lax
from jax.experimental import pallas as pl
from jax.experimental.pallas import tpu as pltpu
from jax.sharding import PartitionSpec as P

BF = jnp.bfloat16
F32 = jnp.float32
FB = 24
CB = 6
ROWS = 80
CR = 16
XL = 4096
EARLY = 7 * 256
IDX = XL + EARLY
VMEM_A, VMEM_B = 20 * 2**20, 24 * 2**20
TILES = 96


def plane_lanes(i, j):
    if i == 3:
        return (j * 256, 256)
    if j == 3:
        return (1024 + i * 256, 256)
    return (1792 + (i * 3 + j) * 128, 128)


def upper_pieces():
    pieces = [(3 * 1024, 1024)]
    pieces += [((i * 4 + 3) * 256, 256) for i in range(3)]
    pieces += [((i * 4 + j) * 256 + 128, 128) for i in range(3) for j in range(3)]
    return pieces


UPPER = sum(width for _, width in upper_pieces())
SENT = 1792 + 5 * 128


def dot(a, b, dims=((1,), (0,))):
    return lax.dot_general(a, b, (dims, ((), ())), preferred_element_type=F32)


def gate(v):
    s = 1.0 / (1.0 + jnp.exp(-v))
    return v * s, s * (1.0 + v * (1.0 - s))


def axis_sides(half):
    inner = [(0, 0, half + 1), (0, 1, half + 3)]
    return inner + ([(-1, 1, 0)] if half else [(1, 0, 5)])


def halo_blocks(p, q):
    blocks = []
    for sx, ox, cx in axis_sides(p):
        for sy, oy, cy in axis_sides(q):
            for sz, oz, cells in (
                (0, 0, [(0, 1), (1, 2)]),
                (0, 1, [(0, 3), (1, 4)]),
                (-1, 1, [(1, 0)]),
                (1, 0, [(0, 5)]),
            ):
                code = 9 * (sx + 1) + 3 * (sy + 1) + sz + 1
                if code != 13:
                    targets = [(r, (cx, cy, cz)) for r, cz in cells]
                    blocks.append((code - (code > 13), 4 * ox + 2 * oy + oz, targets))
    return blocks


HALO = len(halo_blocks(0, 0)) * CR


def swap_halves(tile):
    return jnp.concatenate([tile[:, 64:128], tile[:, 0:64]], axis=1)


def octant_of(x, y, z):
    return 4 * (x // 2) + 2 * (y // 2) + z // 2, 4 * (x % 2) + 2 * (y % 2) + z % 2


def in_hbm(*arrays):
    return [pltpu.with_memory_space_constraint(array, pltpu.HBM) for array in arrays]


def widen(wd_hbm, wc_hbm, down_ref, coarse_ref, turned_ref, wd_ref, wc_ref, sems):
    first = pltpu.make_async_copy(wd_hbm, wd_ref, sems.at[0])
    second = pltpu.make_async_copy(wc_hbm, wc_ref, sems.at[1])
    first.start()
    second.start()
    down_ref[...] = jnp.zeros(down_ref.shape, BF)
    first.wait()
    for ab in range(9):
        tap = [wd_ref[(3 * ab + e) * 64 : (3 * ab + e + 1) * 64, :] for e in range(3)]
        at = ab * 384
        for row, e in ((0, 1), (64, 2), (320, 0)):
            down_ref[at + row : at + row + 64, 0:128] = tap[e]
        for row, e in ((64, 0), (128, 1), (192, 2)):
            down_ref[at + row : at + row + 64, 128:256] = tap[e]
    second.wait()
    zero = jnp.zeros((128, 128), BF)
    for ab in range(9):
        for e in range(3):
            tap = 3 * ab + e
            plain = wc_ref[tap * 128 : (tap + 1) * 128, :]
            other = (26 - tap) * 128
            turned = jnp.transpose(wc_ref[other : other + 128, :].astype(F32)).astype(BF)
            for ref, block in ((coarse_ref, plain), (turned_ref, turned)):
                for r in range(2):
                    row = ab * 512 + (e + r) * 128
                    ref[row : row + 128, r * 128 : (r + 1) * 128] = block
        for ref in (coarse_ref, turned_ref):
            ref[ab * 512 + 384 : ab * 512 + 512, 0:128] = zero
            ref[ab * 512 : ab * 512 + 128, 128:256] = zero


def widened(down_weight, coarse_weight):
    vmem = pl.BlockSpec(memory_space=pltpu.VMEM)
    shapes = ((9 * 384, 256), (9 * 512, 256), (9 * 512, 256))
    return pl.pallas_call(
        widen,
        out_shape=tuple(jax.ShapeDtypeStruct(shape, BF) for shape in shapes),
        in_specs=[pl.BlockSpec(memory_space=pltpu.HBM)] * 2,
        out_specs=(vmem,) * 3,
        scratch_shapes=[
            pltpu.VMEM(down_weight.shape, BF),
            pltpu.VMEM(coarse_weight.shape, BF),
            pltpu.SemaphoreType.DMA((2,)),
        ],
        compiler_params=pltpu.CompilerParams(vmem_limit_bytes=12 * 2**20),
    )(*in_hbm(down_weight, coarse_weight))


def rows_of(refs, lane, width):
    parts = [ref[:, lane : lane + width].astype(F32) for ref in refs]
    return jnp.concatenate(parts + [jnp.zeros((ROWS - 3 * FB, width), F32)], axis=0)


def to_coarse(up, ref):
    return dot(up, ref[...], ((0,), (0,)))


def fill(nl_ref, flat_ref, padded_ref):
    for x in range(4):
        for y in range(4):
            for z in range(4):
                o, v = octant_of(x, y, z)
                padded_ref[x + 1, y + 1, (z + 1) // 2, (z + 1) % 2] = flat_ref[
                    o * CR : (o + 1) * CR, v * 128 : (v + 1) * 128
                ]
    for pq in range(4):
        got = dot(nl_ref[pq], flat_ref[:, pq * 256 : (pq + 1) * 256]).astype(BF)
        for n, (_, _, targets) in enumerate(halo_blocks(pq // 2, pq % 2)):
            for r, (cx, cy, cz) in targets:
                padded_ref[cx, cy, cz // 2, cz % 2] = got[
                    n * CR : (n + 1) * CR, r * 128 : (r + 1) * 128
                ]


def convolve(padded_ref, weight_ref):
    outs = []
    for x in range(0, 4, 1):
        taps = [
            padded_ref[x + a : x + a + 1, b : b + 4, zz // 2 : zz // 2 + 2, zz % 2].reshape(1 * 8 * CR, 128)
            for a in range(3)
            for b in range(3)
            for zz in range(4)
        ]
        outs.append(dot(jnp.concatenate(taps, axis=1), weight_ref[...]))
    return jnp.concatenate(outs, axis=0)


VOXELS = [
    (row * CR, r * 128, octant_of(row // 8, row // 2 % 4, row % 2 * 2 + r))
    for row in range(32)
    for r in range(2)
]


def scatter_flat(ref, value):
    for row, lane, (o, v) in VOXELS:
        piece = value[row : row + CR, lane : lane + 128]
        ref[o * CR : (o + 1) * CR, v * 128 : (v + 1) * 128] = piece


def forward(
    own_ref,
    prev_ref,
    next_ref,
    far_ref,
    wd_ref,
    wc_ref,
    mine_ref,
    up_ref,
    nl_ref,
    cp_ref,
    cslope_ref,
    cout_ref,
    dslope_ref,
    src_ref,
    pad_ref,
    hid_ref,
    cin_ref,
):
    zeros8 = functools.partial(jnp.zeros, dtype=F32)
    rows = functools.partial(rows_of, (prev_ref, own_ref, next_ref))

    idx = rows(IDX, 128)
    row = lax.broadcasted_iota(jnp.int32, (ROWS, 128), 0)
    lane = lax.broadcasted_iota(jnp.int32, (ROWS, 128), 1)
    block = jnp.where(row >= FB, 1.0, 0.0) + jnp.where(row >= 2 * FB, 1.0, 0.0)
    lane_f = lane.astype(F32)

    at = 0
    for n, (start, width) in enumerate(upper_pieces()):
        if width > 128:
            far = far_ref[:, at : at + width].astype(F32)
        else:
            tile = 1792 + (n - 4) // 2 * 128
            far = far_ref[:, tile : tile + 128].astype(F32)
            far = far if (n - 4) % 2 else swap_halves(far)
        parts = [far]
        parts += [r[:, start : start + width].astype(F32) for r in (prev_ref, own_ref, next_ref)]
        src_ref[:, at : at + width] = jnp.concatenate(parts, axis=0).astype(BF)
        at += width

    def pick(code):
        wanted = idx[:, code - 1 : code] + (24.0 * block[:, 0:1] - 1.0)
        wanted = jnp.where(idx[:, code - 1 : code] > 0.0, wanted, -1.0)
        hit = jnp.where(lane_f[:, 0 : 4 * FB] == wanted, 1.0, 0.0)
        return hit.astype(BF)

    picks = {code: pick(code) for code in range(1, 8)}

    def fetch(code, i, j, last):
        start, width = plane_lanes(i, j)
        if last:
            start, width = start + width - 128, 128
        return dot(picks[code], src_ref[:, start : start + width])

    def only_own(array):
        return jnp.concatenate([array[FB : 2 * FB], zeros8((8, array.shape[1]))], axis=0)

    for ip in range(5):
        for jp in range(5):
            i, j = (ip - 1) % 4, (jp - 1) % 4
            code = 4 * (ip == 0) + 2 * (jp == 0)
            if code:
                own = fetch(code, i, j, False)
            else:
                own = rows((i * 4 + j) * 256, 256)
            behind = fetch(code + 1, i, j, True)
            pad_ref[ip * 5 + jp, :, 0:256] = own.astype(BF)
            pad_ref[ip * 5 + jp, :, 256:384] = behind.astype(BF)
            mine_ref[ip * 5 + jp, :, 0:256] = only_own(own).astype(BF)
            mine_ref[ip * 5 + jp, :, 256:384] = only_own(behind).astype(BF)

    outs = []
    for p in range(2):
        for q in range(2):
            taps = [pad_ref[(2 * p + a) * 5 + 2 * q + b] for a in range(3) for b in range(3)]
            outs.append(dot(jnp.concatenate(taps, axis=1), wd_ref[...]))
    pre = jnp.concatenate(outs, axis=0)
    for pq in range(4):
        value, slope = gate(pre[pq * ROWS : (pq + 1) * ROWS])
        hid_ref[:, pq * 256 : (pq + 1) * 256] = value.astype(BF)
        dslope_ref[pq] = slope[FB : 2 * FB]

    code = idx[:, 7:8]
    slot = jnp.where(code > 0.0, code + (48.0 * block[:, 0:1] - 9.0), -1.0)
    column = (lane % CR * 8 + lane // CR).astype(F32)
    up_f = jnp.where(column == slot, 1.0, 0.0)
    up_ref[...] = up_f
    up = up_f.astype(BF)

    row16 = lax.broadcasted_iota(jnp.int32, (CR, ROWS), 0)
    lane80 = lax.broadcasted_iota(jnp.int32, (CR, ROWS), 1)
    device = jnp.where(row16 >= CB, 1, 0) + jnp.where(row16 >= 2 * CB, 1, 0)
    choose = jnp.where(lane80 == row16 + (FB - CB) * device, 1.0, 0.0).astype(BF)
    listed = dot(choose, idx.astype(BF))
    device = device[:, 0:1].astype(F32)
    place = listed + (6.0 * device - 7.0)
    place = jnp.where((listed > 0.0) & (place >= 0.0) & (place < CR), place, -1000.0)
    lane16 = lane_f[0:CR]
    for pq in range(4):
        blocks = []
        for m, octant, _ in halo_blocks(pq // 2, pq % 2):
            wanted = place[:, 8 + m : 9 + m] + float(CR * octant)
            blocks.append(jnp.where(lane16 == wanted, 1.0, 0.0))
        nl_ref[pq] = jnp.concatenate(blocks, axis=0).astype(BF)

    cin_ref[...] = to_coarse(up, hid_ref).astype(BF)
    fill(nl_ref, cin_ref, cp_ref)
    value, slope = gate(convolve(cp_ref, wc_ref))
    cslope_ref[...] = slope
    scatter_flat(cout_ref, value.astype(BF))


def backward(
    own_ref,
    prev_ref,
    next_ref,
    cot_own_ref,
    cot_prev_ref,
    cot_next_ref,
    wt_ref,
    wu_ref,
    mine_ref,
    up_ref,
    nl_ref,
    cp_ref,
    cslope_ref,
    cout_ref,
    dslope_ref,
    dec_ref,
    sum_ref,
    hid_ref,
    cin_ref,
    cs_ref,
    sp_ref,
    cst_ref,
    grad_ref,
    gd_ref,
    gc_ref,
    gu_ref,
):
    zeros8 = functools.partial(jnp.zeros, dtype=F32)
    rows = functools.partial(rows_of, (prev_ref, own_ref, next_ref))


    def cot_rows(lane, width):
        if lane < EARLY:
            return rows(XL + lane, width)
        return rows_of((cot_prev_ref, cot_own_ref, cot_next_ref), lane - EARLY, width)

    up_f = up_ref[...]
    up = up_f.astype(BF)

    up_in = dot(up, cout_ref[...])
    pieces = [up_in[:, v * 128 : (v + 1) * 128] for v in range(8)]
    own_in = [piece[FB : 2 * FB] for piece in pieces]
    out = dot(jnp.concatenate(pieces, axis=0).astype(BF), wu_ref[...])
    all_grad, own_grad = [], []
    for v in range(8):
        p, q, r = v // 4, v // 2 % 2, v % 2
        grads = []
        for ab in range(4):
            a, b = ab // 2, ab % 2
            at = ((2 * p + a) * 4 + 2 * q + b) * 256 + r * 128
            joined = out[v * ROWS : (v + 1) * ROWS, ab * 128 : (ab + 1) * 128] + rows(at, 128)
            value, slope = gate(joined)
            dec_ref[:, at : at + 128] = value[FB : 2 * FB].astype(BF)
            grads.append(cot_rows(at, 128) * slope)
        grad = jnp.concatenate(grads, axis=1)
        own_grad.append(grad[FB : 2 * FB])
        all_grad.append(grad.astype(BF))
    back = dot(jnp.concatenate(all_grad, axis=0), wu_ref[...], ((1,), (1,))).astype(BF)
    for v in range(8):
        hid_ref[:, v * 128 : (v + 1) * 128] = back[v * ROWS : (v + 1) * ROWS]
    own_in = jnp.concatenate(own_in, axis=0).astype(BF)
    own_grad = jnp.concatenate(own_grad, axis=0).astype(BF)
    found = dot(own_in, own_grad, ((0,), (0,)))
    for n in range(4):
        gu_ref[n] = found[:, n * 128 : (n + 1) * 128]

    cin_ref[...] = to_coarse(up, hid_ref).astype(BF)
    row_c = lax.broadcasted_iota(jnp.int32, (8 * CR, 128), 0) % CR
    mine = (row_c >= CB) & (row_c < 2 * CB)
    for row, lane, (o, v) in VOXELS:
        grad = cin_ref[o * CR : (o + 1) * CR, v * 128 : (v + 1) * 128].astype(F32)
        grad = grad * cslope_ref[row : row + CR, lane : lane + 128]
        grad_ref[row : row + CR, lane : lane + 128] = grad
        cs_ref[o * CR : (o + 1) * CR, v * 128 : (v + 1) * 128] = grad.astype(BF)
    for x in range(4):
        for r in range(2):
            kept = grad_ref[x * 128 : (x + 1) * 128, r * 128 : (r + 1) * 128]
            kept = jnp.transpose(jnp.where(mine, kept, 0.0)).astype(BF)
            cst_ref[:, r * 512 + x * 128 : r * 512 + (x + 1) * 128] = kept
    for ab in range(9):
        a, b = ab // 3, ab % 3
        taps = []
        for e in range(3):
            parts = [
                cp_ref[a : a + 4, b : b + 4, (e + r) // 2 : (e + r) // 2 + 2, (e + r) % 2]
                for r in range(2)
            ]
            parts = [part.reshape(32 * CR, 128) for part in parts]
            taps.append(jnp.concatenate(parts, axis=0))
        found = dot(cst_ref[...], jnp.concatenate(taps, axis=1))
        for e in range(3):
            at = (3 * ab + e) * 128
            gc_ref[at : at + 128, :] = jnp.transpose(found[:, e * 128 : (e + 1) * 128])

    fill(nl_ref, cs_ref, sp_ref)
    scatter_flat(cin_ref, convolve(sp_ref, wt_ref).astype(BF))

    hidden_grad = dot(up_f[FB : 2 * FB].astype(BF), cin_ref[...])
    pieces = []
    for pq in range(4):
        slope = hidden_grad[:, pq * 256 : (pq + 1) * 256] * dslope_ref[pq]
        pieces += [slope, zeros8((8, 256))]
    down = jnp.transpose(jnp.concatenate(pieces, axis=0)).astype(BF)
    for ab in range(9):
        a, b = ab // 3, ab % 3
        taps = [mine_ref[(2 * p + a) * 5 + 2 * q + b] for p in range(2) for q in range(2)]
        taps = jnp.concatenate(taps, axis=0)
        low = dot(down[0:128], jnp.concatenate([taps[:, 0:128], taps[:, 256:384]], axis=1))
        high = dot(down[128:256], taps[:, 0:256])
        later = low[:, 0:128] + high[:, 128:256]
        first = low[:, 128:256] + high[:, 0:128]
        gd_ref[(3 * ab) * 64 : (3 * ab + 1) * 64, :] = jnp.transpose(first)[64:128]
        gd_ref[(3 * ab + 1) * 64 : (3 * ab + 3) * 64, :] = jnp.transpose(later)

    for t in range(TILES):
        if t < 27:
            tile = gd_ref[pl.ds(t, 64, stride=27), :]
        elif t < 81:
            tile = gc_ref[pl.ds(t - 27, 64, stride=54), :]
        elif t < 89:
            tile = gu_ref[(t - 81) % 4, pl.ds((t - 81) // 4, 64, stride=2), :]
        else:
            tile = jnp.zeros((64, 128), F32)
        n = t % 12
        sum_ref[t // 12 % 2, t // 24, :, n * 128 : (n + 1) * 128] = tile.astype(BF)


def forward_pass(own, prev, nxt, far, wd, wc):
    vmem = pl.BlockSpec(memory_space=pltpu.VMEM)
    made = (
        ((25, FB + 8, 384), BF),
        ((ROWS, 128), F32),
        ((4, HALO, 128), BF),
        ((6, 6, 3, 2, CR, 128), BF),
        ((32 * CR, 256), F32),
        ((8 * CR, 1024), BF),
        ((4, FB, 256), F32),
    )
    return pl.pallas_call(
        forward,
        out_shape=tuple(jax.ShapeDtypeStruct(*one) for one in made),
        in_specs=[vmem] * 6,
        out_specs=(vmem,) * len(made),
        scratch_shapes=[
            pltpu.VMEM((4 * FB, UPPER), BF),
            pltpu.VMEM((25, ROWS, 384), BF),
            pltpu.VMEM((ROWS, 1024), BF),
            pltpu.VMEM((8 * CR, 1024), BF),
        ],
        compiler_params=pltpu.CompilerParams(vmem_limit_bytes=VMEM_A),
    )(own, prev, nxt, far, wd, wc)


def backward_pass(*given):
    vmem = pl.BlockSpec(memory_space=pltpu.VMEM)
    return pl.pallas_call(
        backward,
        out_shape=(
            jax.ShapeDtypeStruct((FB, XL), BF),
            jax.ShapeDtypeStruct((2, 4, 64, 1536), BF),
        ),
        in_specs=[vmem] * len(given),
        out_specs=(vmem, vmem),
        scratch_shapes=[
            pltpu.VMEM((ROWS, 1024), BF),
            pltpu.VMEM((8 * CR, 1024), BF),
            pltpu.VMEM((8 * CR, 1024), BF),
            pltpu.VMEM((6, 6, 3, 2, CR, 128), BF),
            pltpu.VMEM((128, 64 * CR), BF),
            pltpu.VMEM((32 * CR, 256), F32),
            pltpu.VMEM((1728, 128), F32),
            pltpu.VMEM((3456, 128), F32),
            pltpu.VMEM((4, 128, 128), F32),
        ],
        compiler_params=pltpu.CompilerParams(vmem_limit_bytes=VMEM_B),
    )(*given)


def pack(place_ref, *refs):
    given, held, sems = refs[:5], refs[8:13], refs[13]
    own_ref, cots_ref, far_ref = refs[5:8]
    copies = [
        pltpu.make_async_copy(source, target, sems.at[n])
        for n, (source, target) in enumerate(zip(given, held))
    ]
    for copy in copies:
        copy.start()
    for copy in copies:
        copy.wait()
    x_ref, cot_ref, fine_ref, parent_ref, coarse_ref = held
    place = place_ref[0]
    own_ref[:, 0:XL] = x_ref[...].reshape(FB, XL)
    cot = cot_ref[...].reshape(FB, XL)
    own_ref[:, XL:IDX] = cot[:, 0:EARLY]
    cots_ref[...] = cot[:, EARLY:XL]
    fine = jnp.concatenate([fine_ref[m] for m in range(7)], axis=0)
    fine = jnp.where(fine < 0, 0, fine - (FB * (place - 1) - 1)).astype(F32)
    coarse = jnp.concatenate([coarse_ref[c] for c in range(CB)], axis=0)
    coarse = jnp.where(coarse < 0, 0, coarse - (CB * (place - 1) - 1)).astype(F32)
    coarse = jnp.concatenate([coarse, jnp.zeros((FB - CB, 26), F32)], axis=0)
    parent = (parent_ref[...] - (8 * (CB * place - 1) - 1)).astype(F32)
    lists = jnp.concatenate([fine, parent], axis=0).astype(BF)
    unit = lax.broadcasted_iota(jnp.int32, (FB, FB), 0) == lax.broadcasted_iota(
        jnp.int32, (FB, FB), 1
    )
    lists = dot(jnp.where(unit, 1.0, 0.0).astype(BF), lists, ((1,), (1,)))
    filler = jnp.zeros((FB, 128 - 34), F32)
    own_ref[:, IDX : IDX + 128] = jnp.concatenate([lists, coarse, filler], axis=1).astype(BF)
    at = 0
    last = []
    for start, width in upper_pieces():
        if width > 128:
            far_ref[:, at : at + width] = own_ref[:, start : start + width]
        else:
            last.append(own_ref[:, start : start + width].astype(F32))
        at += width
    upper_half = lax.broadcasted_iota(jnp.int32, (FB, 128), 1) >= 64
    for n in range(5):
        first = swap_halves(last[2 * n])
        second = last[2 * n + 1] if 2 * n + 1 < 9 else first
        tile = jnp.where(upper_half, second, first)
        far_ref[:, 1792 + n * 128 : 1920 + n * 128] = tile.astype(BF)


def packed(place, features, cotangent, fine_nbr, parents, coarse_nbr):
    vmem = pl.BlockSpec(memory_space=pltpu.VMEM)
    return pl.pallas_call(
        pack,
        out_shape=(
            jax.ShapeDtypeStruct((FB, IDX + 128), BF),
            jax.ShapeDtypeStruct((FB, XL - EARLY), BF),
            jax.ShapeDtypeStruct((FB, SENT), BF),
        ),
        in_specs=[pl.BlockSpec(memory_space=pltpu.SMEM)]
        + [pl.BlockSpec(memory_space=pltpu.HBM)] * 5,
        out_specs=(vmem,) * 3,
        scratch_shapes=[
            pltpu.VMEM(array.shape, array.dtype)
            for array in (features, cotangent, fine_nbr, parents, coarse_nbr)
        ]
        + [pltpu.SemaphoreType.DMA((5,))],
        compiler_params=pltpu.CompilerParams(vmem_limit_bytes=8 * 2**20),
    )(place, *in_hbm(features, cotangent, fine_nbr, parents, coarse_nbr))


SPACE = ("x", "z")


def shift(block, distance):
    size = lax.axis_size(SPACE)
    route = [(i, i + distance) for i in range(size) if 0 <= i + distance < size]
    return lax.ppermute(block, SPACE, route)


def sum_copies(in_ref, out_ref):
    total = jnp.sum(in_ref[...].astype(F32), axis=0)
    for n in range(out_ref.shape[0]):
        out_ref[n] = total


def split(in_ref, down_ref, coarse_ref, up_ref):
    whole = jnp.concatenate([in_ref[n] for n in range(8)], axis=0)
    down_ref[...] = whole[0:27]
    coarse_ref[...] = whole[27:81]
    up_ref[...] = whole[81:89]


def spread_sum(sums):
    held = lax.all_to_all(sums, "core", 0, 0)
    held = jnp.sum(held.astype(F32), axis=0).astype(BF)
    held = held.reshape(16, 16, 1536)
    held = lax.all_to_all(held, ("y", "x"), 0, 0)
    held = jnp.sum(held.astype(F32), axis=0).astype(BF)
    held = held.reshape(16, 12, 128)
    held = lax.all_to_all(held, "z", 0, 0)
    held = pl.pallas_call(
        sum_copies,
        out_shape=jax.ShapeDtypeStruct((8, 12, 128), F32),
        compiler_params=pltpu.CompilerParams(vmem_limit_bytes=2 * 2**20),
    )(held)
    held = lax.all_to_all(held, ("y", "core"), 0, 0)
    shares = pl.pallas_call(
        split,
        out_shape=tuple(jax.ShapeDtypeStruct((n, 128), F32) for n in (27, 54, 8)),
        compiler_params=pltpu.CompilerParams(vmem_limit_bytes=2 * 2**20),
    )(held)
    return tuple(share.reshape(-1) for share in shares)


def gradients(
    fine_features,
    cotangent,
    down_weight,
    coarse_weight,
    up_weight,
    fine_neighbours,
    children,
    parent_slots,
    coarse_neighbours,
):
    place = lax.axis_index(SPACE).astype(jnp.int32).reshape(1)
    own, cot, upper = packed(
        place,
        fine_features[0],
        cotangent[0],
        fine_neighbours.transpose(2, 0, 1),
        parent_slots,
        coarse_neighbours[0].reshape(CB, 1, 26),
    )
    prev = shift(own, 1)
    far = shift(upper, 2)
    nxt = shift(own, -1)
    cot_prev = shift(cot, 1)
    cot_next = shift(cot, -1)
    wide_down, wide, turned = widened(down_weight, coarse_weight)
    kept = forward_pass(own, prev, nxt, far, wide_down, wide)
    return backward_pass(own, prev, nxt, cot, cot_prev, cot_next, turned, up_weight, *kept)


def body(fine_features, *rest):
    decoded, sums = gradients(fine_features, *rest)
    return (decoded.reshape(fine_features.shape), *spread_sum(sums))


def solution(mesh):
    mesh = jax.sharding.Mesh(mesh.devices.reshape(4, 2, 4, 16), ("y", "core", "x", "z"))
    dp = ("y", "core")
    in_specs = (
        P(dp, SPACE, None, None, None),
        P(dp, SPACE, None, None, None),
        P(),
        P(),
        P(),
        P(dp, SPACE, None),
        P(dp, SPACE, None),
        P(dp, SPACE),
        P(dp, SPACE, None),
    )
    out_specs = (P(dp, SPACE, None, None, None), P(SPACE), P(SPACE), P(SPACE))
    return jax.shard_map(body, mesh=mesh, in_specs=in_specs, out_specs=out_specs, check_vma=False)
```

```python
import functools

import jax
import jax.numpy as jnp
from jax import lax
from jax.experimental import pallas as pl
from jax.experimental.pallas import tpu as pltpu
from jax.sharding import PartitionSpec as P

BF = jnp.bfloat16
F32 = jnp.float32
FB = 24
CB = 6
ROWS = 80
CR = 16
XL = 4096
IDX = XL
COT = XL + 128
FULL = COT + XL
EARLY = COT + 7 * 256
VMEM_A, VMEM_B = 20 * 2**20, 24 * 2**20
TILES = 96


def plane_lanes(i, j):
    if i == 3:
        return (j * 256, 256)
    if j == 3:
        return (1024 + i * 256, 256)
    return (1792 + (i * 3 + j) * 128, 128)


def upper_pieces():
    pieces = [(3 * 1024, 1024)]
    pieces += [((i * 4 + 3) * 256, 256) for i in range(3)]
    pieces += [((i * 4 + j) * 256 + 128, 128) for i in range(3) for j in range(3)]
    return pieces


UPPER = sum(width for _, width in upper_pieces())
SENT = 1792 + 5 * 128


def dot(a, b, dims=((1,), (0,))):
    return lax.dot_general(a, b, (dims, ((), ())), preferred_element_type=F32)


def gate(v):
    s = 1.0 / (1.0 + jnp.exp(-v))
    return v * s, s * (1.0 + v * (1.0 - s))


def axis_sides(half):
    inner = [(0, 0, half + 1), (0, 1, half + 3)]
    return inner + ([(-1, 1, 0)] if half else [(1, 0, 5)])


def halo_blocks(p, q):
    blocks = []
    for sx, ox, cx in axis_sides(p):
        for sy, oy, cy in axis_sides(q):
            for sz, oz, cells in (
                (0, 0, [(0, 1), (1, 2)]),
                (0, 1, [(0, 3), (1, 4)]),
                (-1, 1, [(1, 0)]),
                (1, 0, [(0, 5)]),
            ):
                code = 9 * (sx + 1) + 3 * (sy + 1) + sz + 1
                if code != 13:
                    targets = [(r, (cx, cy, cz)) for r, cz in cells]
                    blocks.append((code - (code > 13), 4 * ox + 2 * oy + oz, targets))
    return blocks


HALO = len(halo_blocks(0, 0)) * CR


def swap_halves(tile):
    return jnp.concatenate([tile[:, 64:128], tile[:, 0:64]], axis=1)


def octant_of(x, y, z):
    return 4 * (x // 2) + 2 * (y // 2) + z // 2, 4 * (x % 2) + 2 * (y % 2) + z % 2


def in_hbm(*arrays):
    return [pltpu.with_memory_space_constraint(array, pltpu.HBM) for array in arrays]


def widen(wd_hbm, wc_hbm, down_ref, coarse_ref, turned_ref, wd_ref, wc_ref, sems):
    first = pltpu.make_async_copy(wd_hbm, wd_ref, sems.at[0])
    second = pltpu.make_async_copy(wc_hbm, wc_ref, sems.at[1])
    first.start()
    second.start()
    down_ref[...] = jnp.zeros(down_ref.shape, BF)
    first.wait()
    for ab in range(9):
        tap = [wd_ref[(3 * ab + e) * 64 : (3 * ab + e + 1) * 64, :] for e in range(3)]
        at = ab * 384
        for row, e in ((0, 1), (64, 2), (320, 0)):
            down_ref[at + row : at + row + 64, 0:128] = tap[e]
        for row, e in ((64, 0), (128, 1), (192, 2)):
            down_ref[at + row : at + row + 64, 128:256] = tap[e]
    second.wait()
    zero = jnp.zeros((128, 128), BF)
    for ab in range(9):
        for e in range(3):
            tap = 3 * ab + e
            plain = wc_ref[tap * 128 : (tap + 1) * 128, :]
            other = (26 - tap) * 128
            turned = jnp.transpose(wc_ref[other : other + 128, :].astype(F32)).astype(BF)
            for ref, block in ((coarse_ref, plain), (turned_ref, turned)):
                for r in range(2):
                    row = ab * 512 + (e + r) * 128
                    ref[row : row + 128, r * 128 : (r + 1) * 128] = block
        for ref in (coarse_ref, turned_ref):
            ref[ab * 512 + 384 : ab * 512 + 512, 0:128] = zero
            ref[ab * 512 : ab * 512 + 128, 128:256] = zero


def widened(down_weight, coarse_weight):
    vmem = pl.BlockSpec(memory_space=pltpu.VMEM)
    shapes = ((9 * 384, 256), (9 * 512, 256), (9 * 512, 256))
    return pl.pallas_call(
        widen,
        out_shape=tuple(jax.ShapeDtypeStruct(shape, BF) for shape in shapes),
        in_specs=[pl.BlockSpec(memory_space=pltpu.HBM)] * 2,
        out_specs=(vmem,) * 3,
        scratch_shapes=[
            pltpu.VMEM(down_weight.shape, BF),
            pltpu.VMEM(coarse_weight.shape, BF),
            pltpu.SemaphoreType.DMA((2,)),
        ],
        compiler_params=pltpu.CompilerParams(vmem_limit_bytes=12 * 2**20),
    )(*in_hbm(down_weight, coarse_weight))


def rows_of(refs, lane, width):
    parts = [ref[:, lane : lane + width].astype(F32) for ref in refs]
    return jnp.concatenate(parts + [jnp.zeros((ROWS - 3 * FB, width), F32)], axis=0)


def to_coarse(up, ref):
    return dot(up, ref[...], ((0,), (0,)))


def fill(nl_ref, flat_ref, padded_ref):
    for x in range(4):
        for y in range(4):
            for z in range(4):
                o, v = octant_of(x, y, z)
                padded_ref[x + 1, y + 1, (z + 1) // 2, (z + 1) % 2] = flat_ref[
                    o * CR : (o + 1) * CR, v * 128 : (v + 1) * 128
                ]
    for pq in range(4):
        got = dot(nl_ref[pq], flat_ref[:, pq * 256 : (pq + 1) * 256]).astype(BF)
        for n, (_, _, targets) in enumerate(halo_blocks(pq // 2, pq % 2)):
            for r, (cx, cy, cz) in targets:
                padded_ref[cx, cy, cz // 2, cz % 2] = got[
                    n * CR : (n + 1) * CR, r * 128 : (r + 1) * 128
                ]


def convolve(padded_ref, weight_ref):
    outs = []
    for x in range(0, 4, 1):
        taps = [
            padded_ref[x + a : x + a + 1, b : b + 4, zz // 2 : zz // 2 + 2, zz % 2].reshape(1 * 8 * CR, 128)
            for a in range(3)
            for b in range(3)
            for zz in range(4)
        ]
        outs.append(dot(jnp.concatenate(taps, axis=1), weight_ref[...]))
    return jnp.concatenate(outs, axis=0)


VOXELS = [
    (row * CR, r * 128, octant_of(row // 8, row // 2 % 4, row % 2 * 2 + r))
    for row in range(32)
    for r in range(2)
]


def scatter_flat(ref, value):
    for row, lane, (o, v) in VOXELS:
        piece = value[row : row + CR, lane : lane + 128]
        ref[o * CR : (o + 1) * CR, v * 128 : (v + 1) * 128] = piece


def forward(
    own_ref,
    prev_ref,
    next_ref,
    far_ref,
    wd_ref,
    wc_ref,
    mine_ref,
    up_ref,
    nl_ref,
    cp_ref,
    cslope_ref,
    cout_ref,
    dslope_ref,
    src_ref,
    pad_ref,
    hid_ref,
    cin_ref,
):
    zeros8 = functools.partial(jnp.zeros, dtype=F32)
    rows = functools.partial(rows_of, (prev_ref, own_ref, next_ref))

    idx = rows(IDX, 128)
    row = lax.broadcasted_iota(jnp.int32, (ROWS, 128), 0)
    lane = lax.broadcasted_iota(jnp.int32, (ROWS, 128), 1)
    block = jnp.where(row >= FB, 1.0, 0.0) + jnp.where(row >= 2 * FB, 1.0, 0.0)
    lane_f = lane.astype(F32)

    at = 0
    for n, (start, width) in enumerate(upper_pieces()):
        if width > 128:
            far = far_ref[:, at : at + width].astype(F32)
        else:
            tile = 1792 + (n - 4) // 2 * 128
            far = far_ref[:, tile : tile + 128].astype(F32)
            far = far if (n - 4) % 2 else swap_halves(far)
        parts = [far]
        parts += [r[:, start : start + width].astype(F32) for r in (prev_ref, own_ref, next_ref)]
        src_ref[:, at : at + width] = jnp.concatenate(parts, axis=0).astype(BF)
        at += width

    def pick(code):
        wanted = idx[:, code - 1 : code] + (24.0 * block[:, 0:1] - 1.0)
        wanted = jnp.where(idx[:, code - 1 : code] > 0.0, wanted, -1.0)
        hit = jnp.where(lane_f[:, 0 : 4 * FB] == wanted, 1.0, 0.0)
        return hit.astype(BF)

    picks = {code: pick(code) for code in range(1, 8)}

    def fetch(code, i, j, last):
        start, width = plane_lanes(i, j)
        if last:
            start, width = start + width - 128, 128
        return dot(picks[code], src_ref[:, start : start + width])

    def only_own(array):
        return jnp.concatenate([array[FB : 2 * FB], zeros8((8, array.shape[1]))], axis=0)

    for ip in range(5):
        for jp in range(5):
            i, j = (ip - 1) % 4, (jp - 1) % 4
            code = 4 * (ip == 0) + 2 * (jp == 0)
            if code:
                own = fetch(code, i, j, False)
            else:
                own = rows((i * 4 + j) * 256, 256)
            behind = fetch(code + 1, i, j, True)
            pad_ref[ip * 5 + jp, :, 0:256] = own.astype(BF)
            pad_ref[ip * 5 + jp, :, 256:384] = behind.astype(BF)
            mine_ref[ip * 5 + jp, :, 0:256] = only_own(own).astype(BF)
            mine_ref[ip * 5 + jp, :, 256:384] = only_own(behind).astype(BF)

    outs = []
    for p in range(2):
        for q in range(2):
            taps = [pad_ref[(2 * p + a) * 5 + 2 * q + b] for a in range(3) for b in range(3)]
            outs.append(dot(jnp.concatenate(taps, axis=1), wd_ref[...]))
    pre = jnp.concatenate(outs, axis=0)
    for pq in range(4):
        value, slope = gate(pre[pq * ROWS : (pq + 1) * ROWS])
        hid_ref[:, pq * 256 : (pq + 1) * 256] = value.astype(BF)
        dslope_ref[pq] = slope[FB : 2 * FB]

    code = idx[:, 7:8]
    slot = jnp.where(code > 0.0, code + (48.0 * block[:, 0:1] - 9.0), -1.0)
    column = (lane % CR * 8 + lane // CR).astype(F32)
    up_f = jnp.where(column == slot, 1.0, 0.0)
    up_ref[...] = up_f
    up = up_f.astype(BF)

    row16 = lax.broadcasted_iota(jnp.int32, (CR, ROWS), 0)
    lane80 = lax.broadcasted_iota(jnp.int32, (CR, ROWS), 1)
    device = jnp.where(row16 >= CB, 1, 0) + jnp.where(row16 >= 2 * CB, 1, 0)
    choose = jnp.where(lane80 == row16 + (FB - CB) * device, 1.0, 0.0).astype(BF)
    listed = dot(choose, idx.astype(BF))
    device = device[:, 0:1].astype(F32)
    place = listed + (6.0 * device - 7.0)
    place = jnp.where((listed > 0.0) & (place >= 0.0) & (place < CR), place, -1000.0)
    lane16 = lane_f[0:CR]
    for pq in range(4):
        blocks = []
        for m, octant, _ in halo_blocks(pq // 2, pq % 2):
            wanted = place[:, 8 + m : 9 + m] + float(CR * octant)
            blocks.append(jnp.where(lane16 == wanted, 1.0, 0.0))
        nl_ref[pq] = jnp.concatenate(blocks, axis=0).astype(BF)

    cin_ref[...] = to_coarse(up, hid_ref).astype(BF)
    fill(nl_ref, cin_ref, cp_ref)
    value, slope = gate(convolve(cp_ref, wc_ref))
    cslope_ref[...] = slope
    scatter_flat(cout_ref, value.astype(BF))


def backward(
    own_ref,
    prev_ref,
    next_ref,
    late_ref,
    wt_ref,
    wu_ref,
    mine_ref,
    up_ref,
    nl_ref,
    cp_ref,
    cslope_ref,
    cout_ref,
    dslope_ref,
    dec_ref,
    sum_ref,
    hid_ref,
    cin_ref,
    cs_ref,
    sp_ref,
    cst_ref,
    grad_ref,
    gd_ref,
    gc_ref,
    gu_ref,
):
    zeros8 = functools.partial(jnp.zeros, dtype=F32)
    rows = functools.partial(rows_of, (prev_ref, own_ref, next_ref))


    def cot_rows(lane, width):
        lane += COT
        if lane < EARLY:
            return rows(lane, width)
        parts = [late_ref[:, lane - EARLY : lane - EARLY + width].astype(F32)]
        parts += [ref[:, lane : lane + width].astype(F32) for ref in (own_ref, next_ref)]
        return jnp.concatenate(parts + [zeros8((ROWS - 3 * FB, width))], axis=0)

    up_f = up_ref[...]
    up = up_f.astype(BF)

    up_in = dot(up, cout_ref[...])
    pieces = [up_in[:, v * 128 : (v + 1) * 128] for v in range(8)]
    own_in = [piece[FB : 2 * FB] for piece in pieces]
    out = dot(jnp.concatenate(pieces, axis=0).astype(BF), wu_ref[...])
    all_grad, own_grad = [], []
    for v in range(8):
        p, q, r = v // 4, v // 2 % 2, v % 2
        grads = []
        for ab in range(4):
            a, b = ab // 2, ab % 2
            at = ((2 * p + a) * 4 + 2 * q + b) * 256 + r * 128
            joined = out[v * ROWS : (v + 1) * ROWS, ab * 128 : (ab + 1) * 128] + rows(at, 128)
            value, slope = gate(joined)
            dec_ref[:, at : at + 128] = value[FB : 2 * FB].astype(BF)
            grads.append(cot_rows(at, 128) * slope)
        grad = jnp.concatenate(grads, axis=1)
        own_grad.append(grad[FB : 2 * FB])
        all_grad.append(grad.astype(BF))
    back = dot(jnp.concatenate(all_grad, axis=0), wu_ref[...], ((1,), (1,))).astype(BF)
    for v in range(8):
        hid_ref[:, v * 128 : (v + 1) * 128] = back[v * ROWS : (v + 1) * ROWS]
    own_in = jnp.concatenate(own_in, axis=0).astype(BF)
    own_grad = jnp.concatenate(own_grad, axis=0).astype(BF)
    found = dot(own_in, own_grad, ((0,), (0,)))
    for n in range(4):
        gu_ref[n] = found[:, n * 128 : (n + 1) * 128]

    cin_ref[...] = to_coarse(up, hid_ref).astype(BF)
    row_c = lax.broadcasted_iota(jnp.int32, (8 * CR, 128), 0) % CR
    mine = (row_c >= CB) & (row_c < 2 * CB)
    for row, lane, (o, v) in VOXELS:
        grad = cin_ref[o * CR : (o + 1) * CR, v * 128 : (v + 1) * 128].astype(F32)
        grad = grad * cslope_ref[row : row + CR, lane : lane + 128]
        grad_ref[row : row + CR, lane : lane + 128] = grad
        cs_ref[o * CR : (o + 1) * CR, v * 128 : (v + 1) * 128] = grad.astype(BF)
    for x in range(4):
        for r in range(2):
            kept = grad_ref[x * 128 : (x + 1) * 128, r * 128 : (r + 1) * 128]
            kept = jnp.transpose(jnp.where(mine, kept, 0.0)).astype(BF)
            cst_ref[:, r * 512 + x * 128 : r * 512 + (x + 1) * 128] = kept
    for ab in range(9):
        a, b = ab // 3, ab % 3
        taps = []
        for e in range(3):
            parts = [
                cp_ref[a : a + 4, b : b + 4, (e + r) // 2 : (e + r) // 2 + 2, (e + r) % 2]
                for r in range(2)
            ]
            parts = [part.reshape(32 * CR, 128) for part in parts]
            taps.append(jnp.concatenate(parts, axis=0))
        found = dot(cst_ref[...], jnp.concatenate(taps, axis=1))
        for e in range(3):
            at = (3 * ab + e) * 128
            gc_ref[at : at + 128, :] = jnp.transpose(found[:, e * 128 : (e + 1) * 128])

    fill(nl_ref, cs_ref, sp_ref)
    scatter_flat(cin_ref, convolve(sp_ref, wt_ref).astype(BF))

    hidden_grad = dot(up_f[FB : 2 * FB].astype(BF), cin_ref[...])
    pieces = []
    for pq in range(4):
        slope = hidden_grad[:, pq * 256 : (pq + 1) * 256] * dslope_ref[pq]
        pieces += [slope, zeros8((8, 256))]
    down = jnp.transpose(jnp.concatenate(pieces, axis=0)).astype(BF)
    for ab in range(9):
        a, b = ab // 3, ab % 3
        taps = [mine_ref[(2 * p + a) * 5 + 2 * q + b] for p in range(2) for q in range(2)]
        taps = jnp.concatenate(taps, axis=0)
        low = dot(down[0:128], jnp.concatenate([taps[:, 0:128], taps[:, 256:384]], axis=1))
        high = dot(down[128:256], taps[:, 0:256])
        later = low[:, 0:128] + high[:, 128:256]
        first = low[:, 128:256] + high[:, 0:128]
        gd_ref[(3 * ab) * 64 : (3 * ab + 1) * 64, :] = jnp.transpose(first)[64:128]
        gd_ref[(3 * ab + 1) * 64 : (3 * ab + 3) * 64, :] = jnp.transpose(later)

    for t in range(TILES):
        if t < 27:
            tile = gd_ref[pl.ds(t, 64, stride=27), :]
        elif t < 81:
            tile = gc_ref[pl.ds(t - 27, 64, stride=54), :]
        elif t < 89:
            tile = gu_ref[(t - 81) % 4, pl.ds((t - 81) // 4, 64, stride=2), :]
        else:
            tile = jnp.zeros((64, 128), F32)
        n = t % 12
        sum_ref[t // 12 % 2, t // 24, :, n * 128 : (n + 1) * 128] = tile.astype(BF)


def forward_pass(own, prev, nxt, far, wd, wc):
    vmem = pl.BlockSpec(memory_space=pltpu.VMEM)
    made = (
        ((25, FB + 8, 384), BF),
        ((ROWS, 128), F32),
        ((4, HALO, 128), BF),
        ((6, 6, 3, 2, CR, 128), BF),
        ((32 * CR, 256), F32),
        ((8 * CR, 1024), BF),
        ((4, FB, 256), F32),
    )
    return pl.pallas_call(
        forward,
        out_shape=tuple(jax.ShapeDtypeStruct(*one) for one in made),
        in_specs=[vmem] * 6,
        out_specs=(vmem,) * len(made),
        scratch_shapes=[
            pltpu.VMEM((4 * FB, UPPER), BF),
            pltpu.VMEM((25, ROWS, 384), BF),
            pltpu.VMEM((ROWS, 1024), BF),
            pltpu.VMEM((8 * CR, 1024), BF),
        ],
        compiler_params=pltpu.CompilerParams(vmem_limit_bytes=VMEM_A),
    )(own, prev, nxt, far, wd, wc)


def backward_pass(*given):
    vmem = pl.BlockSpec(memory_space=pltpu.VMEM)
    return pl.pallas_call(
        backward,
        out_shape=(
            jax.ShapeDtypeStruct((FB, XL), BF),
            jax.ShapeDtypeStruct((2, 4, 64, 1536), BF),
        ),
        in_specs=[vmem] * len(given),
        out_specs=(vmem, vmem),
        scratch_shapes=[
            pltpu.VMEM((ROWS, 1024), BF),
            pltpu.VMEM((8 * CR, 1024), BF),
            pltpu.VMEM((8 * CR, 1024), BF),
            pltpu.VMEM((6, 6, 3, 2, CR, 128), BF),
            pltpu.VMEM((128, 64 * CR), BF),
            pltpu.VMEM((32 * CR, 256), F32),
            pltpu.VMEM((1728, 128), F32),
            pltpu.VMEM((3456, 128), F32),
            pltpu.VMEM((4, 128, 128), F32),
        ],
        compiler_params=pltpu.CompilerParams(vmem_limit_bytes=VMEM_B),
    )(*given)


def pack(place_ref, *refs):
    given, held, sems = refs[:5], refs[9:14], refs[14]
    own_ref, early_ref, late_ref, far_ref = refs[5:9]
    copies = [
        pltpu.make_async_copy(source, target, sems.at[n])
        for n, (source, target) in enumerate(zip(given, held))
    ]
    for copy in copies:
        copy.start()
    for copy in copies:
        copy.wait()
    x_ref, cot_ref, fine_ref, parent_ref, coarse_ref = held
    place = place_ref[0]
    own_ref[:, 0:XL] = x_ref[...].reshape(FB, XL)
    cot = cot_ref[...].reshape(FB, XL)
    own_ref[:, COT:FULL] = cot
    late_ref[...] = cot[:, EARLY - COT : XL]
    fine = jnp.concatenate([fine_ref[m] for m in range(7)], axis=0)
    fine = jnp.where(fine < 0, 0, fine - (FB * (place - 1) - 1)).astype(F32)
    coarse = jnp.concatenate([coarse_ref[c] for c in range(CB)], axis=0)
    coarse = jnp.where(coarse < 0, 0, coarse - (CB * (place - 1) - 1)).astype(F32)
    coarse = jnp.concatenate([coarse, jnp.zeros((FB - CB, 26), F32)], axis=0)
    parent = (parent_ref[...] - (8 * (CB * place - 1) - 1)).astype(F32)
    lists = jnp.concatenate([fine, parent], axis=0).astype(BF)
    unit = lax.broadcasted_iota(jnp.int32, (FB, FB), 0) == lax.broadcasted_iota(
        jnp.int32, (FB, FB), 1
    )
    lists = dot(jnp.where(unit, 1.0, 0.0).astype(BF), lists, ((1,), (1,)))
    filler = jnp.zeros((FB, 128 - 34), F32)
    own_ref[:, IDX:COT] = jnp.concatenate([lists, coarse, filler], axis=1).astype(BF)
    early_ref[...] = own_ref[:, 0:EARLY]
    at = 0
    last = []
    for start, width in upper_pieces():
        if width > 128:
            far_ref[:, at : at + width] = own_ref[:, start : start + width]
        else:
            last.append(own_ref[:, start : start + width].astype(F32))
        at += width
    upper_half = lax.broadcasted_iota(jnp.int32, (FB, 128), 1) >= 64
    for n in range(5):
        first = swap_halves(last[2 * n])
        second = last[2 * n + 1] if 2 * n + 1 < 9 else first
        tile = jnp.where(upper_half, second, first)
        far_ref[:, 1792 + n * 128 : 1920 + n * 128] = tile.astype(BF)


def packed(place, features, cotangent, fine_nbr, parents, coarse_nbr):
    vmem = pl.BlockSpec(memory_space=pltpu.VMEM)
    return pl.pallas_call(
        pack,
        out_shape=(
            jax.ShapeDtypeStruct((FB, FULL), BF),
            jax.ShapeDtypeStruct((FB, EARLY), BF),
            jax.ShapeDtypeStruct((FB, FULL - EARLY), BF),
            jax.ShapeDtypeStruct((FB, SENT), BF),
        ),
        in_specs=[pl.BlockSpec(memory_space=pltpu.SMEM)]
        + [pl.BlockSpec(memory_space=pltpu.HBM)] * 5,
        out_specs=(vmem,) * 4,
        scratch_shapes=[
            pltpu.VMEM(array.shape, array.dtype)
            for array in (features, cotangent, fine_nbr, parents, coarse_nbr)
        ]
        + [pltpu.SemaphoreType.DMA((5,))],
        compiler_params=pltpu.CompilerParams(vmem_limit_bytes=8 * 2**20),
    )(place, *in_hbm(features, cotangent, fine_nbr, parents, coarse_nbr))


SPACE = ("x", "z")


def shift(block, distance):
    size = lax.axis_size(SPACE)
    route = [(i, i + distance) for i in range(size) if 0 <= i + distance < size]
    return lax.ppermute(block, SPACE, route)


def sum_copies(in_ref, out_ref):
    total = jnp.sum(in_ref[...].astype(F32), axis=0)
    for n in range(out_ref.shape[0]):
        out_ref[n] = total


def split(in_ref, down_ref, coarse_ref, up_ref):
    whole = jnp.concatenate([in_ref[n] for n in range(8)], axis=0)
    down_ref[...] = whole[0:27]
    coarse_ref[...] = whole[27:81]
    up_ref[...] = whole[81:89]


def spread_sum(sums):
    held = lax.all_to_all(sums, "core", 0, 0)
    held = jnp.sum(held.astype(F32), axis=0).astype(BF)
    held = held.reshape(16, 16, 1536)
    held = lax.all_to_all(held, ("y", "x"), 0, 0)
    held = jnp.sum(held.astype(F32), axis=0).astype(BF)
    held = held.reshape(16, 12, 128)
    held = lax.all_to_all(held, "z", 0, 0)
    held = pl.pallas_call(
        sum_copies,
        out_shape=jax.ShapeDtypeStruct((8, 12, 128), F32),
        compiler_params=pltpu.CompilerParams(vmem_limit_bytes=2 * 2**20),
    )(held)
    held = lax.all_to_all(held, ("y", "core"), 0, 0)
    shares = pl.pallas_call(
        split,
        out_shape=tuple(jax.ShapeDtypeStruct((n, 128), F32) for n in (27, 54, 8)),
        compiler_params=pltpu.CompilerParams(vmem_limit_bytes=2 * 2**20),
    )(held)
    return tuple(share.reshape(-1) for share in shares)


def gradients(
    fine_features,
    cotangent,
    down_weight,
    coarse_weight,
    up_weight,
    fine_neighbours,
    children,
    parent_slots,
    coarse_neighbours,
):
    place = lax.axis_index(SPACE).astype(jnp.int32).reshape(1)
    own, early, late, upper = packed(
        place,
        fine_features[0],
        cotangent[0],
        fine_neighbours.transpose(2, 0, 1),
        parent_slots,
        coarse_neighbours[0].reshape(CB, 1, 26),
    )
    prev = shift(early, 1)
    far = shift(upper, 2)
    nxt = shift(own, -1)
    late = shift(late, 1)
    wide_down, wide, turned = widened(down_weight, coarse_weight)
    kept = forward_pass(own, prev, nxt, far, wide_down, wide)
    return backward_pass(own, prev, nxt, late, turned, up_weight, *kept)


def body(fine_features, *rest):
    decoded, sums = gradients(fine_features, *rest)
    return (decoded.reshape(fine_features.shape), *spread_sum(sums))


def solution(mesh):
    mesh = jax.sharding.Mesh(mesh.devices.reshape(4, 2, 4, 16), ("y", "core", "x", "z"))
    dp = ("y", "core")
    in_specs = (
        P(dp, SPACE, None, None, None),
        P(dp, SPACE, None, None, None),
        P(),
        P(),
        P(),
        P(dp, SPACE, None),
        P(dp, SPACE, None),
        P(dp, SPACE),
        P(dp, SPACE, None),
    )
    out_specs = (P(dp, SPACE, None, None, None), P(SPACE), P(SPACE), P(SPACE))
    return jax.shard_map(body, mesh=mesh, in_specs=in_specs, out_specs=out_specs, check_vma=False)
```

```python
import functools

import jax
import jax.numpy as jnp
from jax import lax
from jax.experimental import pallas as pl
from jax.experimental.pallas import tpu as pltpu
from jax.sharding import PartitionSpec as P

BF = jnp.bfloat16
F32 = jnp.float32
FB = 24
CB = 6
ROWS = 80
CR = 16
XL = 4096
EARLY = 7 * 256
IDX = XL + EARLY
VMEM_A, VMEM_B = 20 * 2**20, 24 * 2**20
TILES = 96


def plane_lanes(i, j):
    if i == 3:
        return (j * 256, 256)
    if j == 3:
        return (1024 + i * 256, 256)
    return (1792 + (i * 3 + j) * 128, 128)


def upper_pieces():
    pieces = [(3 * 1024, 1024)]
    pieces += [((i * 4 + 3) * 256, 256) for i in range(3)]
    pieces += [((i * 4 + j) * 256 + 128, 128) for i in range(3) for j in range(3)]
    return pieces


UPPER = sum(width for _, width in upper_pieces())
SENT = 1792 + 5 * 128


def dot(a, b, dims=((1,), (0,))):
    return lax.dot_general(a, b, (dims, ((), ())), preferred_element_type=F32)


def gate(v):
    s = 1.0 / (1.0 + jnp.exp(-v))
    return v * s, s * (1.0 + v * (1.0 - s))


def axis_sides(half):
    inner = [(0, 0, half + 1), (0, 1, half + 3)]
    return inner + ([(-1, 1, 0)] if half else [(1, 0, 5)])


def halo_blocks(p, q):
    blocks = []
    for sx, ox, cx in axis_sides(p):
        for sy, oy, cy in axis_sides(q):
            for sz, oz, cells in (
                (0, 0, [(0, 1), (1, 2)]),
                (0, 1, [(0, 3), (1, 4)]),
                (-1, 1, [(1, 0)]),
                (1, 0, [(0, 5)]),
            ):
                code = 9 * (sx + 1) + 3 * (sy + 1) + sz + 1
                if code != 13:
                    targets = [(r, (cx, cy, cz)) for r, cz in cells]
                    blocks.append((code - (code > 13), 4 * ox + 2 * oy + oz, targets))
    return blocks


HALO = len(halo_blocks(0, 0)) * CR


def swap_halves(tile):
    return jnp.concatenate([tile[:, 64:128], tile[:, 0:64]], axis=1)


def octant_of(x, y, z):
    return 4 * (x // 2) + 2 * (y // 2) + z // 2, 4 * (x % 2) + 2 * (y % 2) + z % 2


def in_hbm(*arrays):
    return [pltpu.with_memory_space_constraint(array, pltpu.HBM) for array in arrays]


def widen(wd_ref, wc_ref, down_ref, coarse_ref, turned_ref):
    down_ref[...] = jnp.zeros(down_ref.shape, BF)
    for ab in range(9):
        tap = [wd_ref[(3 * ab + e) * 64 : (3 * ab + e + 1) * 64, :] for e in range(3)]
        at = ab * 384
        for row, e in ((0, 1), (64, 2), (320, 0)):
            down_ref[at + row : at + row + 64, 0:128] = tap[e]
        for row, e in ((64, 0), (128, 1), (192, 2)):
            down_ref[at + row : at + row + 64, 128:256] = tap[e]
    zero = jnp.zeros((128, 128), BF)
    for ab in range(9):
        for e in range(3):
            tap = 3 * ab + e
            plain = wc_ref[tap * 128 : (tap + 1) * 128, :]
            other = (26 - tap) * 128
            turned = jnp.transpose(wc_ref[other : other + 128, :].astype(F32)).astype(BF)
            for ref, block in ((coarse_ref, plain), (turned_ref, turned)):
                for r in range(2):
                    row = ab * 512 + (e + r) * 128
                    ref[row : row + 128, r * 128 : (r + 1) * 128] = block
        for ref in (coarse_ref, turned_ref):
            ref[ab * 512 + 384 : ab * 512 + 512, 0:128] = zero
            ref[ab * 512 : ab * 512 + 128, 128:256] = zero


def rows_of(refs, lane, width):
    parts = [ref[:, lane : lane + width].astype(F32) for ref in refs]
    return jnp.concatenate(parts + [jnp.zeros((ROWS - 3 * FB, width), F32)], axis=0)


def to_coarse(up, ref):
    return dot(up, ref[...], ((0,), (0,)))


def fill(nl_ref, flat_ref, padded_ref):
    for x in range(4):
        for y in range(4):
            for z in range(4):
                o, v = octant_of(x, y, z)
                padded_ref[x + 1, y + 1, (z + 1) // 2, (z + 1) % 2] = flat_ref[
                    o * CR : (o + 1) * CR, v * 128 : (v + 1) * 128
                ]
    for pq in range(4):
        got = dot(nl_ref[pq], flat_ref[:, pq * 256 : (pq + 1) * 256]).astype(BF)
        for n, (_, _, targets) in enumerate(halo_blocks(pq // 2, pq % 2)):
            for r, (cx, cy, cz) in targets:
                padded_ref[cx, cy, cz // 2, cz % 2] = got[
                    n * CR : (n + 1) * CR, r * 128 : (r + 1) * 128
                ]


def convolve(padded_ref, weight_ref):
    outs = []
    for x in range(0, 4, 1):
        taps = [
            padded_ref[x + a : x + a + 1, b : b + 4, zz // 2 : zz // 2 + 2, zz % 2].reshape(1 * 8 * CR, 128)
            for a in range(3)
            for b in range(3)
            for zz in range(4)
        ]
        outs.append(dot(jnp.concatenate(taps, axis=1), weight_ref[...]))
    return jnp.concatenate(outs, axis=0)


VOXELS = [
    (row * CR, r * 128, octant_of(row // 8, row // 2 % 4, row % 2 * 2 + r))
    for row in range(32)
    for r in range(2)
]


def scatter_flat(ref, value):
    for row, lane, (o, v) in VOXELS:
        piece = value[row : row + CR, lane : lane + 128]
        ref[o * CR : (o + 1) * CR, v * 128 : (v + 1) * 128] = piece


def forward(
    own_ref,
    prev_ref,
    next_ref,
    far_ref,
    wd_hbm,
    wc_hbm,
    wt_ref,
    mine_ref,
    up_ref,
    nl_ref,
    cp_ref,
    cslope_ref,
    cout_ref,
    dslope_ref,
    src_ref,
    pad_ref,
    hid_ref,
    cin_ref,
    raw_down_ref,
    raw_coarse_ref,
    wd_ref,
    wc_ref,
    sems,
):
    copies = [
        pltpu.make_async_copy(wd_hbm, raw_down_ref, sems.at[0]),
        pltpu.make_async_copy(wc_hbm, raw_coarse_ref, sems.at[1]),
    ]
    for copy in copies:
        copy.start()
    zeros8 = functools.partial(jnp.zeros, dtype=F32)
    rows = functools.partial(rows_of, (prev_ref, own_ref, next_ref))

    idx = rows(IDX, 128)
    row = lax.broadcasted_iota(jnp.int32, (ROWS, 128), 0)
    lane = lax.broadcasted_iota(jnp.int32, (ROWS, 128), 1)
    block = jnp.where(row >= FB, 1.0, 0.0) + jnp.where(row >= 2 * FB, 1.0, 0.0)
    lane_f = lane.astype(F32)

    at = 0
    for n, (start, width) in enumerate(upper_pieces()):
        if width > 128:
            far = far_ref[:, at : at + width].astype(F32)
        else:
            tile = 1792 + (n - 4) // 2 * 128
            far = far_ref[:, tile : tile + 128].astype(F32)
            far = far if (n - 4) % 2 else swap_halves(far)
        parts = [far]
        parts += [r[:, start : start + width].astype(F32) for r in (prev_ref, own_ref, next_ref)]
        src_ref[:, at : at + width] = jnp.concatenate(parts, axis=0).astype(BF)
        at += width

    def pick(code):
        wanted = idx[:, code - 1 : code] + (24.0 * block[:, 0:1] - 1.0)
        wanted = jnp.where(idx[:, code - 1 : code] > 0.0, wanted, -1.0)
        hit = jnp.where(lane_f[:, 0 : 4 * FB] == wanted, 1.0, 0.0)
        return hit.astype(BF)

    picks = {code: pick(code) for code in range(1, 8)}

    def fetch(code, i, j, last):
        start, width = plane_lanes(i, j)
        if last:
            start, width = start + width - 128, 128
        return dot(picks[code], src_ref[:, start : start + width])

    def only_own(array):
        return jnp.concatenate([array[FB : 2 * FB], zeros8((8, array.shape[1]))], axis=0)

    for ip in range(5):
        for jp in range(5):
            i, j = (ip - 1) % 4, (jp - 1) % 4
            code = 4 * (ip == 0) + 2 * (jp == 0)
            if code:
                own = fetch(code, i, j, False)
            else:
                own = rows((i * 4 + j) * 256, 256)
            behind = fetch(code + 1, i, j, True)
            pad_ref[ip * 5 + jp, :, 0:256] = own.astype(BF)
            pad_ref[ip * 5 + jp, :, 256:384] = behind.astype(BF)
            mine_ref[ip * 5 + jp, :, 0:256] = only_own(own).astype(BF)
            mine_ref[ip * 5 + jp, :, 256:384] = only_own(behind).astype(BF)

    for copy in copies:
        copy.wait()
    widen(raw_down_ref, raw_coarse_ref, wd_ref, wc_ref, wt_ref)

    outs = []
    for p in range(2):
        for q in range(2):
            taps = [pad_ref[(2 * p + a) * 5 + 2 * q + b] for a in range(3) for b in range(3)]
            outs.append(dot(jnp.concatenate(taps, axis=1), wd_ref[...]))
    pre = jnp.concatenate(outs, axis=0)
    for pq in range(4):
        value, slope = gate(pre[pq * ROWS : (pq + 1) * ROWS])
        hid_ref[:, pq * 256 : (pq + 1) * 256] = value.astype(BF)
        dslope_ref[pq] = slope[FB : 2 * FB]

    code = idx[:, 7:8]
    slot = jnp.where(code > 0.0, code + (48.0 * block[:, 0:1] - 9.0), -1.0)
    column = (lane % CR * 8 + lane // CR).astype(F32)
    up_f = jnp.where(column == slot, 1.0, 0.0)
    up_ref[...] = up_f
    up = up_f.astype(BF)

    row16 = lax.broadcasted_iota(jnp.int32, (CR, ROWS), 0)
    lane80 = lax.broadcasted_iota(jnp.int32, (CR, ROWS), 1)
    device = jnp.where(row16 >= CB, 1, 0) + jnp.where(row16 >= 2 * CB, 1, 0)
    choose = jnp.where(lane80 == row16 + (FB - CB) * device, 1.0, 0.0).astype(BF)
    listed = dot(choose, idx.astype(BF))
    device = device[:, 0:1].astype(F32)
    place = listed + (6.0 * device - 7.0)
    place = jnp.where((listed > 0.0) & (place >= 0.0) & (place < CR), place, -1000.0)
    lane16 = lane_f[0:CR]
    for pq in range(4):
        blocks = []
        for m, octant, _ in halo_blocks(pq // 2, pq % 2):
            wanted = place[:, 8 + m : 9 + m] + float(CR * octant)
            blocks.append(jnp.where(lane16 == wanted, 1.0, 0.0))
        nl_ref[pq] = jnp.concatenate(blocks, axis=0).astype(BF)

    cin_ref[...] = to_coarse(up, hid_ref).astype(BF)
    fill(nl_ref, cin_ref, cp_ref)
    value, slope = gate(convolve(cp_ref, wc_ref))
    cslope_ref[...] = slope
    scatter_flat(cout_ref, value.astype(BF))


def backward(
    own_ref,
    prev_ref,
    next_ref,
    cot_own_ref,
    cot_prev_ref,
    cot_next_ref,
    wt_ref,
    wu_ref,
    mine_ref,
    up_ref,
    nl_ref,
    cp_ref,
    cslope_ref,
    cout_ref,
    dslope_ref,
    dec_ref,
    sum_ref,
    hid_ref,
    cin_ref,
    cs_ref,
    sp_ref,
    cst_ref,
    grad_ref,
    gd_ref,
    gc_ref,
    gu_ref,
):
    zeros8 = functools.partial(jnp.zeros, dtype=F32)
    rows = functools.partial(rows_of, (prev_ref, own_ref, next_ref))


    def cot_rows(lane, width):
        if lane < EARLY:
            return rows(XL + lane, width)
        return rows_of((cot_prev_ref, cot_own_ref, cot_next_ref), lane - EARLY, width)

    up_f = up_ref[...]
    up = up_f.astype(BF)

    up_in = dot(up, cout_ref[...])
    pieces = [up_in[:, v * 128 : (v + 1) * 128] for v in range(8)]
    own_in = [piece[FB : 2 * FB] for piece in pieces]
    out = dot(jnp.concatenate(pieces, axis=0).astype(BF), wu_ref[...])
    all_grad, own_grad = [], []
    for v in range(8):
        p, q, r = v // 4, v // 2 % 2, v % 2
        grads = []
        for ab in range(4):
            a, b = ab // 2, ab % 2
            at = ((2 * p + a) * 4 + 2 * q + b) * 256 + r * 128
            joined = out[v * ROWS : (v + 1) * ROWS, ab * 128 : (ab + 1) * 128] + rows(at, 128)
            value, slope = gate(joined)
            dec_ref[:, at : at + 128] = value[FB : 2 * FB].astype(BF)
            grads.append(cot_rows(at, 128) * slope)
        grad = jnp.concatenate(grads, axis=1)
        own_grad.append(grad[FB : 2 * FB])
        all_grad.append(grad.astype(BF))
    back = dot(jnp.concatenate(all_grad, axis=0), wu_ref[...], ((1,), (1,))).astype(BF)
    for v in range(8):
        hid_ref[:, v * 128 : (v + 1) * 128] = back[v * ROWS : (v + 1) * ROWS]
    own_in = jnp.concatenate(own_in, axis=0).astype(BF)
    own_grad = jnp.concatenate(own_grad, axis=0).astype(BF)
    found = dot(own_in, own_grad, ((0,), (0,)))
    for n in range(4):
        gu_ref[n] = found[:, n * 128 : (n + 1) * 128]

    cin_ref[...] = to_coarse(up, hid_ref).astype(BF)
    row_c = lax.broadcasted_iota(jnp.int32, (8 * CR, 128), 0) % CR
    mine = (row_c >= CB) & (row_c < 2 * CB)
    for row, lane, (o, v) in VOXELS:
        grad = cin_ref[o * CR : (o + 1) * CR, v * 128 : (v + 1) * 128].astype(F32)
        grad = grad * cslope_ref[row : row + CR, lane : lane + 128]
        grad_ref[row : row + CR, lane : lane + 128] = grad
        cs_ref[o * CR : (o + 1) * CR, v * 128 : (v + 1) * 128] = grad.astype(BF)
    for x in range(4):
        for r in range(2):
            kept = grad_ref[x * 128 : (x + 1) * 128, r * 128 : (r + 1) * 128]
            kept = jnp.transpose(jnp.where(mine, kept, 0.0)).astype(BF)
            cst_ref[:, r * 512 + x * 128 : r * 512 + (x + 1) * 128] = kept
    for ab in range(9):
        a, b = ab // 3, ab % 3
        taps = []
        for e in range(3):
            parts = [
                cp_ref[a : a + 4, b : b + 4, (e + r) // 2 : (e + r) // 2 + 2, (e + r) % 2]
                for r in range(2)
            ]
            parts = [part.reshape(32 * CR, 128) for part in parts]
            taps.append(jnp.concatenate(parts, axis=0))
        found = dot(cst_ref[...], jnp.concatenate(taps, axis=1))
        for e in range(3):
            at = (3 * ab + e) * 128
            gc_ref[at : at + 128, :] = jnp.transpose(found[:, e * 128 : (e + 1) * 128])

    fill(nl_ref, cs_ref, sp_ref)
    scatter_flat(cin_ref, convolve(sp_ref, wt_ref).astype(BF))

    hidden_grad = dot(up_f[FB : 2 * FB].astype(BF), cin_ref[...])
    pieces = []
    for pq in range(4):
        slope = hidden_grad[:, pq * 256 : (pq + 1) * 256] * dslope_ref[pq]
        pieces += [slope, zeros8((8, 256))]
    down = jnp.transpose(jnp.concatenate(pieces, axis=0)).astype(BF)
    for ab in range(9):
        a, b = ab // 3, ab % 3
        taps = [mine_ref[(2 * p + a) * 5 + 2 * q + b] for p in range(2) for q in range(2)]
        taps = jnp.concatenate(taps, axis=0)
        low = dot(down[0:128], jnp.concatenate([taps[:, 0:128], taps[:, 256:384]], axis=1))
        high = dot(down[128:256], taps[:, 0:256])
        later = low[:, 0:128] + high[:, 128:256]
        first = low[:, 128:256] + high[:, 0:128]
        gd_ref[(3 * ab) * 64 : (3 * ab + 1) * 64, :] = jnp.transpose(first)[64:128]
        gd_ref[(3 * ab + 1) * 64 : (3 * ab + 3) * 64, :] = jnp.transpose(later)

    for t in range(TILES):
        if t < 27:
            tile = gd_ref[pl.ds(t, 64, stride=27), :]
        elif t < 81:
            tile = gc_ref[pl.ds(t - 27, 64, stride=54), :]
        elif t < 89:
            tile = gu_ref[(t - 81) % 4, pl.ds((t - 81) // 4, 64, stride=2), :]
        else:
            tile = jnp.zeros((64, 128), F32)
        n = t % 12
        sum_ref[t // 12 % 2, t // 24, :, n * 128 : (n + 1) * 128] = tile.astype(BF)


def forward_pass(own, prev, nxt, far, wd, wc):
    vmem = pl.BlockSpec(memory_space=pltpu.VMEM)
    made = (
        ((9 * 512, 256), BF),
        ((25, FB + 8, 384), BF),
        ((ROWS, 128), F32),
        ((4, HALO, 128), BF),
        ((6, 6, 3, 2, CR, 128), BF),
        ((32 * CR, 256), F32),
        ((8 * CR, 1024), BF),
        ((4, FB, 256), F32),
    )
    return pl.pallas_call(
        forward,
        out_shape=tuple(jax.ShapeDtypeStruct(*one) for one in made),
        in_specs=[vmem] * 4 + [pl.BlockSpec(memory_space=pltpu.HBM)] * 2,
        out_specs=(vmem,) * len(made),
        scratch_shapes=[
            pltpu.VMEM((4 * FB, UPPER), BF),
            pltpu.VMEM((25, ROWS, 384), BF),
            pltpu.VMEM((ROWS, 1024), BF),
            pltpu.VMEM((8 * CR, 1024), BF),
            pltpu.VMEM(wd.shape, BF),
            pltpu.VMEM(wc.shape, BF),
            pltpu.VMEM((9 * 384, 256), BF),
            pltpu.VMEM((9 * 512, 256), BF),
            pltpu.SemaphoreType.DMA((2,)),
        ],
        compiler_params=pltpu.CompilerParams(vmem_limit_bytes=VMEM_A),
    )(own, prev, nxt, far, *in_hbm(wd, wc))


def backward_pass(*given):
    vmem = pl.BlockSpec(memory_space=pltpu.VMEM)
    return pl.pallas_call(
        backward,
        out_shape=(
            jax.ShapeDtypeStruct((FB, XL), BF),
            jax.ShapeDtypeStruct((2, 4, 64, 1536), BF),
        ),
        in_specs=[vmem] * len(given),
        out_specs=(vmem, vmem),
        scratch_shapes=[
            pltpu.VMEM((ROWS, 1024), BF),
            pltpu.VMEM((8 * CR, 1024), BF),
            pltpu.VMEM((8 * CR, 1024), BF),
            pltpu.VMEM((6, 6, 3, 2, CR, 128), BF),
            pltpu.VMEM((128, 64 * CR), BF),
            pltpu.VMEM((32 * CR, 256), F32),
            pltpu.VMEM((1728, 128), F32),
            pltpu.VMEM((3456, 128), F32),
            pltpu.VMEM((4, 128, 128), F32),
        ],
        compiler_params=pltpu.CompilerParams(vmem_limit_bytes=VMEM_B),
    )(*given)


def pack(place_ref, *refs):
    given, held, sems = refs[:5], refs[8:13], refs[13]
    own_ref, cots_ref, far_ref = refs[5:8]
    copies = [
        pltpu.make_async_copy(source, target, sems.at[n])
        for n, (source, target) in enumerate(zip(given, held))
    ]
    for copy in copies:
        copy.start()
    for copy in copies:
        copy.wait()
    x_ref, cot_ref, fine_ref, parent_ref, coarse_ref = held
    place = place_ref[0]
    own_ref[:, 0:XL] = x_ref[...].reshape(FB, XL)
    cot = cot_ref[...].reshape(FB, XL)
    own_ref[:, XL:IDX] = cot[:, 0:EARLY]
    cots_ref[...] = cot[:, EARLY:XL]
    fine = jnp.concatenate([fine_ref[m] for m in range(7)], axis=0)
    fine = jnp.where(fine < 0, 0, fine - (FB * (place - 1) - 1)).astype(F32)
    coarse = jnp.concatenate([coarse_ref[c] for c in range(CB)], axis=0)
    coarse = jnp.where(coarse < 0, 0, coarse - (CB * (place - 1) - 1)).astype(F32)
    coarse = jnp.concatenate([coarse, jnp.zeros((FB - CB, 26), F32)], axis=0)
    parent = (parent_ref[...] - (8 * (CB * place - 1) - 1)).astype(F32)
    lists = jnp.concatenate([fine, parent], axis=0).astype(BF)
    unit = lax.broadcasted_iota(jnp.int32, (FB, FB), 0) == lax.broadcasted_iota(
        jnp.int32, (FB, FB), 1
    )
    lists = dot(jnp.where(unit, 1.0, 0.0).astype(BF), lists, ((1,), (1,)))
    filler = jnp.zeros((FB, 128 - 34), F32)
    own_ref[:, IDX : IDX + 128] = jnp.concatenate([lists, coarse, filler], axis=1).astype(BF)
    at = 0
    last = []
    for start, width in upper_pieces():
        if width > 128:
            far_ref[:, at : at + width] = own_ref[:, start : start + width]
        else:
            last.append(own_ref[:, start : start + width].astype(F32))
        at += width
    upper_half = lax.broadcasted_iota(jnp.int32, (FB, 128), 1) >= 64
    for n in range(5):
        first = swap_halves(last[2 * n])
        second = last[2 * n + 1] if 2 * n + 1 < 9 else first
        tile = jnp.where(upper_half, second, first)
        far_ref[:, 1792 + n * 128 : 1920 + n * 128] = tile.astype(BF)


def packed(place, features, cotangent, fine_nbr, parents, coarse_nbr):
    vmem = pl.BlockSpec(memory_space=pltpu.VMEM)
    return pl.pallas_call(
        pack,
        out_shape=(
            jax.ShapeDtypeStruct((FB, IDX + 128), BF),
            jax.ShapeDtypeStruct((FB, XL - EARLY), BF),
            jax.ShapeDtypeStruct((FB, SENT), BF),
        ),
        in_specs=[pl.BlockSpec(memory_space=pltpu.SMEM)]
        + [pl.BlockSpec(memory_space=pltpu.HBM)] * 5,
        out_specs=(vmem,) * 3,
        scratch_shapes=[
            pltpu.VMEM(array.shape, array.dtype)
            for array in (features, cotangent, fine_nbr, parents, coarse_nbr)
        ]
        + [pltpu.SemaphoreType.DMA((5,))],
        compiler_params=pltpu.CompilerParams(vmem_limit_bytes=8 * 2**20),
    )(place, *in_hbm(features, cotangent, fine_nbr, parents, coarse_nbr))


SPACE = ("x", "z")


def shift(block, distance):
    size = lax.axis_size(SPACE)
    route = [(i, i + distance) for i in range(size) if 0 <= i + distance < size]
    return lax.ppermute(block, SPACE, route)


def sum_copies(in_ref, out_ref):
    total = jnp.sum(in_ref[...].astype(F32), axis=0)
    for n in range(out_ref.shape[0]):
        out_ref[n] = total


def split(in_ref, down_ref, coarse_ref, up_ref):
    whole = jnp.concatenate([in_ref[n] for n in range(8)], axis=0)
    down_ref[...] = whole[0:27]
    coarse_ref[...] = whole[27:81]
    up_ref[...] = whole[81:89]


def spread_sum(sums):
    held = lax.all_to_all(sums, "core", 0, 0)
    held = jnp.sum(held.astype(F32), axis=0).astype(BF)
    held = held.reshape(16, 16, 1536)
    held = lax.all_to_all(held, ("y", "x"), 0, 0)
    held = jnp.sum(held.astype(F32), axis=0).astype(BF)
    held = held.reshape(16, 12, 128)
    held = lax.all_to_all(held, "z", 0, 0)
    held = pl.pallas_call(
        sum_copies,
        out_shape=jax.ShapeDtypeStruct((8, 12, 128), F32),
        compiler_params=pltpu.CompilerParams(vmem_limit_bytes=2 * 2**20),
    )(held)
    held = lax.all_to_all(held, ("y", "core"), 0, 0)
    shares = pl.pallas_call(
        split,
        out_shape=tuple(jax.ShapeDtypeStruct((n, 128), F32) for n in (27, 54, 8)),
        compiler_params=pltpu.CompilerParams(vmem_limit_bytes=2 * 2**20),
    )(held)
    return tuple(share.reshape(-1) for share in shares)


def gradients(
    fine_features,
    cotangent,
    down_weight,
    coarse_weight,
    up_weight,
    fine_neighbours,
    children,
    parent_slots,
    coarse_neighbours,
):
    place = lax.axis_index(SPACE).astype(jnp.int32).reshape(1)
    own, cot, upper = packed(
        place,
        fine_features[0],
        cotangent[0],
        fine_neighbours.transpose(2, 0, 1),
        parent_slots,
        coarse_neighbours[0].reshape(CB, 1, 26),
    )
    prev = shift(own, 1)
    far = shift(upper, 2)
    nxt = shift(own, -1)
    cot_prev = shift(cot, 1)
    cot_next = shift(cot, -1)
    turned, *kept = forward_pass(own, prev, nxt, far, down_weight, coarse_weight)
    return backward_pass(own, prev, nxt, cot, cot_prev, cot_next, turned, up_weight, *kept)


def body(fine_features, *rest):
    decoded, sums = gradients(fine_features, *rest)
    return (decoded.reshape(fine_features.shape), *spread_sum(sums))


def solution(mesh):
    mesh = jax.sharding.Mesh(mesh.devices.reshape(4, 2, 4, 16), ("y", "core", "x", "z"))
    dp = ("y", "core")
    in_specs = (
        P(dp, SPACE, None, None, None),
        P(dp, SPACE, None, None, None),
        P(),
        P(),
        P(),
        P(dp, SPACE, None),
        P(dp, SPACE, None),
        P(dp, SPACE),
        P(dp, SPACE, None),
    )
    out_specs = (P(dp, SPACE, None, None, None), P(SPACE), P(SPACE), P(SPACE))
    return jax.shard_map(body, mesh=mesh, in_specs=in_specs, out_specs=out_specs, check_vma=False)
```
